32 devices in a mesh: gx: 4 (over y, core), gy: 8 (over z, x).
Axes of the slice: x: 2, y: 2, z: 4, core: 2. Of those that a mesh axis runs over, the one named last changes fastest.
Arguments:
- payload: bfloat16 [2048, 4, 35, 128], P(('gx', 'gy')), may hold values from -6 to 6
- opacity: bfloat16 [2048, 4, 128], P(('gx', 'gy')), may hold values from 0.049804688 to 0.34960938
- depth_order: int32 [256, 8], P(('gx', 'gy')), may hold values from 0 to 31, as said below
- footprints: int32 [32, 64], replicated, may hold values from 0 to 255, as said below
- panel_map: int32 [8], replicated, may hold values from 0 to 7, each once
- conv1_weight: bfloat16 [9, 32, 36], replicated, may hold values from -0.3125 to 0.3125
- conv1_bias: float32 [32], replicated, may hold values from -3 to 3
- conv2_weight: bfloat16 [9, 32, 32], replicated, may hold values from -0.375 to 0.375
- conv2_bias: float32 [32], replicated, may hold values from -3 to 3
Outputs:
- display: bfloat16 [4, 8, 2, 32, 2048], P('gx', 'gy')
The draws below stay inside these ranges and needn't reach their ends.
Inputs may be any that keep to these rules, and one draw needn't show every extreme that they name: Each tile lists 8 different bricks; brick b lists tile t in footprints exactly when b appears in row t of depth_order, each tile at most once, 64 tiles a brick. The tiles of the brick of device (x, y) are the 4 consecutive screen tile rows 4x + s .. 4x + s + 3 (modulo 32), for some s from 1 to 3, each with all 32 tile columns; so they belong to devices of gx index x or x + 1 modulo 4, every brick has tiles on both, and every device along gy gets exactly 8 of them. `footprints`: tile numbers as described for depth_order.
All inputs are finite; a program needn't handle non-finite values.
Results may differ from the reference program's by a relative error of at most 0.0052.
Values may be sent and summed in bfloat16 or wider, within the bound.
No kernel may reach another device: no remote copies, remote signals or barrier semaphores. Data moves between devices by JAX's collectives and lax.ppermute only.
A program may use at most 64 MiB of HBM per device.

```python
import jax
import jax.numpy as jnp

FEAT = 32
TILE_W = 128
TILE_H = 4
TYD = 4
TXD = 2
TILES_DEV = 8
DEPTH = 8
BRICKS = 32
TILES = 256
FRAGS = 64
CH = 35
STRIP = 2
SCREEN_H = 64
SCREEN_W = 2048
N_GX = 4
N_GY = 8


def tile_layout(key):
    tile_rows = N_GX * TYD
    tile_cols = N_GY * TXD
    column_range = jnp.arange(N_GY, dtype=jnp.int32)
    scores = jax.random.randint(jax.random.fold_in(key, 11), (N_GX, N_GY), 0, 1 << 20) * N_GY + column_range[None, :]
    slab_of = jnp.argsort(jnp.argsort(scores, axis=1), axis=1).astype(jnp.int32)
    holder = jnp.argsort(slab_of, axis=1).astype(jnp.int32)
    shifts = jax.random.randint(jax.random.fold_in(key, 12), (DEPTH,), 1, TYD).astype(jnp.int32)
    tile_range = jnp.arange(TILES, dtype=jnp.int32)
    owner = tile_range // TILES_DEV
    local = tile_range % TILES_DEV
    tile_row = owner // N_GY * TYD + local // TXD
    depth_range = jnp.arange(DEPTH, dtype=jnp.int32)
    cell = (tile_row[:, None] - shifts[None, :]) % tile_rows // TYD
    ordered = cell * N_GY + holder[cell, depth_range[None, :]]
    brick_range = jnp.arange(BRICKS, dtype=jnp.int32)
    brick_row = brick_range // N_GY
    brick_col = brick_range % N_GY
    offset = shifts[slab_of[brick_row, brick_col]]
    frag_range = jnp.arange(FRAGS, dtype=jnp.int32)
    band_step = frag_range // tile_cols
    column = frag_range % tile_cols
    row = (brick_row[:, None] * TYD + offset[:, None] + band_step[None, :]) % tile_rows
    listed = (row // TYD * N_GY + column[None, :] // TXD) * TILES_DEV + row % TYD * TXD + column[None, :] % TXD
    order_scores = jax.random.randint(jax.random.fold_in(key, 13), (BRICKS, FRAGS), 0, 1 << 20) * FRAGS
    order_scores = order_scores + frag_range[None, :]
    shuffle = jnp.argsort(order_scores, axis=1)
    listed = jnp.take_along_axis(listed, shuffle, axis=1)
    return (ordered.astype(jnp.int32), listed.astype(jnp.int32))


def draw_depth_order(key, part):
    return tile_layout(key)[0]


def draw_footprints(key, part):
    return tile_layout(key)[1]


def block_scale(own_key, dims, pieces, least, high):
    def one(dim, parts):
        draws = jax.random.uniform(jax.random.fold_in(jax.random.fold_in(own_key, 6), dim), (parts,), jnp.float32, least / len(pieces), high / len(pieces))
        return jnp.repeat(jnp.exp(draws), dims[dim] // parts).reshape((-1,) + (1,) * (len(dims) - dim - 1))

    gain = one(*pieces[0])
    for cut in pieces[1:]:
        gain = gain * one(*cut)
    return gain


def bell_draw(rng, dims, width, limit, split=(), held_as=jnp.bfloat16):
    drawn = width * jax.random.normal(rng, dims, jnp.float32)
    if split:
        drawn = drawn * block_scale(rng, dims, split, -0.22, 0.18)
    return jnp.clip(drawn, -limit, limit).astype(held_as)


def setup_inputs(seed: int = 0) -> dict:
    seeds = jax.random.split(jax.random.key(seed), 10)
    payload = bell_draw(seeds[0], (BRICKS * FRAGS, TILE_H, CH, TILE_W), 1.0, 6.0, ((0, 32),))
    opacity = jnp.clip(0.049804688 + 0.2998047 * jax.random.uniform(seeds[1], (BRICKS * FRAGS, TILE_H, TILE_W), jnp.float32) ** block_scale(seeds[1], (BRICKS * FRAGS, TILE_H, TILE_W), ((0, 32),), -0.2, 0.2), 0.049804688, 0.34960938).astype(jnp.bfloat16)
    depth_order = draw_depth_order(jax.random.fold_in(seeds[9], 71), 0)
    footprints = draw_footprints(jax.random.fold_in(seeds[9], 71), 0)
    panel_map = jax.random.permutation(seeds[4], N_GY).astype(jnp.int32)
    conv1_weight = bell_draw(seeds[5], (9, FEAT, CH + 1), (9 * (CH + 1)) ** -0.5, 0.3125)
    conv1_bias = bell_draw(seeds[6], (FEAT,), 0.5, 3.0, (), jnp.float32)
    conv2_weight = bell_draw(seeds[7], (9, FEAT, FEAT), (9 * FEAT) ** -0.5, 0.375)
    conv2_bias = bell_draw(seeds[8], (FEAT,), 0.5, 3.0, (), jnp.float32)
    return dict(payload=payload, opacity=opacity, depth_order=depth_order, footprints=footprints, panel_map=panel_map, conv1_weight=conv1_weight, conv1_bias=conv1_bias, conv2_weight=conv2_weight, conv2_bias=conv2_bias)


def conv_layer(field, kernel):
    height = field.shape[0]
    span_cols = field.shape[2]
    padded = jnp.pad(field.astype(jnp.float32), ((1, 1), (0, 0), (1, 1)))
    kernel_wide = kernel.astype(jnp.float32)
    total = jnp.zeros((height, kernel.shape[1], span_cols), jnp.float32)
    for row_shift in range(3):
        for col_shift in range(3):
            window = padded[row_shift:row_shift + height, :, col_shift:col_shift + span_cols]
            total = total + jnp.einsum("oc,hcw->how", kernel_wide[3 * row_shift + col_shift], window)
    return total


def reference(payload, opacity, depth_order, footprints, panel_map, conv1_weight, conv1_bias, conv2_weight, conv2_bias):
    tile_index = jnp.arange(TILES, dtype=jnp.int32)
    frag_index = jnp.arange(FRAGS, dtype=jnp.int32)
    color = jnp.zeros((TILES, TILE_H, CH, TILE_W), jnp.float32)
    transmit = jnp.ones((TILES, TILE_H, TILE_W), jnp.float32)
    for depth_step in range(DEPTH):
        brick = depth_order[:, depth_step]
        foot_rows = footprints[brick]
        position = jnp.sum(jnp.where(foot_rows == tile_index[:, None], frag_index[None, :], 0), axis=1).astype(jnp.int32)
        source = brick * FRAGS + position
        color = color + transmit[:, :, None, :] * payload[source].astype(jnp.float32)
        transmit = transmit * (1.0 - opacity[source].astype(jnp.float32))
    composite = jnp.concatenate([color.astype(jnp.bfloat16), (1.0 - transmit).astype(jnp.bfloat16)[:, :, None, :]], axis=2)
    screen = composite.reshape(N_GX, N_GY, TYD, TXD, TILE_H, CH + 1, TILE_W)
    screen = screen.transpose(0, 2, 4, 5, 1, 3, 6).reshape(SCREEN_H, CH + 1, SCREEN_W)
    hidden = jax.nn.silu(conv_layer(screen, conv1_weight) + conv1_bias[None, :, None]).astype(jnp.bfloat16)
    shaded = conv_layer(hidden, conv2_weight) + conv2_bias[None, :, None] + screen[:, :FEAT, :].astype(jnp.float32)
    shaded = shaded.astype(jnp.bfloat16)
    strips = shaded.reshape(N_GX, N_GY, STRIP, FEAT, SCREEN_W)
    panel_range = jnp.arange(N_GY, dtype=jnp.int32)
    inverse = jnp.sum(jnp.where(panel_map[:, None] == panel_range[None, :], panel_range[:, None], 0), axis=0).astype(jnp.int32)
    return strips[:, inverse]
```

```python
import functools

import jax
import jax.numpy as jnp
from jax import lax
from jax.experimental import pallas as pl
from jax.experimental.pallas import tpu as pltpu
from jax.sharding import PartitionSpec as P

TYD = 4
SPAN = 4 * TYD


def rotated(block, axis, distance):
    count = lax.axis_size(axis)
    return lax.ppermute(block, axis, [(i, (i + distance) % count) for i in range(count)])


def iota(shape, dim):
    return lax.broadcasted_iota(jnp.int32, shape, dim)


class Plan:
    def __init__(self, count, tiles, rows, channels, lanes, depth):
        self.count = count
        self.tiles = tiles
        self.across = tiles // TYD
        self.rows = rows
        self.channels = channels
        self.lanes = lanes
        self.depth = depth
        self.frag = channels + 1
        self.extra = (TYD - 2) * self.across
        self.blocks = lanes // SPAN
        self.halo = -(-(self.frag + 2) // self.blocks)
        self.at_prev = tiles * self.frag
        self.at_next = self.at_prev + self.extra
        self.at_halo = self.at_next + self.extra
        used = self.at_halo + self.halo
        per = 16 // rows
        self.groups = -(-used // per) * per
        self.halo_pad = self.groups - self.at_halo


def pack_kernel(plan, idx, pidx, nidx, payload, opacity, before, after, *rest):
    n = plan.count
    outs, sem = rest[:n], rest[n]
    for k in range(n):

        def place(t, _, k=k):
            f = idx[k * plan.tiles + t]
            at = t * plan.frag
            pltpu.make_async_copy(
                payload.at[f], outs[k].at[pl.ds(at, plan.channels)], sem.at[k]
            ).start()
            pltpu.make_async_copy(
                opacity.at[f], outs[k].at[at + plan.channels], sem.at[k]
            ).start()
            return 0

        lax.fori_loop(0, plan.tiles, place, 0)
        for e in range(plan.extra):
            pltpu.make_async_copy(
                before.at[pidx[k * plan.extra + e]], outs[k].at[plan.at_prev + e], sem.at[k]
            ).start()
            pltpu.make_async_copy(
                after.at[nidx[k * plan.extra + e]], outs[k].at[plan.at_next + e], sem.at[k]
            ).start()
    for k in range(n):
        whole = outs[k].at[pl.ds(0, plan.at_halo)]
        pltpu.make_async_copy(whole, whole, sem.at[k]).wait()
    lane = iota((plan.frag, plan.rows, plan.lanes), 2)
    lane_extra = iota((plan.rows, plan.lanes), 1)
    across = plan.across
    for k in range(n):
        right, left = outs[(k + 1) % n], outs[(k - 1) % n]
        spread = jnp.zeros((plan.frag, plan.rows, plan.lanes), jnp.float32)
        for j in range(TYD):
            at_r = (j * across) * plan.frag
            at_l = (j * across + across - 1) * plan.frag
            pair = jnp.where(
                lane < 2,
                right[at_r : at_r + plan.frag].astype(jnp.float32),
                left[at_l : at_l + plan.frag].astype(jnp.float32),
            )
            pair = pltpu.roll(pair, 4 * j + 2, 2)
            spread = jnp.where((lane >= 4 * j) & (lane < 4 * j + 4), pair, spread)
        parts = [spread[c] for c in range(plan.frag)]
        for at in (plan.at_prev, plan.at_next):
            extra = jnp.zeros((plan.rows, plan.lanes), jnp.float32)
            for j in range(1, TYD - 1):
                e = (j - 1) * across
                pair = jnp.where(
                    lane_extra < 2,
                    right[at + e].astype(jnp.float32),
                    left[at + e + across - 1].astype(jnp.float32),
                )
                pair = pltpu.roll(pair, 4 * j + 2, 1)
                extra = jnp.where((lane_extra >= 4 * j) & (lane_extra < 4 * j + 4), pair, extra)
            parts.append(extra)
        for i in range(plan.halo_pad):
            group = jnp.zeros((plan.rows, plan.lanes), jnp.float32)
            for b in range(plan.blocks):
                c = i * plan.blocks + b
                if c < len(parts):
                    moved = pltpu.roll(parts[c], SPAN * b, 1) if b else parts[c]
                    group = jnp.where(
                        (lane_extra >= SPAN * b) & (lane_extra < SPAN * b + SPAN), moved, group
                    )
            outs[k][plan.at_halo + i] = group.astype(jnp.bfloat16)


def fold(x):
    return x.reshape(x.shape[0] * x.shape[1], x.shape[2])


def blend_kernel(plan, alpha_at, weight_at, *rest):
    n, tiles, across = plan.count, plan.tiles, plan.across
    inbox, own, sent, alpha, weight, clear = rest[:n], *rest[n:]
    rows, lanes = plan.rows, plan.lanes
    pair = 2 * rows
    frag_rows = plan.frag * rows
    halo_row = plan.at_halo * rows
    opaque = plan.channels * rows
    lane = iota((pair, lanes), 1)

    def doubled(x):
        return jnp.concatenate([x, x], axis=0)

    def take(k, row, slot):
        base = row // 16 * 16
        held = inbox[k][base : base + 16, :].astype(jnp.float32)
        part = held[row - base : row - base + rows]
        alpha[slot] = doubled(part)

    at_p, at_n, at_h = n * tiles, n * (tiles + plan.extra), n * (tiles + 2 * plan.extra)
    for k in range(n):
        for t in range(tiles):
            take(k, t * frag_rows + opaque, k * tiles + t)
        for e in range(plan.extra):
            take(k, (plan.at_prev + e) * rows, at_p + k * plan.extra + e)
            take(k, (plan.at_next + e) * rows, at_n + k * plan.extra + e)
        for m in range(3):
            c = plan.channels + m
            i, b = c // plan.blocks, c % plan.blocks
            row = halo_row + i * rows
            base = row // 16 * 16
            held = inbox[k][base : base + 16, :].astype(jnp.float32)
            part = doubled(held[row - base : row - base + rows])
            if b:
                part = pltpu.roll(part, lanes - SPAN * b, 1)
            alpha[at_h + m * n + k] = part

    weight[...] = jnp.zeros_like(weight)
    kinds = 4 * (tiles - across)

    def through(i, _):
        seen = jnp.ones((pair, lanes), jnp.float32)
        for d in range(plan.depth):
            weight[weight_at[i * plan.depth + d]] = seen
            seen = seen * (1.0 - alpha[alpha_at[i * plan.depth + d]])
        clear[i] = seen
        return 0

    lax.fori_loop(0, kinds, through, 0, unroll=4)

    most = tiles - across
    step = 3 * pair
    while frag_rows % step or step % 16:
        step += pair
    for t in range(tiles):
        keeps, gives = t >= across, t < tiles - across
        for at in range(0, frag_rows, step):
            shape = (step // pair, pair, lanes)
            total_own = jnp.zeros(shape, jnp.float32)
            total_next = jnp.zeros(shape, jnp.float32)
            for k in range(n):
                start = t * frag_rows + at
                held = inbox[k][start : start + step, :].astype(jnp.float32).reshape(shape)
                if keeps:
                    total_own += weight[k * tiles + t][None] * held
                if gives:
                    total_next += weight[(2 * n + k) * tiles + t][None] * held
            if at + step == frag_rows:
                mask = (iota(shape, 0) == step // pair - 1) & (iota(shape, 1) >= rows)
                if keeps:
                    total_own = jnp.where(mask, 1.0 - clear[t - across][None], total_own)
                whole = jnp.zeros((pair, lanes), jnp.float32)
                if t < across:
                    whole = 1.0 - clear[most + t]
                total_next = jnp.where(mask, whole[None], total_next)
            if keeps:
                start = (t - across) * frag_rows + at
                own[start : start + step, :] = total_own.reshape(step, lanes)
            start = t * frag_rows + at
            total = total_next if gives else total_own
            sent[start : start + step, :] = total.reshape(step, lanes).astype(jnp.bfloat16)

    halo_shape = (plan.halo_pad * rows // pair, pair, lanes)
    span_lane = iota((pair, lanes), 1)

    def merged(kind, source):
        out = jnp.zeros((pair, lanes), jnp.float32)
        first = across if kind == 0 else 0
        for u in range(most):
            v = first + u
            out = jnp.where((span_lane // 2 == v), source(u, v), out)
        return out

    def widened(x):
        out = jnp.zeros((pair, lanes), jnp.float32)
        for b in range(plan.blocks):
            moved = pltpu.roll(x, SPAN * b, 1) if b else x
            out = jnp.where(span_lane // SPAN == b, moved, out)
        return out

    totals = [jnp.zeros(halo_shape, jnp.float32) for _ in range(2)]
    for k in range(n):
        held = inbox[k][halo_row : halo_row + plan.halo_pad * rows, :].astype(jnp.float32)
        held = held.reshape(halo_shape)
        for kind in range(2):
            base = (2 * kind + 1) * n * tiles + k * tiles
            by = widened(merged(kind, lambda u, v: weight[base + v]))
            totals[kind] += by[None] * held
    i_cov, b_cov = plan.channels // plan.blocks, plan.channels % plan.blocks
    group = iota(halo_shape, 0) * 2 + iota(halo_shape, 1) // rows
    at_cov = (group == i_cov) & (iota(halo_shape, 2) // SPAN == b_cov)
    for kind in range(2):
        cov = merged(kind, lambda u, v: 1.0 - clear[(2 + kind) * most + u])
        if kind == 1:
            cov = jnp.where(span_lane // 4 == 0, cov, 0.0)
        cov = pltpu.roll(cov, SPAN * b_cov, 1) if b_cov else cov
        totals[kind] = jnp.where(at_cov, cov[None], totals[kind])
    unused = group * plan.blocks + iota(halo_shape, 2) // SPAN > plan.channels
    totals = [jnp.where(unused, 0.0, total) for total in totals]
    band = iota(halo_shape, 2) // 4 % TYD
    length = plan.halo_pad * rows
    start = most * frag_rows
    own[start : start + length, :] = totals[0].reshape(length, lanes)
    start = tiles * frag_rows
    both = jnp.where(band == TYD - 1, totals[0], totals[1])
    sent[start : start + length, :] = both.reshape(length, lanes).astype(jnp.bfloat16)


def conv_kernel(plan, feats, spots, panel, own, got, kept, one, top, low, two, keep, b1, b2, *rest):
    out, field, hidden = rest
    tiles, across, rows, lanes = plan.tiles, plan.across, plan.rows, plan.lanes
    frag_rows = plan.frag * rows
    most = tiles - across
    span = across * lanes
    wide = span + lanes
    has_top, has_low = spots[0], spots[1]
    has_left, has_right = spots[2], spots[3]
    zero = jnp.zeros((frag_rows, lanes), jnp.bfloat16)

    def tile(ref, t):
        return ref[t * frag_rows : (t + 1) * frag_rows, :]

    for c in range(across):
        at = slice(c * lanes, (c + 1) * lanes)
        field[0:frag_rows, at] = jnp.where(has_top != 0, tile(got, most + c), zero)
        field[frag_rows : 2 * frag_rows, at] = tile(got, c)
        for j in range(1, TYD):
            value = tile(own, (j - 1) * across + c)
            if j < TYD - 1:
                value = value + tile(got, j * across + c).astype(jnp.float32)
            field[(j + 1) * frag_rows : (j + 2) * frag_rows, at] = value.astype(jnp.bfloat16)
        at_low = (TYD + 1) * frag_rows
        field[at_low : at_low + frag_rows, at] = jnp.where(has_low != 0, tile(kept, c), zero)

    length = plan.halo_pad * rows
    h_own = own[most * frag_rows : most * frag_rows + length, :]
    h_got = got[tiles * frag_rows : tiles * frag_rows + length, :].astype(jnp.float32)
    h_kept = kept[tiles * frag_rows : tiles * frag_rows + length, :].astype(jnp.float32)
    band = iota((length, lanes), 1) // 4 % TYD
    h_all = jnp.where(band == TYD - 1, h_own, h_own + h_got)
    lane = iota((rows, lanes), 1)
    valid = ((lane < 2) & (has_right != 0)) | ((lane >= lanes - 2) & (has_left != 0))

    def unpacked(source, j):
        pieces = []
        for c in range(plan.frag):
            i, b = c // plan.blocks, c % plan.blocks
            piece = source[i * rows : (i + 1) * rows]
            shift = (-(SPAN * b + 4 * j + 2)) % lanes
            pieces.append(jnp.where(valid, pltpu.roll(piece, shift, 1), 0.0))
        return jnp.concatenate(pieces, axis=0).astype(jnp.bfloat16)

    wide_zero = jnp.zeros((frag_rows, lanes), jnp.bfloat16)
    at = slice(span, wide)
    field[0:frag_rows, at] = jnp.where(has_top != 0, unpacked(h_got, TYD - 1), wide_zero)
    for j in range(TYD):
        field[(j + 1) * frag_rows : (j + 2) * frag_rows, at] = unpacked(h_all, j)
    at_low = (TYD + 1) * frag_rows
    field[at_low : at_low + frag_rows, at] = jnp.where(has_low != 0, unpacked(h_kept, 0), wide_zero)

    def shifted_sum(y):
        part = y.shape[0] // 3
        return (
            pltpu.roll(y[:part], 1, 1)
            + y[part : 2 * part]
            + pltpu.roll(y[2 * part :], wide - 1, 1)
        )

    def act(y, bias):
        x = shifted_sum(y) + bias
        return x * (1.0 / (1.0 + jnp.exp(-x)))

    half = 2 * rows
    groups = TYD // 2
    col = iota((1, wide), 1)
    inside = ((col != span) | (has_right != 0)) & ((col != wide - 1) | (has_left != 0))
    for g in range(groups):
        window = field[2 * g * frag_rows : (2 * g + 4) * frag_rows, :]
        y = jnp.dot(one[...], window, preferred_element_type=jnp.float32)
        h = jnp.where(inside, act(y, b1[...]), 0.0)
        at = feats + g * half * feats
        hidden[at : at + half * feats, :] = h.astype(jnp.bfloat16)
    for ref, at_field, at_hidden, has in (
        (top, 0, 0, has_top),
        (low, TYD * frag_rows, feats * (1 + groups * half), has_low),
    ):
        window = field[at_field : at_field + 2 * frag_rows, :]
        y = jnp.dot(ref[...], window, preferred_element_type=jnp.float32)
        h = jnp.where(inside & (has != 0), act(y, b1[0:feats]), 0.0)
        hidden[at_hidden : at_hidden + feats, :] = h.astype(jnp.bfloat16)
    strip = out.shape[1]
    for g in range(groups):
        at = g * half * feats
        window = hidden[at : at + (half + 2) * feats, :]
        y = jnp.dot(two[...], window, preferred_element_type=jnp.float32)
        plain = field[(2 * g + 1) * frag_rows : (2 * g + 3) * frag_rows, 0:span]
        base = jnp.dot(keep[...], plain, preferred_element_type=jnp.float32)
        total = (shifted_sum(y)[:, 0:span] + b2[...] + base).astype(jnp.bfloat16)
        for s in range(half * feats // strip):
            out[panel[g * (half * feats // strip) + s]] = total[s * strip : (s + 1) * strip]


def layer_one(weight, outs, first, blocks, rows):
    taps = weight.reshape(3, 3, *weight.shape[1:])
    q = jnp.arange(outs)[:, None, None]
    p = jnp.arange(blocks * rows)[None, :, None]
    hit = (p - q - first + 1 == jnp.arange(3)[None, None, :]).astype(weight.dtype)
    hit = hit.reshape(outs, blocks, rows, 3)
    spread = jnp.einsum("qbri,isoc->sqobcr", hit, taps)
    return spread.reshape(3 * outs * weight.shape[1], blocks * weight.shape[2] * rows)


def layer_two(weight, outs):
    taps = weight.reshape(3, 3, *weight.shape[1:])
    q = jnp.arange(outs)[:, None, None]
    p = jnp.arange(outs + 2)[None, :, None]
    hit = (p - q == jnp.arange(3)[None, None, :]).astype(weight.dtype)
    spread = jnp.einsum("qpi,isoc->sqopc", hit, taps)
    return spread.reshape(3 * outs * weight.shape[1], (outs + 2) * weight.shape[2])


def carry(feats, channels, rows, dtype):
    q = jnp.arange(2 * rows)[:, None, None, None, None]
    o = jnp.arange(feats)[None, :, None, None, None]
    b = jnp.arange(2)[None, None, :, None, None]
    c = jnp.arange(channels)[None, None, None, :, None]
    r = jnp.arange(rows)[None, None, None, None, :]
    hit = (q == b * rows + r) & (o == c)
    return hit.astype(dtype).reshape(2 * rows * feats, 2 * channels * rows)


def shards(
    payload,
    opacity,
    depth_order,
    footprints,
    panel_map,
    conv1_weight,
    conv1_bias,
    conv2_weight,
    conv2_bias,
):
    row_groups = lax.axis_size("gx")
    n = lax.axis_size("gy")
    x = lax.axis_index("gx")
    y = lax.axis_index("gy")
    _, rows, channels, lanes = payload.shape
    tiles, depth = depth_order.shape
    plan = Plan(n, tiles, rows, channels, lanes, depth)
    feats = conv2_weight.shape[1]
    across = plan.across
    most = tiles - across

    before = rotated(opacity, "gx", 1)
    after = rotated(opacity, "gx", -1)

    brick_rows = jnp.stack([x, (x - 1) % row_groups, (x + 1) % row_groups])
    listed = footprints[brick_rows * n + y]
    slot = listed // tiles % n * tiles + listed % tiles
    hits = slot[:, None, :] == jnp.arange(n * tiles, dtype=jnp.int32)[None, :, None]
    places = jnp.sum(
        jnp.where(hits, jnp.arange(slot.shape[1], dtype=jnp.int32)[None, None, :], 0), axis=2
    )
    places = places.reshape(3, n, tiles)
    turn = (y + jnp.arange(n, dtype=jnp.int32)) % n
    places = places[:, turn]
    idx = places[0].reshape(-1)
    pidx = places[1][:, across:most].reshape(-1)
    nidx = places[2][:, across:most].reshape(-1)

    spec_s = pl.BlockSpec(memory_space=pltpu.SMEM)
    spec_v = pl.BlockSpec(memory_space=pltpu.VMEM)
    spec_a = pl.BlockSpec(memory_space=pl.ANY)
    limit = pltpu.CompilerParams(vmem_limit_bytes=40 << 20)
    message = jax.ShapeDtypeStruct((plan.groups, rows, lanes), payload.dtype)
    outs = pl.pallas_call(
        functools.partial(pack_kernel, plan),
        out_shape=[message] * n,
        in_specs=[spec_s] * 3 + [spec_a] * 4,
        out_specs=[spec_v] * n,
        scratch_shapes=[pltpu.SemaphoreType.DMA((n,))],
        compiler_params=limit,
        name="pack",
    )(idx, pidx, nidx, payload.transpose(0, 2, 1, 3), opacity, before, after)
    inbox = [fold(outs[0])] + [fold(rotated(outs[k], "gy", k)) for k in range(1, n)]

    mine = jnp.stack([depth_order, rotated(depth_order, "gx", -1)])
    left = rotated(mine, "gy", 1)
    right = rotated(mine, "gy", -1)
    beside = jnp.stack([left[:, across - 1 :: across], right[:, 0::across]], axis=2)
    beside = beside.reshape(2, 2 * TYD, depth)

    def tables(order, kind, halo):
        slots = jnp.arange(order.shape[0], dtype=jnp.int32)[:, None] + (across if kind == 0 else 0)
        k = (y - order % n) % n
        local = order // n == x
        other = jnp.clip(slots - across, 0, plan.extra - 1)
        if halo:
            base = n * (tiles + 2 * plan.extra)
            source = base + jnp.where(local, 0, (1 + kind) * n) + k
        else:
            base = n * (tiles + kind * plan.extra)
            source = jnp.where(local, k * tiles + slots, base + k * plan.extra + other)
        target = (2 * kind + halo) * n * tiles + k * tiles + slots
        return source, jnp.where(local, target, 4 * n * tiles)

    pieces = [
        tables(mine[0, across:], 0, 0),
        tables(mine[1, :most], 1, 0),
        tables(beside[0, across:], 0, 1),
        tables(beside[1, :most], 1, 1),
    ]
    alpha_at = jnp.concatenate([a for a, _ in pieces]).reshape(-1)
    weight_at = jnp.concatenate([w for _, w in pieces]).reshape(-1)

    frag_rows = plan.frag * rows
    tail = plan.halo_pad * rows
    own, sent = pl.pallas_call(
        functools.partial(blend_kernel, plan),
        out_shape=[
            jax.ShapeDtypeStruct((most * frag_rows + tail, lanes), jnp.float32),
            jax.ShapeDtypeStruct((tiles * frag_rows + tail, lanes), jnp.bfloat16),
        ],
        in_specs=[spec_s] * 2 + [spec_v] * n,
        out_specs=[spec_v] * 2,
        scratch_shapes=[
            pltpu.VMEM((n * (tiles + 2 * plan.extra + 3), 2 * rows, lanes), jnp.float32),
            pltpu.VMEM((4 * n * tiles + 1, 2 * rows, lanes), jnp.float32),
            pltpu.VMEM((4 * most, 2 * rows, lanes), jnp.float32),
        ],
        compiler_params=limit,
        name="blend",
    )(alpha_at, weight_at, *inbox)
    got = rotated(sent, "gx", 1)

    half = 2 * rows
    one = layer_one(conv1_weight, half, rows, 4, rows)
    top = layer_one(conv1_weight, 1, rows - 1, 2, rows)
    low = layer_one(conv1_weight, 1, rows, 2, rows)
    two = layer_two(conv2_weight, half)
    keep = carry(feats, channels + 1, rows, payload.dtype)
    b1 = jnp.tile(conv1_bias, half)[:, None]
    b2 = jnp.tile(conv2_bias, half)[:, None]
    spots = jnp.stack([x > 0, x < row_groups - 1, y > 0, y < n - 1]).astype(jnp.int32)
    band = TYD * rows
    strip = band // n
    span = across * lanes
    pieces = pl.pallas_call(
        functools.partial(conv_kernel, plan, feats),
        out_shape=jax.ShapeDtypeStruct((n, strip * feats, span), jnp.bfloat16),
        in_specs=[spec_s] * 2 + [spec_v] * 10,
        out_specs=spec_v,
        scratch_shapes=[
            pltpu.VMEM(((TYD + 2) * frag_rows, span + lanes), jnp.bfloat16),
            pltpu.VMEM(((band + 2) * feats, span + lanes), jnp.bfloat16),
        ],
        compiler_params=limit,
        name="conv",
    )(spots, panel_map, own, got, sent, one, top, low, two, keep, b1, b2)
    shown = lax.all_to_all(pieces, "gy", split_axis=0, concat_axis=0, tiled=True)
    shown = shown.transpose(1, 0, 2).reshape(1, 1, strip, feats, n * span)
    return shown


def solution(mesh):
    return jax.shard_map(
        shards,
        mesh=mesh,
        in_specs=(
            P(("gx", "gy"), None, None, None),
            P(("gx", "gy"), None, None),
            P(("gx", "gy"), None),
            P(),
            P(),
            P(),
            P(),
            P(),
            P(),
        ),
        out_specs=P("gx", "gy", None, None, None),
        check_vma=False,
    )
```

```python
import functools

import jax
import jax.numpy as jnp
from jax import lax
from jax.experimental import pallas as pl
from jax.experimental.pallas import tpu as pltpu
from jax.sharding import PartitionSpec as P

TYD = 4
SPAN = 4 * TYD


def rotated(block, axis, distance):
    count = lax.axis_size(axis)
    return lax.ppermute(block, axis, [(i, (i + distance) % count) for i in range(count)])


def iota(shape, dim):
    return lax.broadcasted_iota(jnp.int32, shape, dim)


class Plan:
    def __init__(self, count, tiles, rows, channels, lanes, depth):
        self.count = count
        self.tiles = tiles
        self.across = tiles // TYD
        self.rows = rows
        self.channels = channels
        self.lanes = lanes
        self.depth = depth
        self.frag = channels + 1
        self.extra = (TYD - 2) * self.across
        self.blocks = lanes // SPAN
        self.halo = -(-(self.frag + 2) // self.blocks)
        self.at_prev = tiles * self.frag
        self.at_next = self.at_prev + self.extra
        self.at_halo = self.at_next + self.extra
        used = self.at_halo + self.halo
        per = 16 // rows
        self.at_order = used
        self.groups = -(-(used + 1) // per) * per
        self.halo_pad = self.groups - self.at_halo


def first_kernel(plan, far, place, footprints, payload, opacity, out, table, sem):
    n, tiles = plan.count, plan.tiles
    me, y = place[0], place[1]

    def look(f, _):
        t = footprints[me, f]
        k = lax.rem(lax.rem(lax.div(t, tiles), n) + n - y, n)
        table[k * tiles + lax.rem(t, tiles)] = f
        return 0

    lax.fori_loop(0, footprints.shape[1], look, 0, unroll=8)

    def move(t, _):
        f = table[far * tiles + t]
        start = t * plan.frag
        pltpu.make_async_copy(payload.at[f], out.at[pl.ds(start, plan.channels)], sem).start()
        pltpu.make_async_copy(opacity.at[f], out.at[start + plan.channels], sem).start()
        return 0

    lax.fori_loop(0, tiles, move, 0)
    pltpu.make_async_copy(out, out, sem).wait()


def pack_kernel(
    plan, far, place, footprints, table, payload, opacity, before, after, orders, first, *rest
):
    n, tiles = plan.count, plan.tiles
    late, sem, beside = rest[n - 1], rest[n], rest[n + 1]
    outs = list(rest[: n - 1])
    outs.insert(far, first)
    tails = [(out, plan.at_prev) for out in outs]
    tails[far] = (late, 0)
    for k in range(n):
        if k == far:
            continue

        def move(t, _, k=k):
            f = table[k * tiles + t]
            pltpu.make_async_copy(
                payload.at[f], outs[k].at[pl.ds(t * plan.frag, plan.channels)], sem.at[k]
            ).start()
            return 0

        lax.fori_loop(0, tiles, move, 0)
    y = place[1]
    for m in range(2):
        brick = place[2 + m]

        def look(f, _, m=m, brick=brick):
            t = footprints[brick, f]
            k = lax.rem(lax.rem(lax.div(t, tiles), n) + n - y, n)
            e = lax.rem(t, tiles) - plan.across
            fits = (e >= 0) & (e < plan.extra)
            beside[m, jnp.where(fits, k * plan.extra + e, n * plan.extra)] = f
            return 0

        lax.fori_loop(0, footprints.shape[1], look, 0, unroll=8)
    for k in range(n):
        if k != far:

            def cover(t, _, k=k):
                outs[k][t * plan.frag + plan.channels] = opacity[table[k * tiles + t]]
                return 0

            lax.fori_loop(0, tiles, cover, 0, unroll=True)
        tail, at = tails[k]
        for e in range(plan.extra):
            tail[at + e] = before[beside[0, k * plan.extra + e]]
            tail[at + plan.extra + e] = after[beside[1, k * plan.extra + e]]
        tail[at + plan.at_order - plan.at_prev] = orders[...]
        for g in range(plan.at_order + 1, plan.groups):
            tail[at + g - plan.at_prev] = jnp.zeros_like(orders)
    for k in range(n):
        if k != far:
            whole = outs[k].at[pl.ds(0, tiles * plan.channels)]
            pltpu.make_async_copy(whole, whole, sem.at[k]).wait()
    lane = iota((plan.frag, plan.rows, plan.lanes), 2)
    lane_extra = iota((plan.rows, plan.lanes), 1)
    across = plan.across
    for k in range(n):
        right, left = (k + 1) % n, (k - 1) % n
        spread = jnp.zeros((plan.frag, plan.rows, plan.lanes), jnp.float32)
        for j in range(TYD):
            at_r = (j * across) * plan.frag
            at_l = (j * across + across - 1) * plan.frag
            pair = jnp.where(
                lane < 2,
                outs[right][at_r : at_r + plan.frag].astype(jnp.float32),
                outs[left][at_l : at_l + plan.frag].astype(jnp.float32),
            )
            pair = pltpu.roll(pair, 4 * j + 2, 2)
            spread = jnp.where((lane >= 4 * j) & (lane < 4 * j + 4), pair, spread)
        parts = [spread[c] for c in range(plan.frag)]
        for m in range(2):
            extra = jnp.zeros((plan.rows, plan.lanes), jnp.float32)
            for j in range(1, TYD - 1):
                e = m * plan.extra + (j - 1) * across
                pair = jnp.where(
                    lane_extra < 2,
                    tails[right][0][tails[right][1] + e].astype(jnp.float32),
                    tails[left][0][tails[left][1] + e + across - 1].astype(jnp.float32),
                )
                pair = pltpu.roll(pair, 4 * j + 2, 1)
                extra = jnp.where((lane_extra >= 4 * j) & (lane_extra < 4 * j + 4), pair, extra)
            parts.append(extra)
        tail, at = tails[k]
        for i in range(plan.halo):
            group = jnp.zeros((plan.rows, plan.lanes), jnp.float32)
            for b in range(plan.blocks):
                c = i * plan.blocks + b
                if c < len(parts):
                    moved = pltpu.roll(parts[c], SPAN * b, 1) if b else parts[c]
                    group = jnp.where(
                        (lane_extra >= SPAN * b) & (lane_extra < SPAN * b + SPAN), moved, group
                    )
            tail[at + 2 * plan.extra + i] = group.astype(jnp.bfloat16)


def fold(x):
    return x.reshape(x.shape[0] * x.shape[1], x.shape[2])


def blend_kernel(plan, far, alpha_at, weight_at, *rest):
    n, tiles, across = plan.count, plan.tiles, plan.across
    inbox, late, own, sent, alpha, weight, clear = rest[:n], *rest[n:]
    rows, lanes = plan.rows, plan.lanes
    pair = 2 * rows
    frag_rows = plan.frag * rows
    halo_row = plan.at_halo * rows
    opaque = plan.channels * rows
    lane = iota((pair, lanes), 1)

    def doubled(x):
        return jnp.concatenate([x, x], axis=0)

    main = tiles * frag_rows

    def read(k, start, stop):
        if k == far and start >= main:
            return late[start - main : stop - main, :].astype(jnp.float32)
        return inbox[k][start:stop, :].astype(jnp.float32)

    def take(k, row, slot):
        base = row // 16 * 16
        held = read(k, base, base + 16)
        part = held[row - base : row - base + rows]
        alpha[slot] = doubled(part)

    at_p, at_n, at_h = n * tiles, n * (tiles + plan.extra), n * (tiles + 2 * plan.extra)
    for k in range(n):
        for t in range(tiles):
            take(k, t * frag_rows + opaque, k * tiles + t)
        for e in range(plan.extra):
            take(k, (plan.at_prev + e) * rows, at_p + k * plan.extra + e)
            take(k, (plan.at_next + e) * rows, at_n + k * plan.extra + e)
        for m in range(3):
            c = plan.channels + m
            i, b = c // plan.blocks, c % plan.blocks
            row = halo_row + i * rows
            base = row // 16 * 16
            held = read(k, base, base + 16)
            part = doubled(held[row - base : row - base + rows])
            if b:
                part = pltpu.roll(part, lanes - SPAN * b, 1)
            alpha[at_h + m * n + k] = part

    weight[...] = jnp.zeros_like(weight)
    kinds = 4 * (tiles - across)

    def through(i, _):
        seen = jnp.ones((pair, lanes), jnp.float32)
        for d in range(plan.depth):
            weight[weight_at[i * plan.depth + d]] = seen
            seen = seen * (1.0 - alpha[alpha_at[i * plan.depth + d]])
        clear[i] = seen
        return 0

    lax.fori_loop(0, kinds, through, 0, unroll=4)

    most = tiles - across
    step = 3 * pair
    while frag_rows % step or step % 16:
        step += pair
    for t in range(tiles):
        keeps, gives = t >= across, t < tiles - across
        for at in range(0, frag_rows, step):
            shape = (step // pair, pair, lanes)
            total_own = jnp.zeros(shape, jnp.float32)
            total_next = jnp.zeros(shape, jnp.float32)
            for k in range(n):
                start = t * frag_rows + at
                held = inbox[k][start : start + step, :].astype(jnp.float32).reshape(shape)
                if keeps:
                    total_own += weight[k * tiles + t][None] * held
                if gives:
                    total_next += weight[(2 * n + k) * tiles + t][None] * held
            if at + step == frag_rows:
                mask = (iota(shape, 0) == step // pair - 1) & (iota(shape, 1) >= rows)
                if keeps:
                    total_own = jnp.where(mask, 1.0 - clear[t - across][None], total_own)
                whole = jnp.zeros((pair, lanes), jnp.float32)
                if t < across:
                    whole = 1.0 - clear[most + t]
                total_next = jnp.where(mask, whole[None], total_next)
            if keeps:
                start = (t - across) * frag_rows + at
                own[start : start + step, :] = total_own.reshape(step, lanes)
            start = t * frag_rows + at
            total = total_next if gives else total_own
            sent[start : start + step, :] = total.reshape(step, lanes).astype(jnp.bfloat16)

    halo_shape = (plan.halo_pad * rows // pair, pair, lanes)
    span_lane = iota((pair, lanes), 1)

    def merged(kind, source):
        out = jnp.zeros((pair, lanes), jnp.float32)
        first = across if kind == 0 else 0
        for u in range(most):
            v = first + u
            out = jnp.where((span_lane // 2 == v), source(u, v), out)
        return out

    def widened(x):
        out = jnp.zeros((pair, lanes), jnp.float32)
        for b in range(plan.blocks):
            moved = pltpu.roll(x, SPAN * b, 1) if b else x
            out = jnp.where(span_lane // SPAN == b, moved, out)
        return out

    totals = [jnp.zeros(halo_shape, jnp.float32) for _ in range(2)]
    for k in range(n):
        held = read(k, halo_row, halo_row + plan.halo_pad * rows).reshape(halo_shape)
        for kind in range(2):
            base = (2 * kind + 1) * n * tiles + k * tiles
            by = widened(merged(kind, lambda u, v: weight[base + v]))
            totals[kind] += by[None] * held
    i_cov, b_cov = plan.channels // plan.blocks, plan.channels % plan.blocks
    group = iota(halo_shape, 0) * 2 + iota(halo_shape, 1) // rows
    at_cov = (group == i_cov) & (iota(halo_shape, 2) // SPAN == b_cov)
    for kind in range(2):
        cov = merged(kind, lambda u, v: 1.0 - clear[(2 + kind) * most + u])
        if kind == 1:
            cov = jnp.where(span_lane // 4 == 0, cov, 0.0)
        cov = pltpu.roll(cov, SPAN * b_cov, 1) if b_cov else cov
        totals[kind] = jnp.where(at_cov, cov[None], totals[kind])
    unused = group * plan.blocks + iota(halo_shape, 2) // SPAN > plan.channels
    totals = [jnp.where(unused, 0.0, total) for total in totals]
    band = iota(halo_shape, 2) // 4 % TYD
    length = plan.halo_pad * rows
    start = most * frag_rows
    own[start : start + length, :] = totals[0].reshape(length, lanes)
    start = tiles * frag_rows
    both = jnp.where(band == TYD - 1, totals[0], totals[1])
    sent[start : start + length, :] = both.reshape(length, lanes).astype(jnp.bfloat16)


def conv_kernel(plan, feats, spots, panel, own, got, kept, one, top, low, two, keep, b1, b2, *rest):
    out, field, hidden = rest
    tiles, across, rows, lanes = plan.tiles, plan.across, plan.rows, plan.lanes
    frag_rows = plan.frag * rows
    most = tiles - across
    span = across * lanes
    wide = span + lanes
    has_top, has_low = spots[0], spots[1]
    has_left, has_right = spots[2], spots[3]
    zero = jnp.zeros((frag_rows, lanes), jnp.bfloat16)

    def tile(ref, t):
        return ref[t * frag_rows : (t + 1) * frag_rows, :]

    for c in range(across):
        at = slice(c * lanes, (c + 1) * lanes)
        field[0:frag_rows, at] = jnp.where(has_top != 0, tile(got, most + c), zero)
        field[frag_rows : 2 * frag_rows, at] = tile(got, c)
        for j in range(1, TYD):
            value = tile(own, (j - 1) * across + c)
            if j < TYD - 1:
                value = value + tile(got, j * across + c).astype(jnp.float32)
            field[(j + 1) * frag_rows : (j + 2) * frag_rows, at] = value.astype(jnp.bfloat16)
        at_low = (TYD + 1) * frag_rows
        field[at_low : at_low + frag_rows, at] = jnp.where(has_low != 0, tile(kept, c), zero)

    length = plan.halo_pad * rows
    h_own = own[most * frag_rows : most * frag_rows + length, :]
    h_got = got[tiles * frag_rows : tiles * frag_rows + length, :].astype(jnp.float32)
    h_kept = kept[tiles * frag_rows : tiles * frag_rows + length, :].astype(jnp.float32)
    band = iota((length, lanes), 1) // 4 % TYD
    h_all = jnp.where(band == TYD - 1, h_own, h_own + h_got)
    lane = iota((rows, lanes), 1)
    valid = ((lane < 2) & (has_right != 0)) | ((lane >= lanes - 2) & (has_left != 0))

    def unpacked(source, j):
        pieces = []
        for c in range(plan.frag):
            i, b = c // plan.blocks, c % plan.blocks
            piece = source[i * rows : (i + 1) * rows]
            shift = (-(SPAN * b + 4 * j + 2)) % lanes
            pieces.append(jnp.where(valid, pltpu.roll(piece, shift, 1), 0.0))
        return jnp.concatenate(pieces, axis=0).astype(jnp.bfloat16)

    wide_zero = jnp.zeros((frag_rows, lanes), jnp.bfloat16)
    at = slice(span, wide)
    field[0:frag_rows, at] = jnp.where(has_top != 0, unpacked(h_got, TYD - 1), wide_zero)
    for j in range(TYD):
        field[(j + 1) * frag_rows : (j + 2) * frag_rows, at] = unpacked(h_all, j)
    at_low = (TYD + 1) * frag_rows
    field[at_low : at_low + frag_rows, at] = jnp.where(has_low != 0, unpacked(h_kept, 0), wide_zero)

    def shifted_sum(y):
        part = y.shape[0] // 3
        return (
            pltpu.roll(y[:part], 1, 1)
            + y[part : 2 * part]
            + pltpu.roll(y[2 * part :], wide - 1, 1)
        )

    def act(y, bias):
        x = shifted_sum(y) + bias
        return x * (1.0 / (1.0 + jnp.exp(-x)))

    half = 2 * rows
    groups = TYD // 2
    col = iota((1, wide), 1)
    inside = ((col != span) | (has_right != 0)) & ((col != wide - 1) | (has_left != 0))
    for g in range(groups):
        window = field[2 * g * frag_rows : (2 * g + 4) * frag_rows, :]
        y = jnp.dot(one[...], window, preferred_element_type=jnp.float32)
        h = jnp.where(inside, act(y, b1[...]), 0.0)
        at = feats + g * half * feats
        hidden[at : at + half * feats, :] = h.astype(jnp.bfloat16)
    for ref, at_field, at_hidden, has in (
        (top, 0, 0, has_top),
        (low, TYD * frag_rows, feats * (1 + groups * half), has_low),
    ):
        window = field[at_field : at_field + 2 * frag_rows, :]
        y = jnp.dot(ref[...], window, preferred_element_type=jnp.float32)
        h = jnp.where(inside & (has != 0), act(y, b1[0:feats]), 0.0)
        hidden[at_hidden : at_hidden + feats, :] = h.astype(jnp.bfloat16)
    strip = out.shape[1]
    for g in range(groups):
        at = g * half * feats
        window = hidden[at : at + (half + 2) * feats, :]
        y = jnp.dot(two[...], window, preferred_element_type=jnp.float32)
        plain = field[(2 * g + 1) * frag_rows : (2 * g + 3) * frag_rows, 0:span]
        base = jnp.dot(keep[...], plain, preferred_element_type=jnp.float32)
        total = (shifted_sum(y)[:, 0:span] + b2[...] + base).astype(jnp.bfloat16)
        for s in range(half * feats // strip):
            out[panel[g * (half * feats // strip) + s]] = total[s * strip : (s + 1) * strip]


def spread_kernel(plan, feats, outs, w1, w2, one, top, low, two, keep):
    rows, frag = plan.rows, plan.frag
    block = frag * rows
    part = 3 * feats

    def place(shape):
        channel = iota(shape, 0)
        column = iota(shape, 1)
        inner = column % block
        pixel = column // block * rows + inner % rows
        return jnp.where(inner // rows == channel, pixel, -1)

    def taps(weight, i):
        return weight[i * part : (i + 1) * part, :]

    def sums(weight, hit, first):
        total = 0.0
        for i in range(3):
            mask = (hit == first + i).astype(jnp.float32).astype(jnp.bfloat16)
            total = total + jnp.dot(taps(weight, i), mask, preferred_element_type=jnp.float32)
        return total.astype(jnp.bfloat16)

    hit = place((frag, one.shape[1]))
    for q in range(outs):
        rows_q = sums(w1, hit, q + rows - 1)
        for s in range(3):
            at = (s * outs + q) * feats
            one[at : at + feats, :] = rows_q[s * feats : (s + 1) * feats]
        if q == 0:
            low[...] = rows_q[:, : low.shape[1]]
    top[...] = sums(w1, place((frag, top.shape[1])), rows - 2)
    shape = (feats, two.shape[1])
    hit = jnp.where(iota(shape, 1) % feats == iota(shape, 0), iota(shape, 1) // feats, -1)
    for q in range(outs):
        rows_q = sums(w2, hit, q)
        for s in range(3):
            at = (s * outs + q) * feats
            two[at : at + feats, :] = rows_q[s * feats : (s + 1) * feats]
    shape = keep.shape
    inner = iota(shape, 1) % block
    pixel = iota(shape, 1) // block * rows + inner % rows
    same = (iota(shape, 0) // feats == pixel) & (iota(shape, 0) % feats == inner // rows)
    keep[...] = same.astype(jnp.float32).astype(jnp.bfloat16)


def shards(
    payload,
    opacity,
    depth_order,
    footprints,
    panel_map,
    conv1_weight,
    conv1_bias,
    conv2_weight,
    conv2_bias,
):
    row_groups = lax.axis_size("gx")
    n = lax.axis_size("gy")
    x = lax.axis_index("gx")
    y = lax.axis_index("gy")
    _, rows, channels, lanes = payload.shape
    tiles, depth = depth_order.shape
    plan = Plan(n, tiles, rows, channels, lanes, depth)
    feats = conv2_weight.shape[1]
    across = plan.across
    most = tiles - across

    before = rotated(opacity, "gx", 1)
    after = rotated(opacity, "gx", -1)

    me = x * n + y
    prior = (x + row_groups - 1) % row_groups * n + y
    following = (x + 1) % row_groups * n + y
    place = jnp.stack([me, y, prior, following]).astype(jnp.int32)

    spec_s = pl.BlockSpec(memory_space=pltpu.SMEM)
    spec_v = pl.BlockSpec(memory_space=pltpu.VMEM)
    spec_h = pl.BlockSpec(memory_space=pltpu.HBM)
    limit = pltpu.CompilerParams(vmem_limit_bytes=40 << 20)
    far = n // 2
    pixels = payload.transpose(0, 2, 1, 3)

    def message(groups):
        return jax.ShapeDtypeStruct((groups, rows, lanes), payload.dtype)

    def cost(micros):
        return pl.CostEstimate(flops=0, bytes_accessed=int(micros * 3.6e6), transcendentals=0)

    first, table = pl.pallas_call(
        functools.partial(first_kernel, plan, far),
        out_shape=[message(plan.at_prev), jax.ShapeDtypeStruct((n * tiles,), jnp.int32)],
        in_specs=[spec_s] * 2 + [spec_h] * 2,
        out_specs=[spec_v, spec_s],
        scratch_shapes=[pltpu.SemaphoreType.DMA],
        compiler_params=limit,
        cost_estimate=cost(2),
        name="first",
    )(place, footprints, pixels, opacity)

    mine = jnp.stack([depth_order, rotated(depth_order, "gx", -1)])
    flat = mine.reshape(-1).astype(payload.dtype)
    orders = jnp.pad(flat, (0, rows * lanes - flat.shape[0])).reshape(rows, lanes)

    *outs, late = pl.pallas_call(
        functools.partial(pack_kernel, plan, far),
        out_shape=[message(plan.groups)] * (n - 1) + [message(plan.groups - plan.at_prev)],
        in_specs=[spec_s] * 3 + [spec_h] + [spec_v] * 5,
        out_specs=[spec_v] * n,
        scratch_shapes=[
            pltpu.SemaphoreType.DMA((n,)),
            pltpu.SMEM((2, n * plan.extra + 1), jnp.int32),
        ],
        compiler_params=limit,
        cost_estimate=cost(7),
        name="pack",
    )(place, footprints, table, pixels, opacity, before, after, orders, first)
    outs.insert(far, first)
    received = [outs[0]] + [rotated(outs[k], "gy", k) for k in range(1, n)]
    inbox = [fold(r) for r in received]
    late_in = fold(rotated(late, "gy", far))

    def order_of(r):
        return r[plan.at_order].reshape(-1)[: flat.shape[0]].astype(jnp.int32).reshape(mine.shape)

    left, right = order_of(received[1]), order_of(received[n - 1])
    beside = jnp.stack([left[:, across - 1 :: across], right[:, 0::across]], axis=2)
    beside = beside.reshape(2, 2 * TYD, depth)

    def tables(order, kind, halo):
        slots = jnp.arange(order.shape[0], dtype=jnp.int32)[:, None] + (across if kind == 0 else 0)
        k = (y - order % n) % n
        local = order // n == x
        other = jnp.clip(slots - across, 0, plan.extra - 1)
        if halo:
            base = n * (tiles + 2 * plan.extra)
            source = base + jnp.where(local, 0, (1 + kind) * n) + k
        else:
            base = n * (tiles + kind * plan.extra)
            source = jnp.where(local, k * tiles + slots, base + k * plan.extra + other)
        target = (2 * kind + halo) * n * tiles + k * tiles + slots
        return source, jnp.where(local, target, 4 * n * tiles)

    pieces = [
        tables(mine[0, across:], 0, 0),
        tables(mine[1, :most], 1, 0),
        tables(beside[0, across:], 0, 1),
        tables(beside[1, :most], 1, 1),
    ]
    alpha_at = jnp.concatenate([a for a, _ in pieces]).reshape(-1)
    weight_at = jnp.concatenate([w for _, w in pieces]).reshape(-1)

    frag_rows = plan.frag * rows
    tail = plan.halo_pad * rows
    own, sent = pl.pallas_call(
        functools.partial(blend_kernel, plan, far),
        out_shape=[
            jax.ShapeDtypeStruct((most * frag_rows + tail, lanes), jnp.float32),
            jax.ShapeDtypeStruct((tiles * frag_rows + tail, lanes), jnp.bfloat16),
        ],
        in_specs=[spec_s] * 2 + [spec_v] * (n + 1),
        out_specs=[spec_v] * 2,
        scratch_shapes=[
            pltpu.VMEM((n * (tiles + 2 * plan.extra + 3), 2 * rows, lanes), jnp.float32),
            pltpu.VMEM((4 * n * tiles + 1, 2 * rows, lanes), jnp.float32),
            pltpu.VMEM((4 * most, 2 * rows, lanes), jnp.float32),
        ],
        compiler_params=limit,
        cost_estimate=cost(3),
        name="blend",
    )(alpha_at, weight_at, *inbox, late_in)
    got = rotated(sent, "gx", 1)

    half = 2 * rows
    w1, w2, _ = lax.optimization_barrier((conv1_weight, conv2_weight, late))
    w1 = w1.reshape(-1, w1.shape[2])
    w2 = w2.reshape(-1, w2.shape[2])

    def matrix(height, width):
        return jax.ShapeDtypeStruct((height, width), payload.dtype)

    one, top, low, two, keep = pl.pallas_call(
        functools.partial(spread_kernel, plan, feats, half),
        out_shape=[
            matrix(3 * half * feats, 4 * frag_rows),
            matrix(3 * feats, 2 * frag_rows),
            matrix(3 * feats, 2 * frag_rows),
            matrix(3 * half * feats, (half + 2) * feats),
            matrix(half * feats, 2 * frag_rows),
        ],
        in_specs=[spec_v] * 2,
        out_specs=[spec_v] * 5,
        compiler_params=limit,
        cost_estimate=cost(4),
        name="spread",
    )(w1, w2)
    b1 = jnp.tile(conv1_bias, half)[:, None]
    b2 = jnp.tile(conv2_bias, half)[:, None]
    spots = jnp.stack([x > 0, x < row_groups - 1, y > 0, y < n - 1]).astype(jnp.int32)
    band = TYD * rows
    strip = band // n
    span = across * lanes
    pieces = pl.pallas_call(
        functools.partial(conv_kernel, plan, feats),
        out_shape=jax.ShapeDtypeStruct((n, strip * feats, span), jnp.bfloat16),
        in_specs=[spec_s] * 2 + [spec_v] * 10,
        out_specs=spec_v,
        scratch_shapes=[
            pltpu.VMEM(((TYD + 2) * frag_rows, span + lanes), jnp.bfloat16),
            pltpu.VMEM(((band + 2) * feats, span + lanes), jnp.bfloat16),
        ],
        compiler_params=limit,
        cost_estimate=cost(4),
        name="conv",
    )(spots, panel_map, own, got, sent, one, top, low, two, keep, b1, b2)
    shown = lax.all_to_all(pieces, "gy", split_axis=0, concat_axis=0, tiled=True)
    shown = shown.transpose(1, 0, 2).reshape(1, 1, strip, feats, n * span)
    return shown


def solution(mesh):
    return jax.shard_map(
        shards,
        mesh=mesh,
        in_specs=(
            P(("gx", "gy"), None, None, None),
            P(("gx", "gy"), None, None),
            P(("gx", "gy"), None),
            P(),
            P(),
            P(),
            P(),
            P(),
            P(),
        ),
        out_specs=P("gx", "gy", None, None, None),
        check_vma=False,
    )
```

```python
import functools

import jax
import jax.numpy as jnp
from jax import lax
from jax.experimental import pallas as pl
from jax.experimental.pallas import tpu as pltpu
from jax.sharding import PartitionSpec as P

TYD = 4
SPAN = 4 * TYD


def rotated(block, axis, distance):
    count = lax.axis_size(axis)
    return lax.ppermute(block, axis, [(i, (i + distance) % count) for i in range(count)])


def paired(block, axis, step):
    return lax.ppermute(block, axis, [(i, i ^ step) for i in range(lax.axis_size(axis))])


def split(value, size):
    if size & (size - 1) == 0:
        return value >> (size.bit_length() - 1), value & (size - 1)
    return lax.div(value, size), lax.rem(value, size)


def iota(shape, dim):
    return lax.broadcasted_iota(jnp.int32, shape, dim)


class Plan:
    def __init__(self, count, tiles, rows, channels, lanes, depth):
        self.count = count
        self.half = count // 2
        self.tiles = tiles
        self.across = tiles // TYD
        self.rows = rows
        self.channels = channels
        self.lanes = lanes
        self.depth = depth
        self.frag = channels + 1
        self.blocks = lanes // SPAN
        self.halo = -(-self.frag // self.blocks)
        self.at_halo = tiles * self.frag
        per = 16 // rows
        self.groups = -(-(self.at_halo + self.halo) // per) * per
        self.halo_pad = self.groups - self.at_halo
        self.thin = -(-(tiles + 2) // 2) * 2
        self.thin_pair = -(-2 * self.thin // per) * per


def neighbours(plan, column):
    n, tiles = plan.count, plan.tiles
    right = jnp.where(column == n - 1, 0, column + 1) * tiles
    left = jnp.where(column == 0, n - 1, column - 1) * tiles + plan.across - 1
    return right, left


def joined(right, left, j, lane, axis):
    both = jnp.where(lane < 2, right.astype(jnp.float32), left.astype(jnp.float32))
    return pltpu.roll(both, 4 * j + 2, axis)


def thin_part(plan, table, opacity, order, out):
    n, tiles = plan.count, plan.tiles
    lane = iota((plan.rows, plan.lanes), 1)
    empty = jnp.zeros((plan.rows, plan.lanes), jnp.bfloat16)
    for d in range(n):
        places = [(d, 0), (d ^ plan.half, plan.thin)]
        for t in range(tiles):
            group = opacity[table[d * tiles + t]]
            for to, at in places:
                out[to, at + t] = group
        right = (d + 1) % n * tiles
        left = (d - 1) % n * tiles + plan.across - 1
        halo = jnp.zeros((plan.rows, plan.lanes), jnp.float32)
        for j in range(TYD):
            f_r, f_l = table[right + j * plan.across], table[left + j * plan.across]
            inside = (lane >= 4 * j) & (lane < 4 * j + 4)
            halo = jnp.where(inside, joined(opacity[f_r], opacity[f_l], j, lane, 1), halo)
        for to, at in places:
            out[to, at + tiles] = halo.astype(jnp.bfloat16)
        for i in range(2):
            out[d, i * plan.thin + tiles + 1] = order[i * plan.rows : (i + 1) * plan.rows]
            for g in range(tiles + 2, plan.thin):
                out[d, i * plan.thin + g] = empty
        for g in range(2 * plan.thin, plan.thin_pair):
            out[d, g] = empty


def send_fragments(plan, columns, table, payload, outs, sem):
    for e, column in enumerate(columns):

        def move(t, _, e=e, column=column):
            f = table[column * plan.tiles + t]
            pltpu.make_async_copy(
                payload.at[f], outs[e].at[pl.ds(t * plan.frag, plan.channels)], sem.at[e]
            ).start()
            return 0

        lax.fori_loop(0, plan.tiles, move, 0)


def add_edges(plan, columns, table, payload, opacity, outs):
    across = plan.across
    lane = iota((plan.channels, plan.rows, plan.lanes), 2)
    lane_one = iota((plan.rows, plan.lanes), 1)
    for out, column in zip(outs, columns):
        for t in range(plan.tiles):
            out[t * plan.frag + plan.channels] = opacity[table[column * plan.tiles + t]]
        right, left = neighbours(plan, column)
        spread = jnp.zeros((plan.channels, plan.rows, plan.lanes), jnp.float32)
        for j in range(TYD):
            f_r, f_l = table[right + j * across], table[left + j * across]
            inside = (lane >= 4 * j) & (lane < 4 * j + 4)
            spread = jnp.where(inside, joined(payload[f_r], payload[f_l], j, lane, 2), spread)
        for i in range(plan.halo_pad):
            group = jnp.zeros((plan.rows, plan.lanes), jnp.float32)
            for b in range(plan.blocks):
                c = i * plan.blocks + b
                if c < plan.channels:
                    moved = pltpu.roll(spread[c], SPAN * b, 1) if b else spread[c]
                    group = jnp.where(
                        (lane_one >= SPAN * b) & (lane_one < SPAN * b + SPAN), moved, group
                    )
            out[plan.at_halo + i] = group.astype(jnp.bfloat16)


def await_fragments(plan, outs, sem):
    for e, out in enumerate(outs):
        whole = out.at[pl.ds(0, plan.tiles * plan.channels)]
        pltpu.make_async_copy(whole, whole, sem.at[e]).wait()


def first_kernel(plan, footprints, depth_order, payload, opacity, *rest):
    n, tiles, half = plan.count, plan.tiles, plan.half
    outs = rest[:half]
    thin, table, held, cover, sem, sem_held, sem_cover = rest[half:]
    x, y = lax.axis_index("gx"), lax.axis_index("gy")
    me = x * n + y
    bring_cover = pltpu.make_async_copy(opacity, cover, sem_cover)
    bring_cover.start()
    bring = pltpu.make_async_copy(payload, held, sem_held)
    bring.start()

    def look(f, _):
        owner, slot = split(footprints[me, f], tiles)
        table[split(owner, n)[1] * tiles + slot] = f
        return 0

    lax.fori_loop(0, footprints.shape[1], look, 0, unroll=8)
    columns = [y ^ half ^ k for k in range(half)]
    send_fragments(plan, columns, table, payload, outs, sem)
    order = depth_order[...].astype(jnp.float32)
    order = jnp.concatenate(
        [order, jnp.zeros((tiles, plan.lanes - plan.depth), jnp.float32)], axis=1
    ).astype(jnp.bfloat16)
    bring_cover.wait()
    thin_part(plan, table, cover, order, thin)
    bring.wait()
    add_edges(plan, columns, table, held, cover, outs)
    await_fragments(plan, outs, sem)


def pack_kernel(plan, table, payload, opacity, out, sem):
    half = plan.half
    y = lax.axis_index("gy")
    base = y - (y & (half - 1))
    columns = [base + e for e in range(half)]
    outs = [out.at[e] for e in range(half)]
    send_fragments(plan, columns, table, payload, outs, sem)
    add_edges(plan, columns, table, payload, opacity, outs)
    await_fragments(plan, outs, sem)


def fold(x):
    return x.reshape(x.shape[0] * x.shape[1], x.shape[2])


def blend_kernel(plan, mirror, alpha_at, weight_at, own_in, prev_in, next_in, *rest):
    *inbox, out_own, out_next, alpha, weight, clear = rest
    n, tiles, across, sources = plan.count, plan.tiles, plan.across, plan.half
    rows, lanes = plan.rows, plan.lanes
    pair = 2 * rows
    frag_rows = plan.frag * rows
    halo_row = plan.at_halo * rows
    message = plan.groups * rows
    lane = iota((pair, lanes), 1)
    most = tiles - across

    def read(k, start, stop):
        ref, at = (inbox[k], 0) if mirror else (inbox[0], k * message)
        return ref[at + start : at + stop, :].astype(jnp.float32)

    for kind, ref in enumerate((own_in, prev_in, next_in)):
        for s in range(n):
            for t in range(tiles + 1):
                if kind and t < tiles and not across <= t < most:
                    continue
                row = (s * plan.thin_pair + mirror * plan.thin + t) * rows
                base = row // 16 * 16
                held = ref[base : base + 16, :].astype(jnp.float32)
                part = held[row - base : row - base + rows]
                alpha[(kind * n + s) * (tiles + 1) + t] = jnp.concatenate([part, part], axis=0)

    weight[...] = jnp.zeros_like(weight)

    def through(i, _):
        seen = jnp.ones((pair, lanes), jnp.float32)
        for d in range(plan.depth):
            weight[weight_at[i * plan.depth + d]] = seen
            seen = seen * (1.0 - alpha[alpha_at[i * plan.depth + d]])
        clear[i] = seen
        return 0

    lax.fori_loop(0, 4 * most, through, 0, unroll=4)

    step = 3 * pair
    while frag_rows % step or step % 16:
        step += pair
    shape = (step // pair, pair, lanes)
    for t in range(tiles):
        keeps, gives = t >= across, t < most
        for at in range(0, frag_rows, step):
            total_own = jnp.zeros(shape, jnp.float32)
            total_next = jnp.zeros(shape, jnp.float32)
            for k in range(sources):
                start = t * frag_rows + at
                held = read(k, start, start + step).reshape(shape)
                if keeps:
                    total_own += weight[k * tiles + t][None] * held
                if gives:
                    total_next += weight[(2 * sources + k) * tiles + t][None] * held
            if at + step == frag_rows:
                mask = (iota(shape, 0) == step // pair - 1) & (iota(shape, 1) >= rows)
                cover = jnp.zeros((pair, lanes), jnp.float32)
                if keeps and not mirror:
                    cover = 1.0 - clear[t - across]
                total_own = jnp.where(mask, cover[None], total_own)
                cover = jnp.zeros((pair, lanes), jnp.float32)
                if t < across and not mirror:
                    cover = 1.0 - clear[most + t]
                total_next = jnp.where(mask, cover[None], total_next)
            start = t * frag_rows + at
            total = total_next if gives else total_own
            out_next[start : start + step, :] = total.reshape(step, lanes).astype(jnp.bfloat16)
            if mirror:
                total = total_own if keeps else total_next
                out_own[start : start + step, :] = total.reshape(step, lanes).astype(jnp.bfloat16)
            elif keeps:
                start = (t - across) * frag_rows + at
                out_own[start : start + step, :] = total_own.reshape(step, lanes)

    halo_shape = (plan.halo_pad * rows // pair, pair, lanes)

    def merged(kind, source):
        out = jnp.zeros((pair, lanes), jnp.float32)
        first = across if kind == 0 else 0
        for u in range(most):
            out = jnp.where(lane // 2 == first + u, source(u, first + u), out)
        return out

    def widened(x):
        out = jnp.zeros((pair, lanes), jnp.float32)
        for b in range(plan.blocks):
            moved = pltpu.roll(x, SPAN * b, 1) if b else x
            out = jnp.where(lane // SPAN == b, moved, out)
        return out

    totals = [jnp.zeros(halo_shape, jnp.float32) for _ in range(2)]
    for k in range(sources):
        held = read(k, halo_row, halo_row + plan.halo_pad * rows).reshape(halo_shape)
        for kind in range(2):
            base = (2 * kind + 1) * sources * tiles + k * tiles
            by = widened(merged(kind, lambda u, v: weight[base + v]))
            totals[kind] += by[None] * held
    if not mirror:
        i_cov, b_cov = plan.channels // plan.blocks, plan.channels % plan.blocks
        group = iota(halo_shape, 0) * 2 + iota(halo_shape, 1) // rows
        at_cov = (group == i_cov) & (iota(halo_shape, 2) // SPAN == b_cov)
        for kind in range(2):
            cov = merged(kind, lambda u, v: 1.0 - clear[(2 + kind) * most + u])
            if kind == 1:
                cov = jnp.where(lane // 4 == 0, cov, 0.0)
            cov = pltpu.roll(cov, SPAN * b_cov, 1) if b_cov else cov
            totals[kind] = jnp.where(at_cov, cov[None], totals[kind])
    band = iota(halo_shape, 2) // 4 % TYD
    length = plan.halo_pad * rows
    start = tiles * frag_rows
    both = jnp.where(band == TYD - 1, totals[0], totals[1])
    out_next[start : start + length, :] = both.reshape(length, lanes).astype(jnp.bfloat16)
    if mirror:
        both = jnp.where(band == 0, totals[1], totals[0])
        out_own[start : start + length, :] = both.reshape(length, lanes).astype(jnp.bfloat16)
    else:
        start = most * frag_rows
        out_own[start : start + length, :] = totals[0].reshape(length, lanes)


def conv_kernel(
    plan, feats, spots, panel, own, kept, got, over, cross, one, top, low, two, keep, b1, b2, *rest
):
    out, field, hidden = rest
    tiles, across, rows, lanes = plan.tiles, plan.across, plan.rows, plan.lanes
    frag_rows = plan.frag * rows
    most = tiles - across
    span = across * lanes
    wide = span + lanes
    has_top, has_low = spots[0], spots[1]
    has_left, has_right = spots[2], spots[3]

    def tile(*refs, t):
        total = 0.0
        for ref in refs:
            total = total + ref[t * frag_rows : (t + 1) * frag_rows, :].astype(jnp.float32)
        return total

    for c in range(across):
        at = slice(c * lanes, (c + 1) * lanes)
        value = jnp.where(has_top != 0, tile(got, cross, t=most + c), 0.0)
        field[0:frag_rows, at] = value.astype(jnp.bfloat16)
        for j in range(TYD):
            if j == 0:
                value = tile(got, cross, t=c)
            elif j < TYD - 1:
                value = tile(got, cross, over, t=j * across + c)
            else:
                value = tile(over, t=j * across + c)
            if j > 0:
                value = value + tile(own, t=(j - 1) * across + c)
            field[(j + 1) * frag_rows : (j + 2) * frag_rows, at] = value.astype(jnp.bfloat16)
        at_low = (TYD + 1) * frag_rows
        value = jnp.where(has_low != 0, tile(kept, over, t=c), 0.0)
        field[at_low : at_low + frag_rows, at] = value.astype(jnp.bfloat16)

    length = plan.halo_pad * rows

    def edge(ref):
        return ref[tiles * frag_rows : tiles * frag_rows + length, :].astype(jnp.float32)

    h_own = own[most * frag_rows : most * frag_rows + length, :]
    h_over = edge(over)
    h_got = edge(got) + edge(cross)
    h_kept = edge(kept) + h_over
    band = iota((length, lanes), 1) // 4 % TYD
    h_here = h_own + h_over
    h_all = jnp.where(band == TYD - 1, h_here, jnp.where(band == 0, h_got, h_here + h_got))
    lane = iota((rows, lanes), 1)
    valid = ((lane < 2) & (has_right != 0)) | ((lane >= lanes - 2) & (has_left != 0))

    def unpacked(source, j):
        pieces = []
        for c in range(plan.frag):
            i, b = c // plan.blocks, c % plan.blocks
            piece = source[i * rows : (i + 1) * rows]
            shift = (-(SPAN * b + 4 * j + 2)) % lanes
            pieces.append(jnp.where(valid, pltpu.roll(piece, shift, 1), 0.0))
        return jnp.concatenate(pieces, axis=0).astype(jnp.bfloat16)

    wide_zero = jnp.zeros((frag_rows, lanes), jnp.bfloat16)
    at = slice(span, wide)
    field[0:frag_rows, at] = jnp.where(has_top != 0, unpacked(h_got, TYD - 1), wide_zero)
    for j in range(TYD):
        field[(j + 1) * frag_rows : (j + 2) * frag_rows, at] = unpacked(h_all, j)
    at_low = (TYD + 1) * frag_rows
    field[at_low : at_low + frag_rows, at] = jnp.where(has_low != 0, unpacked(h_kept, 0), wide_zero)

    def shifted_sum(y):
        part = y.shape[0] // 3
        return (
            pltpu.roll(y[:part], 1, 1)
            + y[part : 2 * part]
            + pltpu.roll(y[2 * part :], wide - 1, 1)
        )

    def act(y, bias):
        x = shifted_sum(y) + bias
        return x * (1.0 / (1.0 + jnp.exp(-x)))

    half = 2 * rows
    groups = TYD // 2
    col = iota((1, wide), 1)
    inside = ((col != span) | (has_right != 0)) & ((col != wide - 1) | (has_left != 0))
    for g in range(groups):
        window = field[2 * g * frag_rows : (2 * g + 4) * frag_rows, :]
        y = jnp.dot(one[...], window, preferred_element_type=jnp.float32)
        h = jnp.where(inside, act(y, b1[...]), 0.0)
        at = feats + g * half * feats
        hidden[at : at + half * feats, :] = h.astype(jnp.bfloat16)
    for ref, at_field, at_hidden, has in (
        (top, 0, 0, has_top),
        (low, TYD * frag_rows, feats * (1 + groups * half), has_low),
    ):
        window = field[at_field : at_field + 2 * frag_rows, :]
        y = jnp.dot(ref[...], window, preferred_element_type=jnp.float32)
        h = jnp.where(inside & (has != 0), act(y, b1[0:feats]), 0.0)
        hidden[at_hidden : at_hidden + feats, :] = h.astype(jnp.bfloat16)
    strip = out.shape[1]
    for g in range(groups):
        at = g * half * feats
        window = hidden[at : at + (half + 2) * feats, :]
        y = jnp.dot(two[...], window, preferred_element_type=jnp.float32)
        plain = field[(2 * g + 1) * frag_rows : (2 * g + 3) * frag_rows, 0:span]
        base = jnp.dot(keep[...], plain, preferred_element_type=jnp.float32)
        total = (shifted_sum(y)[:, 0:span] + b2[...] + base).astype(jnp.bfloat16)
        for s in range(half * feats // strip):
            out[panel[g * (half * feats // strip) + s]] = total[s * strip : (s + 1) * strip]


def spread_kernel(plan, feats, outs, w1, w2, one, top, low, two, keep):
    rows, frag = plan.rows, plan.frag
    block = frag * rows
    part = 3 * feats

    def place(shape):
        channel = iota(shape, 0)
        column = iota(shape, 1)
        inner = column % block
        pixel = column // block * rows + inner % rows
        return jnp.where(inner // rows == channel, pixel, -1)

    def taps(weight, i):
        return weight[i * part : (i + 1) * part, :]

    def sums(weight, hit, first):
        total = 0.0
        for i in range(3):
            mask = (hit == first + i).astype(jnp.float32).astype(jnp.bfloat16)
            total = total + jnp.dot(taps(weight, i), mask, preferred_element_type=jnp.float32)
        return total.astype(jnp.bfloat16)

    hit = place((frag, one.shape[1]))
    for q in range(outs):
        rows_q = sums(w1, hit, q + rows - 1)
        for s in range(3):
            at = (s * outs + q) * feats
            one[at : at + feats, :] = rows_q[s * feats : (s + 1) * feats]
        if q == 0:
            low[...] = rows_q[:, : low.shape[1]]
    top[...] = sums(w1, place((frag, top.shape[1])), rows - 2)
    shape = (feats, two.shape[1])
    hit = jnp.where(iota(shape, 1) % feats == iota(shape, 0), iota(shape, 1) // feats, -1)
    for q in range(outs):
        rows_q = sums(w2, hit, q)
        for s in range(3):
            at = (s * outs + q) * feats
            two[at : at + feats, :] = rows_q[s * feats : (s + 1) * feats]
    shape = keep.shape
    inner = iota(shape, 1) % block
    pixel = iota(shape, 1) // block * rows + inner % rows
    same = (iota(shape, 0) // feats == pixel) & (iota(shape, 0) % feats == inner // rows)
    keep[...] = same.astype(jnp.float32).astype(jnp.bfloat16)


def shards(
    payload,
    opacity,
    depth_order,
    footprints,
    panel_map,
    conv1_weight,
    conv1_bias,
    conv2_weight,
    conv2_bias,
):
    row_groups = lax.axis_size("gx")
    n = lax.axis_size("gy")
    x = lax.axis_index("gx")
    y = lax.axis_index("gy")
    _, rows, channels, lanes = payload.shape
    tiles, depth = depth_order.shape
    plan = Plan(n, tiles, rows, channels, lanes, depth)
    feats = conv2_weight.shape[1]
    across = plan.across
    most = tiles - across

    half = n // 2
    spec_s = pl.BlockSpec(memory_space=pltpu.SMEM)
    spec_v = pl.BlockSpec(memory_space=pltpu.VMEM)
    spec_h = pl.BlockSpec(memory_space=pltpu.HBM)
    limit = pltpu.CompilerParams(vmem_limit_bytes=40 << 20)
    pixels = payload.transpose(0, 2, 1, 3)

    def cost(micros):
        return pl.CostEstimate(flops=0, bytes_accessed=int(micros * 3.6e6), transcendentals=0)

    message = jax.ShapeDtypeStruct((plan.groups, rows, lanes), payload.dtype)
    *packed, thin, table = pl.pallas_call(
        functools.partial(first_kernel, plan),
        out_shape=[message] * half
        + [
            jax.ShapeDtypeStruct((n, plan.thin_pair, rows, lanes), payload.dtype),
            jax.ShapeDtypeStruct((n * tiles,), jnp.int32),
        ],
        in_specs=[spec_s, spec_v, spec_h, spec_h],
        out_specs=[spec_v] * (half + 1) + [spec_s],
        scratch_shapes=[
            pltpu.VMEM(pixels.shape, payload.dtype),
            pltpu.VMEM(opacity.shape, payload.dtype),
            pltpu.SemaphoreType.DMA((half,)),
            pltpu.SemaphoreType.DMA,
            pltpu.SemaphoreType.DMA,
        ],
        compiler_params=pltpu.CompilerParams(vmem_limit_bytes=60 << 20),
        cost_estimate=cost(5),
        name="first",
    )(footprints, depth_order, pixels, opacity)
    inbox_mirror = [packed[0]] + [paired(packed[k], "gy", k) for k in range(1, half)]
    inbox_mirror = [block.reshape(-1, lanes) for block in inbox_mirror]

    thin = lax.all_to_all(thin, "gy", split_axis=0, concat_axis=0, tiled=True)
    thins = [thin, rotated(thin, "gx", 1), rotated(thin, "gx", -1)]

    near = [list(range(i, i + half)) for i in range(0, n, half)]
    inbox_own = pl.pallas_call(
        functools.partial(pack_kernel, plan),
        out_shape=jax.ShapeDtypeStruct((half, plan.groups, rows, lanes), payload.dtype),
        in_specs=[spec_s] + [spec_v] * 2,
        out_specs=spec_v,
        scratch_shapes=[pltpu.SemaphoreType.DMA((half,))],
        compiler_params=limit,
        cost_estimate=cost(4),
        name="pack",
    )(table, pixels, opacity)
    inbox_own = lax.all_to_all(
        inbox_own, "gy", split_axis=0, concat_axis=0, axis_index_groups=near, tiled=True
    )
    inbox_own = [inbox_own.reshape(-1, lanes)]

    def order_of(block):
        block = block[:, tiles + 1 : 2 * plan.thin : plan.thin]
        return block.astype(jnp.int32).reshape(n, 2 * rows, lanes)[:, :tiles, :depth]

    orders = [order_of(thins[0]), order_of(thins[2])]
    thins = [block.reshape(-1, lanes) for block in thins]

    def tables(order, kind, halo, mirror):
        slots = jnp.arange(order.shape[0], dtype=jnp.int32)[:, None] + (across if kind == 0 else 0)
        column = order % n
        local = order // n == x
        source = jnp.where(local, 0, 1 + kind) * n + column
        source = source * (tiles + 1) + (tiles if halo else slots)
        mine = local & (column // half == y // half)
        sender = (column ^ y) % half if mirror else column % half
        target = ((2 * kind + halo) * half + sender) * tiles + slots
        return source, jnp.where(mine, target, 4 * half * tiles)

    frag_rows = plan.frag * rows
    tail = plan.halo_pad * rows

    def blend(mirror, inbox):
        column = y ^ half if mirror else y

        def beside_of(order, step):
            return lax.dynamic_index_in_dim(order, (column + n + step) % n, 0, keepdims=False)

        here = [beside_of(order, 0) for order in orders]
        beside = [
            jnp.stack(
                [beside_of(order, -1)[across - 1 :: across], beside_of(order, 1)[0::across]], axis=1
            ).reshape(2 * TYD, depth)
            for order in orders
        ]
        pieces = [
            tables(here[0][across:], 0, 0, mirror),
            tables(here[1][:most], 1, 0, mirror),
            tables(beside[0][across:], 0, 1, mirror),
            tables(beside[1][:most], 1, 1, mirror),
        ]
        alpha_at = jnp.concatenate([a for a, _ in pieces]).reshape(-1)
        weight_at = jnp.concatenate([w for _, w in pieces]).reshape(-1)
        sums = jax.ShapeDtypeStruct((tiles * frag_rows + tail, lanes), payload.dtype)
        local = jax.ShapeDtypeStruct((most * frag_rows + tail, lanes), jnp.float32)
        return pl.pallas_call(
            functools.partial(blend_kernel, plan, mirror),
            out_shape=[sums if mirror else local, sums],
            in_specs=[spec_s] * 2 + [spec_v] * (3 + len(inbox)),
            out_specs=[spec_v] * 2,
            scratch_shapes=[
                pltpu.VMEM((3 * n * (tiles + 1), 2 * rows, lanes), jnp.float32),
                pltpu.VMEM((4 * half * tiles + 1, 2 * rows, lanes), jnp.float32),
                pltpu.VMEM((4 * most, 2 * rows, lanes), jnp.float32),
            ],
            compiler_params=limit,
            cost_estimate=cost(3),
            name="blend_mirror" if mirror else "blend_own",
        )(alpha_at, weight_at, *thins, *inbox)

    over, cross = blend(1, inbox_mirror)
    over = paired(over, "gy", half)
    route = [
        (i * n + j, (i + 1) % row_groups * n + (j ^ half))
        for i in range(row_groups)
        for j in range(n)
    ]
    cross = lax.ppermute(cross, ("gx", "gy"), route)
    own, kept = blend(0, inbox_own)
    got = rotated(kept, "gx", 1)

    band_half = 2 * rows
    w1, w2, _ = lax.optimization_barrier((conv1_weight, conv2_weight, table))
    w1 = w1.reshape(-1, w1.shape[2])
    w2 = w2.reshape(-1, w2.shape[2])

    def matrix(height, width):
        return jax.ShapeDtypeStruct((height, width), payload.dtype)

    one, top, low, two, keep = pl.pallas_call(
        functools.partial(spread_kernel, plan, feats, band_half),
        out_shape=[
            matrix(3 * band_half * feats, 4 * frag_rows),
            matrix(3 * feats, 2 * frag_rows),
            matrix(3 * feats, 2 * frag_rows),
            matrix(3 * band_half * feats, (band_half + 2) * feats),
            matrix(band_half * feats, 2 * frag_rows),
        ],
        in_specs=[spec_v] * 2,
        out_specs=[spec_v] * 5,
        compiler_params=limit,
        cost_estimate=cost(4),
        name="spread",
    )(w1, w2)
    b1 = jnp.tile(conv1_bias, band_half)[:, None]
    b2 = jnp.tile(conv2_bias, band_half)[:, None]
    spots = jnp.stack([x > 0, x < row_groups - 1, y > 0, y < n - 1]).astype(jnp.int32)
    band = TYD * rows
    strip = band // n
    span = across * lanes
    pieces = pl.pallas_call(
        functools.partial(conv_kernel, plan, feats),
        out_shape=jax.ShapeDtypeStruct((n, strip * feats, span), jnp.bfloat16),
        in_specs=[spec_s] * 2 + [spec_v] * 12,
        out_specs=spec_v,
        scratch_shapes=[
            pltpu.VMEM(((TYD + 2) * frag_rows, span + lanes), jnp.bfloat16),
            pltpu.VMEM(((band + 2) * feats, span + lanes), jnp.bfloat16),
        ],
        compiler_params=limit,
        cost_estimate=cost(4),
        name="conv",
    )(spots, panel_map, own, kept, got, over, cross, one, top, low, two, keep, b1, b2)
    shown = lax.all_to_all(pieces, "gy", split_axis=0, concat_axis=0, tiled=True)
    shown = shown.transpose(1, 0, 2).reshape(1, 1, strip, feats, n * span)
    return shown


def solution(mesh):
    return jax.shard_map(
        shards,
        mesh=mesh,
        in_specs=(
            P(("gx", "gy"), None, None, None),
            P(("gx", "gy"), None, None),
            P(("gx", "gy"), None),
            P(),
            P(),
            P(),
            P(),
            P(),
            P(),
        ),
        out_specs=P("gx", "gy", None, None, None),
        check_vma=False,
    )
```

```python
import functools

import jax
import jax.numpy as jnp
from jax import lax
from jax.experimental import pallas as pl
from jax.experimental.pallas import tpu as pltpu
from jax.sharding import PartitionSpec as P

TYD = 4
SPAN = 4 * TYD


def rotated(block, axis, distance):
    count = lax.axis_size(axis)
    return lax.ppermute(block, axis, [(i, (i + distance) % count) for i in range(count)])


def paired(block, axis, step):
    return lax.ppermute(block, axis, [(i, i ^ step) for i in range(lax.axis_size(axis))])


def split(value, size):
    if size & (size - 1) == 0:
        return value >> (size.bit_length() - 1), value & (size - 1)
    return lax.div(value, size), lax.rem(value, size)


def iota(shape, dim):
    return lax.broadcasted_iota(jnp.int32, shape, dim)


class Plan:
    def __init__(self, count, tiles, rows, channels, lanes, depth):
        self.count = count
        self.half = count // 2
        self.tiles = tiles
        self.across = tiles // TYD
        self.rows = rows
        self.channels = channels
        self.lanes = lanes
        self.depth = depth
        self.frag = channels + 1
        self.blocks = lanes // SPAN
        self.halo = -(-self.frag // self.blocks)
        self.at_halo = tiles * self.frag
        per = 16 // rows
        self.groups = -(-(self.at_halo + self.halo) // per) * per
        self.halo_pad = self.groups - self.at_halo
        self.thin = -(-(tiles + 2) // 2) * 2
        self.thin_pair = -(-2 * self.thin // per) * per


def neighbours(plan, column):
    n, tiles = plan.count, plan.tiles
    right = jnp.where(column == n - 1, 0, column + 1) * tiles
    left = jnp.where(column == 0, n - 1, column - 1) * tiles + plan.across - 1
    return right, left


def joined(right, left, j, lane, axis):
    both = jnp.where(lane < 2, right.astype(jnp.float32), left.astype(jnp.float32))
    return pltpu.roll(both, 4 * j + 2, axis)


def thin_part(plan, table, opacity, order, out):
    n, tiles = plan.count, plan.tiles
    lane = iota((plan.rows, plan.lanes), 1)
    empty = jnp.zeros((plan.rows, plan.lanes), jnp.bfloat16)
    for d in range(n):
        places = [(d, 0), (d ^ plan.half, plan.thin)]
        for t in range(tiles):
            group = opacity[table[d * tiles + t]]
            for to, at in places:
                out[to, at + t] = group
        right = (d + 1) % n * tiles
        left = (d - 1) % n * tiles + plan.across - 1
        halo = jnp.zeros((plan.rows, plan.lanes), jnp.float32)
        for j in range(TYD):
            f_r, f_l = table[right + j * plan.across], table[left + j * plan.across]
            inside = (lane >= 4 * j) & (lane < 4 * j + 4)
            halo = jnp.where(inside, joined(opacity[f_r], opacity[f_l], j, lane, 1), halo)
        for to, at in places:
            out[to, at + tiles] = halo.astype(jnp.bfloat16)
        for i in range(2):
            out[d, i * plan.thin + tiles + 1] = order[i * plan.rows : (i + 1) * plan.rows]
            for g in range(tiles + 2, plan.thin):
                out[d, i * plan.thin + g] = empty
        for g in range(2 * plan.thin, plan.thin_pair):
            out[d, g] = empty


def send_fragments(plan, columns, table, payload, outs, sem):
    for e, column in enumerate(columns):

        def move(t, _, e=e, column=column):
            f = table[column * plan.tiles + t]
            pltpu.make_async_copy(
                payload.at[f], outs[e].at[pl.ds(t * plan.frag, plan.channels)], sem.at[e]
            ).start()
            return 0

        lax.fori_loop(0, plan.tiles, move, 0)


def add_edges(plan, columns, table, payload, opacity, outs):
    across = plan.across
    lane = iota((plan.channels, plan.rows, plan.lanes), 2)
    lane_one = iota((plan.rows, plan.lanes), 1)
    for out, column in zip(outs, columns):
        for t in range(plan.tiles):
            out[t * plan.frag + plan.channels] = opacity[table[column * plan.tiles + t]]
        right, left = neighbours(plan, column)
        spread = jnp.zeros((plan.channels, plan.rows, plan.lanes), jnp.float32)
        for j in range(TYD):
            f_r, f_l = table[right + j * across], table[left + j * across]
            inside = (lane >= 4 * j) & (lane < 4 * j + 4)
            spread = jnp.where(inside, joined(payload[f_r], payload[f_l], j, lane, 2), spread)
        for i in range(plan.halo_pad):
            group = jnp.zeros((plan.rows, plan.lanes), jnp.float32)
            for b in range(plan.blocks):
                c = i * plan.blocks + b
                if c < plan.channels:
                    moved = pltpu.roll(spread[c], SPAN * b, 1) if b else spread[c]
                    group = jnp.where(
                        (lane_one >= SPAN * b) & (lane_one < SPAN * b + SPAN), moved, group
                    )
            out[plan.at_halo + i] = group.astype(jnp.bfloat16)


def await_fragments(plan, outs, sem):
    for e, out in enumerate(outs):
        whole = out.at[pl.ds(0, plan.tiles * plan.channels)]
        pltpu.make_async_copy(whole, whole, sem.at[e]).wait()


def first_kernel(plan, footprints, depth_order, payload, opacity, *rest):
    n, tiles, half = plan.count, plan.tiles, plan.half
    outs = rest[:half]
    thin, table, held, cover, sem, sem_held, sem_cover = rest[half:]
    x, y = lax.axis_index("gx"), lax.axis_index("gy")
    me = x * n + y
    bring_cover = pltpu.make_async_copy(opacity, cover, sem_cover)
    bring_cover.start()
    bring = pltpu.make_async_copy(payload, held, sem_held)
    bring.start()

    def look(f, _):
        owner, slot = split(footprints[me, f], tiles)
        table[split(owner, n)[1] * tiles + slot] = f
        return 0

    lax.fori_loop(0, footprints.shape[1], look, 0, unroll=8)
    columns = [y ^ half ^ k for k in range(half)]
    send_fragments(plan, columns, table, payload, outs, sem)
    order = depth_order[...].astype(jnp.float32)
    order = jnp.concatenate(
        [order, jnp.zeros((tiles, plan.lanes - plan.depth), jnp.float32)], axis=1
    ).astype(jnp.bfloat16)
    bring_cover.wait()
    thin_part(plan, table, cover, order, thin)
    bring.wait()
    add_edges(plan, columns, table, held, cover, outs)
    await_fragments(plan, outs, sem)


def pack_kernel(plan, table, payload, opacity, out, sem):
    half = plan.half
    y = lax.axis_index("gy")
    base = y - (y & (half - 1))
    columns = [base + e for e in range(half)]
    outs = [out.at[e] for e in range(half)]
    send_fragments(plan, columns, table, payload, outs, sem)
    add_edges(plan, columns, table, payload, opacity, outs)
    await_fragments(plan, outs, sem)


def fold(x):
    return x.reshape(x.shape[0] * x.shape[1], x.shape[2])


def blend_kernel(plan, mirror, alpha_at, weight_at, own_in, prev_in, next_in, *rest):
    *inbox, out_own, out_next, alpha, weight, clear = rest
    n, tiles, across, sources = plan.count, plan.tiles, plan.across, plan.half
    rows, lanes = plan.rows, plan.lanes
    pair = 2 * rows
    frag_rows = plan.frag * rows
    halo_row = plan.at_halo * rows
    message = plan.groups * rows
    lane = iota((pair, lanes), 1)
    most = tiles - across

    def read(k, start, stop):
        ref, at = (inbox[k], 0) if mirror else (inbox[0], k * message)
        return ref[at + start : at + stop, :].astype(jnp.float32)

    for kind, ref in enumerate((own_in, prev_in, next_in)):
        for s in range(n):
            for t in range(tiles + 1):
                if kind and t < tiles and not across <= t < most:
                    continue
                row = (s * plan.thin_pair + mirror * plan.thin + t) * rows
                base = row // 16 * 16
                held = ref[base : base + 16, :].astype(jnp.float32)
                part = held[row - base : row - base + rows]
                alpha[(kind * n + s) * (tiles + 1) + t] = jnp.concatenate([part, part], axis=0)

    weight[...] = jnp.zeros_like(weight)

    def through(i, _):
        seen = jnp.ones((pair, lanes), jnp.float32)
        for d in range(plan.depth):
            weight[weight_at[i * plan.depth + d]] = seen
            seen = seen * (1.0 - alpha[alpha_at[i * plan.depth + d]])
        clear[i] = seen
        return 0

    lax.fori_loop(0, 4 * most, through, 0, unroll=4)

    step = 3 * pair
    while frag_rows % step or step % 16:
        step += pair
    shape = (step // pair, pair, lanes)
    def turned(x, by):
        return pltpu.roll(x, by % pair, 1)

    low_rows = iota(shape, 1) % rows < rows // 2
    for at in range(0, frag_rows, step):
        edges = {}
        for t in range(tiles):
            keeps, gives = t >= across, t < most
            total_own = jnp.zeros(shape, jnp.float32)
            total_next = jnp.zeros(shape, jnp.float32)
            for k in range(sources):
                start = t * frag_rows + at
                held = read(k, start, start + step).reshape(shape)
                if keeps:
                    total_own += weight[k * tiles + t][None] * held
                if gives:
                    total_next += weight[(2 * sources + k) * tiles + t][None] * held
            if at + step == frag_rows:
                mask = (iota(shape, 0) == step // pair - 1) & (iota(shape, 1) >= rows)
                cover = jnp.zeros((pair, lanes), jnp.float32)
                if keeps and not mirror:
                    cover = 1.0 - clear[t - across]
                total_own = jnp.where(mask, cover[None], total_own)
                cover = jnp.zeros((pair, lanes), jnp.float32)
                if t < across and not mirror:
                    cover = 1.0 - clear[most + t]
                total_next = jnp.where(mask, cover[None], total_next)

            def put(ref, slot, total):
                start = slot * frag_rows + at
                ref[start : start + step, :] = total.reshape(step, lanes).astype(ref.dtype)

            if gives:
                put(out_next, t, total_next)
            if keeps:
                put(out_own, t - across + mirror, total_own)
            if t < across:
                edges[t] = total_next
            if t >= most:
                edges[t] = total_own
        first, last = edges[most], edges[tiles - 1]
        put(out_next, most, jnp.where(low_rows, turned(first, -(rows // 2)), last))
        if mirror:
            first, last = edges[0], edges[across - 1]
            put(out_own, 0, jnp.where(low_rows, first, turned(last, rows // 2)))

    halo_shape = (plan.halo_pad * rows // pair, pair, lanes)

    def merged(kind, source):
        out = jnp.zeros((pair, lanes), jnp.float32)
        first = across if kind == 0 else 0
        for u in range(most):
            out = jnp.where(lane // 2 == first + u, source(u, first + u), out)
        return out

    def widened(x):
        out = jnp.zeros((pair, lanes), jnp.float32)
        for b in range(plan.blocks):
            moved = pltpu.roll(x, SPAN * b, 1) if b else x
            out = jnp.where(lane // SPAN == b, moved, out)
        return out

    totals = [jnp.zeros(halo_shape, jnp.float32) for _ in range(2)]
    for k in range(sources):
        held = read(k, halo_row, halo_row + plan.halo_pad * rows).reshape(halo_shape)
        for kind in range(2):
            base = (2 * kind + 1) * sources * tiles + k * tiles
            by = widened(merged(kind, lambda u, v: weight[base + v]))
            totals[kind] += by[None] * held
    if not mirror:
        i_cov, b_cov = plan.channels // plan.blocks, plan.channels % plan.blocks
        group = iota(halo_shape, 0) * 2 + iota(halo_shape, 1) // rows
        at_cov = (group == i_cov) & (iota(halo_shape, 2) // SPAN == b_cov)
        for kind in range(2):
            cov = merged(kind, lambda u, v: 1.0 - clear[(2 + kind) * most + u])
            if kind == 1:
                cov = jnp.where(lane // 4 == 0, cov, 0.0)
            cov = pltpu.roll(cov, SPAN * b_cov, 1) if b_cov else cov
            totals[kind] = jnp.where(at_cov, cov[None], totals[kind])
    band = iota(halo_shape, 2) // 4 % TYD
    length = plan.halo_pad * rows
    start = (most + 1) * frag_rows
    both = jnp.where(band == TYD - 1, totals[0], totals[1])
    out_next[start : start + length, :] = both.reshape(length, lanes).astype(jnp.bfloat16)
    if mirror:
        both = jnp.where(band == 0, totals[1], totals[0])
        out_own[start : start + length, :] = both.reshape(length, lanes).astype(jnp.bfloat16)
    else:
        start = most * frag_rows
        out_own[start : start + length, :] = totals[0].reshape(length, lanes)


def conv_kernel(
    plan, feats, spots, panel, own, kept, got, over, cross, one, top, low, two, keep, b1, b2, *rest
):
    out, field, hidden = rest
    tiles, across, rows, lanes = plan.tiles, plan.across, plan.rows, plan.lanes
    frag_rows = plan.frag * rows
    most = tiles - across
    span = across * lanes
    wide = span + lanes
    has_top, has_low = spots[0], spots[1]
    has_left, has_right = spots[2], spots[3]

    def tile(ref, t, turn=0):
        part = ref[t * frag_rows : (t + 1) * frag_rows, :].astype(jnp.float32)
        if turn:
            part = part.reshape(-1, 2 * rows, lanes)
            part = pltpu.roll(part, turn % (2 * rows), 1).reshape(frag_rows, lanes)
        return part

    for c in range(across):
        at = slice(c * lanes, (c + 1) * lanes)
        last = c == across - 1
        turn = 0 if last else rows // 2
        value = tile(got, most, turn) + tile(cross, most, turn)
        value = jnp.where(has_top != 0, value, 0.0)
        field[0:frag_rows, at] = value.astype(jnp.bfloat16)
        for j in range(TYD):
            t = j * across + c
            value = 0.0
            if j < TYD - 1:
                value = tile(got, t) + tile(cross, t)
            if j > 0:
                value = value + tile(own, t - across) + tile(over, t - across + 1)
            field[(j + 1) * frag_rows : (j + 2) * frag_rows, at] = value.astype(jnp.bfloat16)
        at_low = (TYD + 1) * frag_rows
        value = tile(kept, c) + tile(over, 0, -(rows // 2) if last else 0)
        value = jnp.where(has_low != 0, value, 0.0)
        field[at_low : at_low + frag_rows, at] = value.astype(jnp.bfloat16)

    length = plan.halo_pad * rows

    def edge(ref):
        at = ref.shape[0] - length
        return ref[at : at + length, :].astype(jnp.float32)

    h_own = own[most * frag_rows : most * frag_rows + length, :]
    h_over = edge(over)
    h_got = edge(got) + edge(cross)
    h_kept = edge(kept) + h_over
    band = iota((length, lanes), 1) // 4 % TYD
    h_here = h_own + h_over
    h_all = jnp.where(band == TYD - 1, h_here, jnp.where(band == 0, h_got, h_here + h_got))
    lane = iota((rows, lanes), 1)
    valid = ((lane < 2) & (has_right != 0)) | ((lane >= lanes - 2) & (has_left != 0))

    def unpacked(source, j):
        pieces = []
        for c in range(plan.frag):
            i, b = c // plan.blocks, c % plan.blocks
            piece = source[i * rows : (i + 1) * rows]
            shift = (-(SPAN * b + 4 * j + 2)) % lanes
            pieces.append(jnp.where(valid, pltpu.roll(piece, shift, 1), 0.0))
        return jnp.concatenate(pieces, axis=0).astype(jnp.bfloat16)

    wide_zero = jnp.zeros((frag_rows, lanes), jnp.bfloat16)
    at = slice(span, wide)
    field[0:frag_rows, at] = jnp.where(has_top != 0, unpacked(h_got, TYD - 1), wide_zero)
    for j in range(TYD):
        field[(j + 1) * frag_rows : (j + 2) * frag_rows, at] = unpacked(h_all, j)
    at_low = (TYD + 1) * frag_rows
    field[at_low : at_low + frag_rows, at] = jnp.where(has_low != 0, unpacked(h_kept, 0), wide_zero)

    def shifted_sum(y):
        part = y.shape[0] // 3
        return (
            pltpu.roll(y[:part], 1, 1)
            + y[part : 2 * part]
            + pltpu.roll(y[2 * part :], wide - 1, 1)
        )

    def act(y, bias):
        x = shifted_sum(y) + bias
        return x * (1.0 / (1.0 + jnp.exp(-x)))

    half = 2 * rows
    groups = TYD // 2
    col = iota((1, wide), 1)
    inside = ((col != span) | (has_right != 0)) & ((col != wide - 1) | (has_left != 0))
    for g in range(groups):
        window = field[2 * g * frag_rows : (2 * g + 4) * frag_rows, :]
        y = jnp.dot(one[...], window, preferred_element_type=jnp.float32)
        h = jnp.where(inside, act(y, b1[...]), 0.0)
        at = feats + g * half * feats
        hidden[at : at + half * feats, :] = h.astype(jnp.bfloat16)
    for ref, at_field, at_hidden, has in (
        (top, 0, 0, has_top),
        (low, TYD * frag_rows, feats * (1 + groups * half), has_low),
    ):
        window = field[at_field : at_field + 2 * frag_rows, :]
        y = jnp.dot(ref[...], window, preferred_element_type=jnp.float32)
        h = jnp.where(inside & (has != 0), act(y, b1[0:feats]), 0.0)
        hidden[at_hidden : at_hidden + feats, :] = h.astype(jnp.bfloat16)
    strip = out.shape[1]
    for g in range(groups):
        at = g * half * feats
        window = hidden[at : at + (half + 2) * feats, :]
        y = jnp.dot(two[...], window, preferred_element_type=jnp.float32)
        plain = field[(2 * g + 1) * frag_rows : (2 * g + 3) * frag_rows, 0:span]
        base = jnp.dot(keep[...], plain, preferred_element_type=jnp.float32)
        total = (shifted_sum(y)[:, 0:span] + b2[...] + base).astype(jnp.bfloat16)
        for s in range(half * feats // strip):
            out[panel[g * (half * feats // strip) + s]] = total[s * strip : (s + 1) * strip]


def spread_kernel(plan, feats, outs, w1, w2, one, top, low, two, keep):
    rows, frag = plan.rows, plan.frag
    block = frag * rows
    part = 3 * feats

    def place(shape):
        channel = iota(shape, 0)
        column = iota(shape, 1)
        inner = column % block
        pixel = column // block * rows + inner % rows
        return jnp.where(inner // rows == channel, pixel, -1)

    def taps(weight, i):
        return weight[i * part : (i + 1) * part, :]

    def sums(weight, hit, first):
        total = 0.0
        for i in range(3):
            mask = (hit == first + i).astype(jnp.float32).astype(jnp.bfloat16)
            total = total + jnp.dot(taps(weight, i), mask, preferred_element_type=jnp.float32)
        return total.astype(jnp.bfloat16)

    hit = place((frag, one.shape[1]))
    for q in range(outs):
        rows_q = sums(w1, hit, q + rows - 1)
        for s in range(3):
            at = (s * outs + q) * feats
            one[at : at + feats, :] = rows_q[s * feats : (s + 1) * feats]
        if q == 0:
            low[...] = rows_q[:, : low.shape[1]]
    top[...] = sums(w1, place((frag, top.shape[1])), rows - 2)
    shape = (feats, two.shape[1])
    hit = jnp.where(iota(shape, 1) % feats == iota(shape, 0), iota(shape, 1) // feats, -1)
    for q in range(outs):
        rows_q = sums(w2, hit, q)
        for s in range(3):
            at = (s * outs + q) * feats
            two[at : at + feats, :] = rows_q[s * feats : (s + 1) * feats]
    shape = keep.shape
    inner = iota(shape, 1) % block
    pixel = iota(shape, 1) // block * rows + inner % rows
    same = (iota(shape, 0) // feats == pixel) & (iota(shape, 0) % feats == inner // rows)
    keep[...] = same.astype(jnp.float32).astype(jnp.bfloat16)


def shards(
    payload,
    opacity,
    depth_order,
    footprints,
    panel_map,
    conv1_weight,
    conv1_bias,
    conv2_weight,
    conv2_bias,
):
    row_groups = lax.axis_size("gx")
    n = lax.axis_size("gy")
    x = lax.axis_index("gx")
    y = lax.axis_index("gy")
    _, rows, channels, lanes = payload.shape
    tiles, depth = depth_order.shape
    plan = Plan(n, tiles, rows, channels, lanes, depth)
    feats = conv2_weight.shape[1]
    across = plan.across
    most = tiles - across

    half = n // 2
    spec_s = pl.BlockSpec(memory_space=pltpu.SMEM)
    spec_v = pl.BlockSpec(memory_space=pltpu.VMEM)
    spec_h = pl.BlockSpec(memory_space=pltpu.HBM)
    limit = pltpu.CompilerParams(vmem_limit_bytes=40 << 20)
    pixels = payload.transpose(0, 2, 1, 3)

    def cost(micros):
        return pl.CostEstimate(flops=0, bytes_accessed=int(micros * 3.6e6), transcendentals=0)

    message = jax.ShapeDtypeStruct((plan.groups, rows, lanes), payload.dtype)
    *packed, thin, table = pl.pallas_call(
        functools.partial(first_kernel, plan),
        out_shape=[message] * half
        + [
            jax.ShapeDtypeStruct((n, plan.thin_pair, rows, lanes), payload.dtype),
            jax.ShapeDtypeStruct((n * tiles,), jnp.int32),
        ],
        in_specs=[spec_s, spec_v, spec_h, spec_h],
        out_specs=[spec_v] * (half + 1) + [spec_s],
        scratch_shapes=[
            pltpu.VMEM(pixels.shape, payload.dtype),
            pltpu.VMEM(opacity.shape, payload.dtype),
            pltpu.SemaphoreType.DMA((half,)),
            pltpu.SemaphoreType.DMA,
            pltpu.SemaphoreType.DMA,
        ],
        compiler_params=pltpu.CompilerParams(vmem_limit_bytes=60 << 20),
        cost_estimate=cost(5),
        name="first",
    )(footprints, depth_order, pixels, opacity)
    inbox_mirror = [packed[0]] + [paired(packed[k], "gy", k) for k in range(1, half)]
    inbox_mirror = [block.reshape(-1, lanes) for block in inbox_mirror]

    thin = lax.all_to_all(thin, "gy", split_axis=0, concat_axis=0, tiled=True)
    thins = [thin, rotated(thin, "gx", 1), rotated(thin, "gx", -1)]

    near = [list(range(i, i + half)) for i in range(0, n, half)]
    inbox_own = pl.pallas_call(
        functools.partial(pack_kernel, plan),
        out_shape=jax.ShapeDtypeStruct((half, plan.groups, rows, lanes), payload.dtype),
        in_specs=[spec_s] + [spec_v] * 2,
        out_specs=spec_v,
        scratch_shapes=[pltpu.SemaphoreType.DMA((half,))],
        compiler_params=limit,
        cost_estimate=cost(4),
        name="pack",
    )(table, pixels, opacity)
    inbox_own = lax.all_to_all(
        inbox_own, "gy", split_axis=0, concat_axis=0, axis_index_groups=near, tiled=True
    )
    inbox_own = [inbox_own.reshape(-1, lanes)]

    def order_of(block):
        block = block[:, tiles + 1 : 2 * plan.thin : plan.thin]
        return block.astype(jnp.int32).reshape(n, 2 * rows, lanes)[:, :tiles, :depth]

    orders = [order_of(thins[0]), order_of(thins[2])]
    thins = [block.reshape(-1, lanes) for block in thins]

    def tables(order, kind, halo, mirror):
        slots = jnp.arange(order.shape[0], dtype=jnp.int32)[:, None] + (across if kind == 0 else 0)
        column = order % n
        local = order // n == x
        source = jnp.where(local, 0, 1 + kind) * n + column
        source = source * (tiles + 1) + (tiles if halo else slots)
        mine = local & (column // half == y // half)
        sender = (column ^ y) % half if mirror else column % half
        target = ((2 * kind + halo) * half + sender) * tiles + slots
        return source, jnp.where(mine, target, 4 * half * tiles)

    frag_rows = plan.frag * rows
    tail = plan.halo_pad * rows

    def blend(mirror, inbox):
        column = y ^ half if mirror else y

        def beside_of(order, step):
            return lax.dynamic_index_in_dim(order, (column + n + step) % n, 0, keepdims=False)

        here = [beside_of(order, 0) for order in orders]
        beside = [
            jnp.stack(
                [beside_of(order, -1)[across - 1 :: across], beside_of(order, 1)[0::across]], axis=1
            ).reshape(2 * TYD, depth)
            for order in orders
        ]
        pieces = [
            tables(here[0][across:], 0, 0, mirror),
            tables(here[1][:most], 1, 0, mirror),
            tables(beside[0][across:], 0, 1, mirror),
            tables(beside[1][:most], 1, 1, mirror),
        ]
        alpha_at = jnp.concatenate([a for a, _ in pieces]).reshape(-1)
        weight_at = jnp.concatenate([w for _, w in pieces]).reshape(-1)
        sums = jax.ShapeDtypeStruct(((most + 1) * frag_rows + tail, lanes), payload.dtype)
        local = jax.ShapeDtypeStruct((most * frag_rows + tail, lanes), jnp.float32)
        return pl.pallas_call(
            functools.partial(blend_kernel, plan, mirror),
            out_shape=[sums if mirror else local, sums],
            in_specs=[spec_s] * 2 + [spec_v] * (3 + len(inbox)),
            out_specs=[spec_v] * 2,
            scratch_shapes=[
                pltpu.VMEM((3 * n * (tiles + 1), 2 * rows, lanes), jnp.float32),
                pltpu.VMEM((4 * half * tiles + 1, 2 * rows, lanes), jnp.float32),
                pltpu.VMEM((4 * most, 2 * rows, lanes), jnp.float32),
            ],
            compiler_params=limit,
            cost_estimate=cost(3),
            name="blend_mirror" if mirror else "blend_own",
        )(alpha_at, weight_at, *thins, *inbox)

    over, cross = blend(1, inbox_mirror)
    over, thins[0] = lax.optimization_barrier((over, thins[0]))
    over = paired(over, "gy", half)
    route = [
        (i * n + j, (i + 1) % row_groups * n + (j ^ half))
        for i in range(row_groups)
        for j in range(n)
    ]
    cross = lax.ppermute(cross, ("gx", "gy"), route)
    own, kept = blend(0, inbox_own)
    got = rotated(kept, "gx", 1)

    band_half = 2 * rows
    w1, w2, _ = lax.optimization_barrier((conv1_weight, conv2_weight, table))
    w1 = w1.reshape(-1, w1.shape[2])
    w2 = w2.reshape(-1, w2.shape[2])

    def matrix(height, width):
        return jax.ShapeDtypeStruct((height, width), payload.dtype)

    one, top, low, two, keep = pl.pallas_call(
        functools.partial(spread_kernel, plan, feats, band_half),
        out_shape=[
            matrix(3 * band_half * feats, 4 * frag_rows),
            matrix(3 * feats, 2 * frag_rows),
            matrix(3 * feats, 2 * frag_rows),
            matrix(3 * band_half * feats, (band_half + 2) * feats),
            matrix(band_half * feats, 2 * frag_rows),
        ],
        in_specs=[spec_v] * 2,
        out_specs=[spec_v] * 5,
        compiler_params=limit,
        cost_estimate=cost(4),
        name="spread",
    )(w1, w2)
    b1 = jnp.tile(conv1_bias, band_half)[:, None]
    b2 = jnp.tile(conv2_bias, band_half)[:, None]
    spots = jnp.stack([x > 0, x < row_groups - 1, y > 0, y < n - 1]).astype(jnp.int32)
    band = TYD * rows
    strip = band // n
    span = across * lanes
    pieces = pl.pallas_call(
        functools.partial(conv_kernel, plan, feats),
        out_shape=jax.ShapeDtypeStruct((n, strip * feats, span), jnp.bfloat16),
        in_specs=[spec_s] * 2 + [spec_v] * 12,
        out_specs=spec_v,
        scratch_shapes=[
            pltpu.VMEM(((TYD + 2) * frag_rows, span + lanes), jnp.bfloat16),
            pltpu.VMEM(((band + 2) * feats, span + lanes), jnp.bfloat16),
        ],
        compiler_params=limit,
        cost_estimate=cost(4),
        name="conv",
    )(spots, panel_map, own, kept, got, over, cross, one, top, low, two, keep, b1, b2)
    shown = lax.all_to_all(pieces, "gy", split_axis=0, concat_axis=0, tiled=True)
    shown = shown.transpose(1, 0, 2).reshape(1, 1, strip, feats, n * span)
    return shown


def solution(mesh):
    return jax.shard_map(
        shards,
        mesh=mesh,
        in_specs=(
            P(("gx", "gy"), None, None, None),
            P(("gx", "gy"), None, None),
            P(("gx", "gy"), None),
            P(),
            P(),
            P(),
            P(),
            P(),
            P(),
        ),
        out_specs=P("gx", "gy", None, None, None),
        check_vma=False,
    )
```

```python
import functools

import jax
import jax.numpy as jnp
from jax import lax
from jax.experimental import pallas as pl
from jax.experimental.pallas import tpu as pltpu
from jax.sharding import PartitionSpec as P

TYD = 4
SPAN = 4 * TYD


def rotated(block, axis, distance):
    count = lax.axis_size(axis)
    return lax.ppermute(block, axis, [(i, (i + distance) % count) for i in range(count)])


def paired(block, axis, step):
    return lax.ppermute(block, axis, [(i, i ^ step) for i in range(lax.axis_size(axis))])


def split(value, size):
    if size & (size - 1) == 0:
        return value >> (size.bit_length() - 1), value & (size - 1)
    return lax.div(value, size), lax.rem(value, size)


def iota(shape, dim):
    return lax.broadcasted_iota(jnp.int32, shape, dim)


class Plan:
    def __init__(self, count, tiles, rows, channels, lanes, depth):
        self.count = count
        self.half = count // 2
        self.tiles = tiles
        self.across = tiles // TYD
        self.rows = rows
        self.channels = channels
        self.lanes = lanes
        self.depth = depth
        self.frag = channels + 1
        self.blocks = lanes // SPAN
        self.halo = -(-self.frag // self.blocks)
        self.at_halo = tiles * self.frag
        per = 16 // rows
        self.groups = -(-(self.at_halo + self.halo) // per) * per
        self.halo_pad = self.groups - self.at_halo
        self.thin = -(-(tiles + 2) // 2) * 2
        self.thin_pair = -(-2 * self.thin // per) * per


def neighbours(plan, column):
    n, tiles = plan.count, plan.tiles
    right = jnp.where(column == n - 1, 0, column + 1) * tiles
    left = jnp.where(column == 0, n - 1, column - 1) * tiles + plan.across - 1
    return right, left


def joined(right, left, j, lane, axis):
    both = jnp.where(lane < 2, right.astype(jnp.float32), left.astype(jnp.float32))
    return pltpu.roll(both, 4 * j + 2, axis)


def thin_part(plan, table, opacity, order, out):
    n, tiles = plan.count, plan.tiles
    lane = iota((plan.rows, plan.lanes), 1)
    empty = jnp.zeros((plan.rows, plan.lanes), jnp.bfloat16)
    for d in range(n):
        places = [(d, 0), (d ^ plan.half, plan.thin)]
        for t in range(tiles):
            group = opacity[table[d * tiles + t]]
            for to, at in places:
                out[to, at + t] = group
        right = (d + 1) % n * tiles
        left = (d - 1) % n * tiles + plan.across - 1
        halo = jnp.zeros((plan.rows, plan.lanes), jnp.float32)
        for j in range(TYD):
            f_r, f_l = table[right + j * plan.across], table[left + j * plan.across]
            inside = (lane >= 4 * j) & (lane < 4 * j + 4)
            halo = jnp.where(inside, joined(opacity[f_r], opacity[f_l], j, lane, 1), halo)
        for to, at in places:
            out[to, at + tiles] = halo.astype(jnp.bfloat16)
        for i in range(2):
            out[d, i * plan.thin + tiles + 1] = order[i * plan.rows : (i + 1) * plan.rows]
            for g in range(tiles + 2, plan.thin):
                out[d, i * plan.thin + g] = empty
        for g in range(2 * plan.thin, plan.thin_pair):
            out[d, g] = empty


def send_fragments(plan, columns, table, payload, outs, sem):
    for e, column in enumerate(columns):

        def move(t, _, e=e, column=column):
            f = table[column * plan.tiles + t]
            pltpu.make_async_copy(
                payload.at[f], outs[e].at[pl.ds(t * plan.frag, plan.channels)], sem.at[e]
            ).start()
            return 0

        lax.fori_loop(0, plan.tiles, move, 0)


def add_edges(plan, columns, table, payload, opacity, outs):
    across = plan.across
    lane = iota((plan.channels, plan.rows, plan.lanes), 2)
    lane_one = iota((plan.rows, plan.lanes), 1)
    for out, column in zip(outs, columns):
        for t in range(plan.tiles):
            out[t * plan.frag + plan.channels] = opacity[table[column * plan.tiles + t]]
        right, left = neighbours(plan, column)
        spread = jnp.zeros((plan.channels, plan.rows, plan.lanes), jnp.float32)
        for j in range(TYD):
            f_r, f_l = table[right + j * across], table[left + j * across]
            inside = (lane >= 4 * j) & (lane < 4 * j + 4)
            spread = jnp.where(inside, joined(payload[f_r], payload[f_l], j, lane, 2), spread)
        for i in range(plan.halo_pad):
            group = jnp.zeros((plan.rows, plan.lanes), jnp.float32)
            for b in range(plan.blocks):
                c = i * plan.blocks + b
                if c < plan.channels:
                    moved = pltpu.roll(spread[c], SPAN * b, 1) if b else spread[c]
                    group = jnp.where(
                        (lane_one >= SPAN * b) & (lane_one < SPAN * b + SPAN), moved, group
                    )
            out[plan.at_halo + i] = group.astype(jnp.bfloat16)


def await_fragments(plan, outs, sem):
    for e, out in enumerate(outs):
        whole = out.at[pl.ds(0, plan.tiles * plan.channels)]
        pltpu.make_async_copy(whole, whole, sem.at[e]).wait()


def first_kernel(plan, footprints, depth_order, payload, opacity, *rest):
    n, tiles, half = plan.count, plan.tiles, plan.half
    outs = rest[:half]
    thin, table, held, cover, sem, sem_held, sem_cover = rest[half:]
    x, y = lax.axis_index("gx"), lax.axis_index("gy")
    me = x * n + y
    bring_cover = pltpu.make_async_copy(opacity, cover, sem_cover)
    bring_cover.start()
    bring = pltpu.make_async_copy(payload, held, sem_held)
    bring.start()

    def look(f, _):
        owner, slot = split(footprints[me, f], tiles)
        table[split(owner, n)[1] * tiles + slot] = f
        return 0

    lax.fori_loop(0, footprints.shape[1], look, 0, unroll=8)
    columns = [y ^ half ^ k for k in range(half)]
    send_fragments(plan, columns, table, payload, outs, sem)
    order = depth_order[...].astype(jnp.float32)
    order = jnp.concatenate(
        [order, jnp.zeros((tiles, plan.lanes - plan.depth), jnp.float32)], axis=1
    ).astype(jnp.bfloat16)
    bring_cover.wait()
    thin_part(plan, table, cover, order, thin)
    bring.wait()
    add_edges(plan, columns, table, held, cover, outs)
    await_fragments(plan, outs, sem)


def pack_kernel(plan, table, payload, opacity, out, sem):
    half = plan.half
    y = lax.axis_index("gy")
    base = y - (y & (half - 1))
    columns = [base + e for e in range(half)]
    outs = [out.at[e] for e in range(half)]
    send_fragments(plan, columns, table, payload, outs, sem)
    add_edges(plan, columns, table, payload, opacity, outs)
    await_fragments(plan, outs, sem)


def fold(x):
    return x.reshape(x.shape[0] * x.shape[1], x.shape[2])


def blend_kernel(plan, mirror, alpha_at, weight_at, own_in, prev_in, next_in, *rest):
    if mirror:
        *inbox, out_own, out_next, edge_over, edge_cross, alpha, weight, clear = rest
    else:
        *inbox, out_own, out_next, alpha, weight, clear = rest
    n, tiles, across, sources = plan.count, plan.tiles, plan.across, plan.half
    rows, lanes = plan.rows, plan.lanes
    pair = 2 * rows
    frag_rows = plan.frag * rows
    halo_row = plan.at_halo * rows
    message = plan.groups * rows
    lane = iota((pair, lanes), 1)
    most = tiles - across

    def read(k, start, stop):
        ref, at = (inbox[k], 0) if mirror else (inbox[0], k * message)
        return ref[at + start : at + stop, :].astype(jnp.float32)

    for kind, ref in enumerate((own_in, prev_in, next_in)):
        for s in range(n):
            for t in range(tiles + 1):
                if kind and t < tiles and not across <= t < most:
                    continue
                row = (s * plan.thin_pair + mirror * plan.thin + t) * rows
                base = row // 16 * 16
                held = ref[base : base + 16, :].astype(jnp.float32)
                part = held[row - base : row - base + rows]
                alpha[(kind * n + s) * (tiles + 1) + t] = jnp.concatenate([part, part], axis=0)

    weight[...] = jnp.zeros_like(weight)

    def through(i, _):
        seen = jnp.ones((pair, lanes), jnp.float32)
        for d in range(plan.depth):
            weight[weight_at[i * plan.depth + d]] = seen
            seen = seen * (1.0 - alpha[alpha_at[i * plan.depth + d]])
        clear[i] = seen
        return 0

    lax.fori_loop(0, 4 * most, through, 0, unroll=4)

    step = 3 * pair
    while frag_rows % step or step % 16:
        step += pair
    shape = (step // pair, pair, lanes)
    def turned(x, by):
        return pltpu.roll(x, by % pair, 1)

    low_rows = iota(shape, 1) % rows < rows // 2
    for at in range(0, frag_rows, step):
        edges = {}
        for t in range(tiles):
            keeps, gives = t >= across, t < most
            total_own = jnp.zeros(shape, jnp.float32)
            total_next = jnp.zeros(shape, jnp.float32)
            for k in range(sources):
                start = t * frag_rows + at
                held = read(k, start, start + step).reshape(shape)
                if keeps:
                    total_own += weight[k * tiles + t][None] * held
                if gives:
                    total_next += weight[(2 * sources + k) * tiles + t][None] * held
            if at + step == frag_rows:
                mask = (iota(shape, 0) == step // pair - 1) & (iota(shape, 1) >= rows)
                cover = jnp.zeros((pair, lanes), jnp.float32)
                if keeps and not mirror:
                    cover = 1.0 - clear[t - across]
                total_own = jnp.where(mask, cover[None], total_own)
                cover = jnp.zeros((pair, lanes), jnp.float32)
                if t < across and not mirror:
                    cover = 1.0 - clear[most + t]
                total_next = jnp.where(mask, cover[None], total_next)

            def put(ref, slot, total):
                start = slot * frag_rows + at
                ref[start : start + step, :] = total.reshape(step, lanes).astype(ref.dtype)

            if t < across:
                edges[t] = total_next
            if t >= most:
                edges[t] = total_own
            if not mirror:
                if gives:
                    put(out_next, t, total_next)
                if keeps:
                    put(out_own, t - across, total_own)
            elif gives and keeps:
                put(out_next, t - across, total_next)
                put(out_own, t - across, total_own)
        first, last = edges[most], edges[tiles - 1]
        top = jnp.where(low_rows, turned(first, -(rows // 2)), last)
        if mirror:
            for c in range(across):
                put(edge_cross, c, edges[c])
                put(edge_over, 1 + c, edges[most + c])
            put(edge_cross, across, top)
            first, last = edges[0], edges[across - 1]
            put(edge_over, 0, jnp.where(low_rows, first, turned(last, rows // 2)))
        else:
            put(out_next, most, top)

    halo_shape = (plan.halo_pad * rows // pair, pair, lanes)

    def merged(kind, source):
        out = jnp.zeros((pair, lanes), jnp.float32)
        first = across if kind == 0 else 0
        for u in range(most):
            out = jnp.where(lane // 2 == first + u, source(u, first + u), out)
        return out

    def widened(x):
        out = jnp.zeros((pair, lanes), jnp.float32)
        for b in range(plan.blocks):
            moved = pltpu.roll(x, SPAN * b, 1) if b else x
            out = jnp.where(lane // SPAN == b, moved, out)
        return out

    totals = [jnp.zeros(halo_shape, jnp.float32) for _ in range(2)]
    for k in range(sources):
        held = read(k, halo_row, halo_row + plan.halo_pad * rows).reshape(halo_shape)
        for kind in range(2):
            base = (2 * kind + 1) * sources * tiles + k * tiles
            by = widened(merged(kind, lambda u, v: weight[base + v]))
            totals[kind] += by[None] * held
    if not mirror:
        i_cov, b_cov = plan.channels // plan.blocks, plan.channels % plan.blocks
        group = iota(halo_shape, 0) * 2 + iota(halo_shape, 1) // rows
        at_cov = (group == i_cov) & (iota(halo_shape, 2) // SPAN == b_cov)
        for kind in range(2):
            cov = merged(kind, lambda u, v: 1.0 - clear[(2 + kind) * most + u])
            if kind == 1:
                cov = jnp.where(lane // 4 == 0, cov, 0.0)
            cov = pltpu.roll(cov, SPAN * b_cov, 1) if b_cov else cov
            totals[kind] = jnp.where(at_cov, cov[None], totals[kind])
    length = plan.halo_pad * rows

    def put_halo(ref, total):
        start = ref.shape[0] - length
        ref[start : start + length, :] = total.reshape(length, lanes).astype(ref.dtype)

    put_halo(out_own, totals[0])
    if mirror:
        put_halo(out_next, totals[1])
        put_halo(edge_over, totals[1])
        put_halo(edge_cross, totals[0])
    else:
        band = iota(halo_shape, 2) // 4 % TYD
        put_halo(out_next, jnp.where(band == TYD - 1, totals[0], totals[1]))


def conv_kernel(
    plan,
    feats,
    spots,
    panel,
    own,
    kept,
    inner,
    edge_over,
    edge_cross,
    *rest,
):
    *got, one, top, low, two, keep, b1, b2, out, field, hidden = rest
    tiles, across, rows, lanes = plan.tiles, plan.across, plan.rows, plan.lanes
    frag_rows = plan.frag * rows
    most = tiles - across
    span = across * lanes
    wide = span + lanes
    has_top, has_low = spots[0], spots[1]
    has_left, has_right = spots[2], spots[3]

    def tile(ref, t, turn=0):
        part = ref[t * frag_rows : (t + 1) * frag_rows, :].astype(jnp.float32)
        if turn:
            part = part.reshape(-1, 2 * rows, lanes)
            part = pltpu.roll(part, turn % (2 * rows), 1).reshape(frag_rows, lanes)
        return part

    def shifted(t, turn=0):
        for ref in got:
            slots = ref.shape[0] // frag_rows
            if t < slots:
                return tile(ref, t, turn)
            t -= slots

    for c in range(across):
        at = slice(c * lanes, (c + 1) * lanes)
        last = c == across - 1
        turn = 0 if last else rows // 2
        value = shifted(most, turn) + tile(edge_cross, across, turn)
        value = jnp.where(has_top != 0, value, 0.0)
        field[0:frag_rows, at] = value.astype(jnp.bfloat16)
        for j in range(TYD):
            t = j * across + c
            if j == 0:
                value = shifted(t) + tile(edge_cross, c)
            elif j < TYD - 1:
                value = shifted(t) + tile(own, t - across) + tile(inner, t - across)
            else:
                value = tile(own, t - across) + tile(edge_over, 1 + c)
            field[(j + 1) * frag_rows : (j + 2) * frag_rows, at] = value.astype(jnp.bfloat16)
        at_low = (TYD + 1) * frag_rows
        value = tile(kept, c) + tile(edge_over, 0, -(rows // 2) if last else 0)
        value = jnp.where(has_low != 0, value, 0.0)
        field[at_low : at_low + frag_rows, at] = value.astype(jnp.bfloat16)

    length = plan.halo_pad * rows

    def edge(ref):
        at = ref.shape[0] - length
        return ref[at : at + length, :].astype(jnp.float32)

    h_got = edge(got[-1])
    band = iota((length, lanes), 1) // 4 % TYD
    h_all = edge(own) + edge(inner) + jnp.where(band == TYD - 1, 0.0, h_got)
    h_kept = edge(kept) + edge(edge_over)
    h_got = h_got + edge(edge_cross)
    lane = iota((rows, lanes), 1)
    valid = ((lane < 2) & (has_right != 0)) | ((lane >= lanes - 2) & (has_left != 0))

    def unpacked(source, j):
        pieces = []
        for c in range(plan.frag):
            i, b = c // plan.blocks, c % plan.blocks
            piece = source[i * rows : (i + 1) * rows]
            shift = (-(SPAN * b + 4 * j + 2)) % lanes
            pieces.append(jnp.where(valid, pltpu.roll(piece, shift, 1), 0.0))
        return jnp.concatenate(pieces, axis=0).astype(jnp.bfloat16)

    wide_zero = jnp.zeros((frag_rows, lanes), jnp.bfloat16)
    at = slice(span, wide)
    field[0:frag_rows, at] = jnp.where(has_top != 0, unpacked(h_got, TYD - 1), wide_zero)
    for j in range(TYD):
        field[(j + 1) * frag_rows : (j + 2) * frag_rows, at] = unpacked(h_all, j)
    at_low = (TYD + 1) * frag_rows
    field[at_low : at_low + frag_rows, at] = jnp.where(has_low != 0, unpacked(h_kept, 0), wide_zero)

    def shifted_sum(y):
        part = y.shape[0] // 3
        return (
            pltpu.roll(y[:part], 1, 1)
            + y[part : 2 * part]
            + pltpu.roll(y[2 * part :], wide - 1, 1)
        )

    def act(y, bias):
        x = shifted_sum(y) + bias
        return x * (1.0 / (1.0 + jnp.exp(-x)))

    half = 2 * rows
    groups = TYD // 2
    col = iota((1, wide), 1)
    inside = ((col != span) | (has_right != 0)) & ((col != wide - 1) | (has_left != 0))
    for g in range(groups):
        window = field[2 * g * frag_rows : (2 * g + 4) * frag_rows, :]
        y = jnp.dot(one[...], window, preferred_element_type=jnp.float32)
        h = jnp.where(inside, act(y, b1[...]), 0.0)
        at = feats + g * half * feats
        hidden[at : at + half * feats, :] = h.astype(jnp.bfloat16)
    for ref, at_field, at_hidden, has in (
        (top, 0, 0, has_top),
        (low, TYD * frag_rows, feats * (1 + groups * half), has_low),
    ):
        window = field[at_field : at_field + 2 * frag_rows, :]
        y = jnp.dot(ref[...], window, preferred_element_type=jnp.float32)
        h = jnp.where(inside & (has != 0), act(y, b1[0:feats]), 0.0)
        hidden[at_hidden : at_hidden + feats, :] = h.astype(jnp.bfloat16)
    strip = out.shape[1]
    for g in range(groups):
        at = g * half * feats
        window = hidden[at : at + (half + 2) * feats, :]
        y = jnp.dot(two[...], window, preferred_element_type=jnp.float32)
        plain = field[(2 * g + 1) * frag_rows : (2 * g + 3) * frag_rows, 0:span]
        base = jnp.dot(keep[...], plain, preferred_element_type=jnp.float32)
        total = (shifted_sum(y)[:, 0:span] + b2[...] + base).astype(jnp.bfloat16)
        for s in range(half * feats // strip):
            out[panel[g * (half * feats // strip) + s]] = total[s * strip : (s + 1) * strip]


def spread_kernel(plan, feats, outs, w1, w2, one, top, low, two, keep):
    rows, frag = plan.rows, plan.frag
    block = frag * rows
    part = 3 * feats

    def place(shape):
        channel = iota(shape, 0)
        column = iota(shape, 1)
        inner = column % block
        pixel = column // block * rows + inner % rows
        return jnp.where(inner // rows == channel, pixel, -1)

    def taps(weight, i):
        return weight[i * part : (i + 1) * part, :]

    def sums(weight, hit, first):
        total = 0.0
        for i in range(3):
            mask = (hit == first + i).astype(jnp.float32).astype(jnp.bfloat16)
            total = total + jnp.dot(taps(weight, i), mask, preferred_element_type=jnp.float32)
        return total.astype(jnp.bfloat16)

    hit = place((frag, one.shape[1]))
    for q in range(outs):
        rows_q = sums(w1, hit, q + rows - 1)
        for s in range(3):
            at = (s * outs + q) * feats
            one[at : at + feats, :] = rows_q[s * feats : (s + 1) * feats]
        if q == 0:
            low[...] = rows_q[:, : low.shape[1]]
    top[...] = sums(w1, place((frag, top.shape[1])), rows - 2)
    shape = (feats, two.shape[1])
    hit = jnp.where(iota(shape, 1) % feats == iota(shape, 0), iota(shape, 1) // feats, -1)
    for q in range(outs):
        rows_q = sums(w2, hit, q)
        for s in range(3):
            at = (s * outs + q) * feats
            two[at : at + feats, :] = rows_q[s * feats : (s + 1) * feats]
    shape = keep.shape
    inner = iota(shape, 1) % block
    pixel = iota(shape, 1) // block * rows + inner % rows
    same = (iota(shape, 0) // feats == pixel) & (iota(shape, 0) % feats == inner // rows)
    keep[...] = same.astype(jnp.float32).astype(jnp.bfloat16)


def shards(
    payload,
    opacity,
    depth_order,
    footprints,
    panel_map,
    conv1_weight,
    conv1_bias,
    conv2_weight,
    conv2_bias,
):
    row_groups = lax.axis_size("gx")
    n = lax.axis_size("gy")
    x = lax.axis_index("gx")
    y = lax.axis_index("gy")
    _, rows, channels, lanes = payload.shape
    tiles, depth = depth_order.shape
    plan = Plan(n, tiles, rows, channels, lanes, depth)
    feats = conv2_weight.shape[1]
    across = plan.across
    most = tiles - across

    half = n // 2
    spec_s = pl.BlockSpec(memory_space=pltpu.SMEM)
    spec_v = pl.BlockSpec(memory_space=pltpu.VMEM)
    spec_h = pl.BlockSpec(memory_space=pltpu.HBM)
    limit = pltpu.CompilerParams(vmem_limit_bytes=40 << 20)
    pixels = payload.transpose(0, 2, 1, 3)

    def cost(micros):
        return pl.CostEstimate(flops=0, bytes_accessed=int(micros * 3.6e6), transcendentals=0)

    message = jax.ShapeDtypeStruct((plan.groups, rows, lanes), payload.dtype)
    *packed, thin, table = pl.pallas_call(
        functools.partial(first_kernel, plan),
        out_shape=[message] * half
        + [
            jax.ShapeDtypeStruct((n, plan.thin_pair, rows, lanes), payload.dtype),
            jax.ShapeDtypeStruct((n * tiles,), jnp.int32),
        ],
        in_specs=[spec_s, spec_v, spec_h, spec_h],
        out_specs=[spec_v] * (half + 1) + [spec_s],
        scratch_shapes=[
            pltpu.VMEM(pixels.shape, payload.dtype),
            pltpu.VMEM(opacity.shape, payload.dtype),
            pltpu.SemaphoreType.DMA((half,)),
            pltpu.SemaphoreType.DMA,
            pltpu.SemaphoreType.DMA,
        ],
        compiler_params=pltpu.CompilerParams(vmem_limit_bytes=60 << 20),
        cost_estimate=cost(5),
        name="first",
    )(footprints, depth_order, pixels, opacity)
    inbox_mirror = [packed[0]] + [paired(packed[k], "gy", k) for k in range(1, half)]
    inbox_mirror = [block.reshape(-1, lanes) for block in inbox_mirror]

    thin = lax.all_to_all(thin, "gy", split_axis=0, concat_axis=0, tiled=True)
    thins = [thin, rotated(thin, "gx", 1), rotated(thin, "gx", -1)]

    near = [list(range(i, i + half)) for i in range(0, n, half)]
    inbox_own = pl.pallas_call(
        functools.partial(pack_kernel, plan),
        out_shape=jax.ShapeDtypeStruct((half, plan.groups, rows, lanes), payload.dtype),
        in_specs=[spec_s] + [spec_v] * 2,
        out_specs=spec_v,
        scratch_shapes=[pltpu.SemaphoreType.DMA((half,))],
        compiler_params=limit,
        cost_estimate=cost(4),
        name="pack",
    )(table, pixels, opacity)
    inbox_own = lax.all_to_all(
        inbox_own, "gy", split_axis=0, concat_axis=0, axis_index_groups=near, tiled=True
    )
    inbox_own = [inbox_own.reshape(-1, lanes)]

    def order_of(block):
        block = block[:, tiles + 1 : 2 * plan.thin : plan.thin]
        return block.astype(jnp.int32).reshape(n, 2 * rows, lanes)[:, :tiles, :depth]

    orders = [order_of(thins[0]), order_of(thins[2])]
    thins = [block.reshape(-1, lanes) for block in thins]

    def tables(order, kind, halo, mirror):
        slots = jnp.arange(order.shape[0], dtype=jnp.int32)[:, None] + (across if kind == 0 else 0)
        column = order % n
        local = order // n == x
        source = jnp.where(local, 0, 1 + kind) * n + column
        source = source * (tiles + 1) + (tiles if halo else slots)
        mine = local & (column // half == y // half)
        sender = (column ^ y) % half if mirror else column % half
        target = ((2 * kind + halo) * half + sender) * tiles + slots
        return source, jnp.where(mine, target, 4 * half * tiles)

    frag_rows = plan.frag * rows
    tail = plan.halo_pad * rows

    def blend(mirror, inbox):
        column = y ^ half if mirror else y

        def beside_of(order, step):
            return lax.dynamic_index_in_dim(order, (column + n + step) % n, 0, keepdims=False)

        here = [beside_of(order, 0) for order in orders]
        beside = [
            jnp.stack(
                [beside_of(order, -1)[across - 1 :: across], beside_of(order, 1)[0::across]], axis=1
            ).reshape(2 * TYD, depth)
            for order in orders
        ]
        pieces = [
            tables(here[0][across:], 0, 0, mirror),
            tables(here[1][:most], 1, 0, mirror),
            tables(beside[0][across:], 0, 1, mirror),
            tables(beside[1][:most], 1, 1, mirror),
        ]
        alpha_at = jnp.concatenate([a for a, _ in pieces]).reshape(-1)
        weight_at = jnp.concatenate([w for _, w in pieces]).reshape(-1)
        def sums(slots, dtype=payload.dtype):
            return jax.ShapeDtypeStruct((slots * frag_rows + tail, lanes), dtype)

        middle = most - across
        if mirror:
            made = [sums(middle, jnp.float32), sums(middle), sums(across + 1), sums(across + 1)]
        else:
            made = [sums(most, jnp.float32), sums(most + 1)]
        return pl.pallas_call(
            functools.partial(blend_kernel, plan, mirror),
            out_shape=made,
            in_specs=[spec_s] * 2 + [spec_v] * (3 + len(inbox)),
            out_specs=[spec_v] * len(made),
            scratch_shapes=[
                pltpu.VMEM((3 * n * (tiles + 1), 2 * rows, lanes), jnp.float32),
                pltpu.VMEM((4 * half * tiles + 1, 2 * rows, lanes), jnp.float32),
                pltpu.VMEM((4 * most, 2 * rows, lanes), jnp.float32),
            ],
            compiler_params=limit,
            cost_estimate=cost(3),
            name="blend_mirror" if mirror else "blend_own",
        )(alpha_at, weight_at, *thins, *inbox)

    inner, inner_next, edge_over, edge_cross = blend(1, inbox_mirror)
    edge_over = paired(edge_over, "gy", half)
    route = [
        (i * n + j, (i + 1) % row_groups * n + (j ^ half))
        for i in range(row_groups)
        for j in range(n)
    ]
    edge_cross = lax.ppermute(edge_cross, ("gx", "gy"), route)
    inner_next = rotated(inner_next, "gx", 1)
    inner = (inner + inner_next.astype(jnp.float32)).astype(payload.dtype)
    inner, thins[0] = lax.optimization_barrier((inner, thins[0]))
    inner = paired(inner, "gy", half)
    own, kept = blend(0, inbox_own)
    cut = most // 2 * frag_rows
    got = [kept[:cut], kept[cut : 2 * cut], kept[2 * cut :]]
    got = [rotated(piece, "gx", 1) for piece in got]

    band_half = 2 * rows
    w1, w2, _ = lax.optimization_barrier((conv1_weight, conv2_weight, table))
    w1 = w1.reshape(-1, w1.shape[2])
    w2 = w2.reshape(-1, w2.shape[2])

    def matrix(height, width):
        return jax.ShapeDtypeStruct((height, width), payload.dtype)

    one, top, low, two, keep = pl.pallas_call(
        functools.partial(spread_kernel, plan, feats, band_half),
        out_shape=[
            matrix(3 * band_half * feats, 4 * frag_rows),
            matrix(3 * feats, 2 * frag_rows),
            matrix(3 * feats, 2 * frag_rows),
            matrix(3 * band_half * feats, (band_half + 2) * feats),
            matrix(band_half * feats, 2 * frag_rows),
        ],
        in_specs=[spec_v] * 2,
        out_specs=[spec_v] * 5,
        compiler_params=limit,
        cost_estimate=cost(4),
        name="spread",
    )(w1, w2)
    b1 = jnp.tile(conv1_bias, band_half)[:, None]
    b2 = jnp.tile(conv2_bias, band_half)[:, None]
    spots = jnp.stack([x > 0, x < row_groups - 1, y > 0, y < n - 1]).astype(jnp.int32)
    band = TYD * rows
    strip = band // n
    span = across * lanes
    pieces = pl.pallas_call(
        functools.partial(conv_kernel, plan, feats),
        out_shape=jax.ShapeDtypeStruct((n, strip * feats, span), jnp.bfloat16),
        in_specs=[spec_s] * 2 + [spec_v] * (12 + len(got)),
        out_specs=spec_v,
        scratch_shapes=[
            pltpu.VMEM(((TYD + 2) * frag_rows, span + lanes), jnp.bfloat16),
            pltpu.VMEM(((band + 2) * feats, span + lanes), jnp.bfloat16),
        ],
        compiler_params=limit,
        cost_estimate=cost(4),
        name="conv",
    )(spots, panel_map, own, kept, inner, edge_over, edge_cross, *got, one, top, low, two, keep, b1, b2)
    shown = lax.all_to_all(pieces, "gy", split_axis=0, concat_axis=0, tiled=True)
    shown = shown.transpose(1, 0, 2).reshape(1, 1, strip, feats, n * span)
    return shown


def solution(mesh):
    return jax.shard_map(
        shards,
        mesh=mesh,
        in_specs=(
            P(("gx", "gy"), None, None, None),
            P(("gx", "gy"), None, None),
            P(("gx", "gy"), None),
            P(),
            P(),
            P(),
            P(),
            P(),
            P(),
        ),
        out_specs=P("gx", "gy", None, None, None),
        check_vma=False,
    )
```

```python
import functools

import jax
import jax.numpy as jnp
from jax import lax
from jax.experimental import pallas as pl
from jax.experimental.pallas import tpu as pltpu
from jax.sharding import PartitionSpec as P

TYD = 4
SPAN = 4 * TYD


def rotated(block, axis, distance):
    count = lax.axis_size(axis)
    return lax.ppermute(block, axis, [(i, (i + distance) % count) for i in range(count)])


def paired(block, axis, step):
    return lax.ppermute(block, axis, [(i, i ^ step) for i in range(lax.axis_size(axis))])


def split(value, size):
    if size & (size - 1) == 0:
        return value >> (size.bit_length() - 1), value & (size - 1)
    return lax.div(value, size), lax.rem(value, size)


def iota(shape, dim):
    return lax.broadcasted_iota(jnp.int32, shape, dim)


class Plan:
    def __init__(self, count, tiles, rows, channels, lanes, depth):
        self.count = count
        self.half = count // 2
        self.tiles = tiles
        self.across = tiles // TYD
        self.rows = rows
        self.channels = channels
        self.lanes = lanes
        self.depth = depth
        self.frag = channels + 1
        self.blocks = lanes // SPAN
        self.halo = -(-self.frag // self.blocks)
        self.at_halo = tiles * self.frag
        per = 16 // rows
        self.groups = -(-(self.at_halo + self.halo) // per) * per
        self.halo_pad = self.groups - self.at_halo
        self.thin = -(-(tiles + 2) // 2) * 2
        self.thin_pair = -(-2 * self.thin // per) * per


def neighbours(plan, column):
    n, tiles = plan.count, plan.tiles
    right = jnp.where(column == n - 1, 0, column + 1) * tiles
    left = jnp.where(column == 0, n - 1, column - 1) * tiles + plan.across - 1
    return right, left


def joined(right, left, j, lane, axis):
    both = jnp.where(lane < 2, right.astype(jnp.float32), left.astype(jnp.float32))
    return pltpu.roll(both, 4 * j + 2, axis)


def thin_part(plan, table, opacity, order, out):
    n, tiles = plan.count, plan.tiles
    lane = iota((plan.rows, plan.lanes), 1)
    empty = jnp.zeros((plan.rows, plan.lanes), jnp.bfloat16)
    for d in range(n):
        places = [(d, 0), (d ^ plan.half, plan.thin)]
        for t in range(tiles):
            group = opacity[table[d * tiles + t]]
            for to, at in places:
                out[to, at + t] = group
        right = (d + 1) % n * tiles
        left = (d - 1) % n * tiles + plan.across - 1
        halo = jnp.zeros((plan.rows, plan.lanes), jnp.float32)
        for j in range(TYD):
            f_r, f_l = table[right + j * plan.across], table[left + j * plan.across]
            inside = (lane >= 4 * j) & (lane < 4 * j + 4)
            halo = jnp.where(inside, joined(opacity[f_r], opacity[f_l], j, lane, 1), halo)
        for to, at in places:
            out[to, at + tiles] = halo.astype(jnp.bfloat16)
        for i in range(2):
            out[d, i * plan.thin + tiles + 1] = order[i * plan.rows : (i + 1) * plan.rows]
            for g in range(tiles + 2, plan.thin):
                out[d, i * plan.thin + g] = empty
        for g in range(2 * plan.thin, plan.thin_pair):
            out[d, g] = empty


def send_fragments(plan, columns, table, payload, outs, sem):
    for e, column in enumerate(columns):

        def move(t, _, e=e, column=column):
            f = table[column * plan.tiles + t]
            pltpu.make_async_copy(
                payload.at[f], outs[e].at[pl.ds(t * plan.frag, plan.channels)], sem.at[e]
            ).start()
            return 0

        lax.fori_loop(0, plan.tiles, move, 0)


def add_edges(plan, columns, table, payload, opacity, outs):
    across = plan.across
    lane = iota((plan.channels, plan.rows, plan.lanes), 2)
    lane_one = iota((plan.rows, plan.lanes), 1)
    for out, column in zip(outs, columns):
        for t in range(plan.tiles):
            out[t * plan.frag + plan.channels] = opacity[table[column * plan.tiles + t]]
        right, left = neighbours(plan, column)
        spread = jnp.zeros((plan.channels, plan.rows, plan.lanes), jnp.float32)
        for j in range(TYD):
            f_r, f_l = table[right + j * across], table[left + j * across]
            inside = (lane >= 4 * j) & (lane < 4 * j + 4)
            spread = jnp.where(inside, joined(payload[f_r], payload[f_l], j, lane, 2), spread)
        for i in range(plan.halo_pad):
            group = jnp.zeros((plan.rows, plan.lanes), jnp.float32)
            for b in range(plan.blocks):
                c = i * plan.blocks + b
                if c < plan.channels:
                    moved = pltpu.roll(spread[c], SPAN * b, 1) if b else spread[c]
                    group = jnp.where(
                        (lane_one >= SPAN * b) & (lane_one < SPAN * b + SPAN), moved, group
                    )
            out[plan.at_halo + i] = group.astype(jnp.bfloat16)


def await_fragments(plan, outs, sem):
    for e, out in enumerate(outs):
        whole = out.at[pl.ds(0, plan.tiles * plan.channels)]
        pltpu.make_async_copy(whole, whole, sem.at[e]).wait()


def first_kernel(plan, footprints, depth_order, payload, opacity, *rest):
    n, tiles, half = plan.count, plan.tiles, plan.half
    outs = rest[:half]
    thin, table, held, cover, sem, sem_held, sem_cover = rest[half:]
    x, y = lax.axis_index("gx"), lax.axis_index("gy")
    me = x * n + y
    bring_cover = pltpu.make_async_copy(opacity, cover, sem_cover)
    bring_cover.start()
    bring = pltpu.make_async_copy(payload, held, sem_held)
    bring.start()

    def look(f, _):
        owner, slot = split(footprints[me, f], tiles)
        table[split(owner, n)[1] * tiles + slot] = f
        return 0

    lax.fori_loop(0, footprints.shape[1], look, 0, unroll=8)
    columns = [y ^ half ^ k for k in range(half)]
    send_fragments(plan, columns, table, payload, outs, sem)
    order = depth_order[...].astype(jnp.float32)
    order = jnp.concatenate(
        [order, jnp.zeros((tiles, plan.lanes - plan.depth), jnp.float32)], axis=1
    ).astype(jnp.bfloat16)
    bring_cover.wait()
    thin_part(plan, table, cover, order, thin)
    bring.wait()
    add_edges(plan, columns, table, held, cover, outs)
    await_fragments(plan, outs, sem)


def pack_kernel(plan, table, payload, opacity, out, sem):
    half = plan.half
    y = lax.axis_index("gy")
    base = y - (y & (half - 1))
    columns = [base + e for e in range(half)]
    outs = [out.at[e] for e in range(half)]
    send_fragments(plan, columns, table, payload, outs, sem)
    add_edges(plan, columns, table, payload, opacity, outs)
    await_fragments(plan, outs, sem)


def fold(x):
    return x.reshape(x.shape[0] * x.shape[1], x.shape[2])


def blend_kernel(plan, mirror, alpha_at, weight_at, own_in, prev_in, next_in, *rest):
    if mirror:
        *inbox, out_own, out_next, edge_over, edge_cross, alpha, weight, clear = rest
    else:
        *inbox, out_own, next_first, next_middle, out_next, alpha, weight, clear = rest
    n, tiles, across, sources = plan.count, plan.tiles, plan.across, plan.half
    rows, lanes = plan.rows, plan.lanes
    pair = 2 * rows
    frag_rows = plan.frag * rows
    halo_row = plan.at_halo * rows
    message = plan.groups * rows
    lane = iota((pair, lanes), 1)
    most = tiles - across

    def read(k, start, stop):
        ref, at = (inbox[k], 0) if mirror else (inbox[0], k * message)
        return ref[at + start : at + stop, :].astype(jnp.float32)

    for kind, ref in enumerate((own_in, prev_in, next_in)):
        for s in range(n):
            for t in range(tiles + 1):
                if kind and t < tiles and not across <= t < most:
                    continue
                row = (s * plan.thin_pair + mirror * plan.thin + t) * rows
                base = row // 16 * 16
                held = ref[base : base + 16, :].astype(jnp.float32)
                part = held[row - base : row - base + rows]
                alpha[(kind * n + s) * (tiles + 1) + t] = jnp.concatenate([part, part], axis=0)

    weight[...] = jnp.zeros_like(weight)

    def through(i, _):
        seen = jnp.ones((pair, lanes), jnp.float32)
        for d in range(plan.depth):
            weight[weight_at[i * plan.depth + d]] = seen
            seen = seen * (1.0 - alpha[alpha_at[i * plan.depth + d]])
        clear[i] = seen
        return 0

    lax.fori_loop(0, 4 * most, through, 0, unroll=4)

    step = 3 * pair
    while frag_rows % step or step % 16:
        step += pair
    shape = (step // pair, pair, lanes)
    def turned(x, by):
        return pltpu.roll(x, by % pair, 1)

    low_rows = iota(shape, 1) % rows < rows // 2
    for at in range(0, frag_rows, step):
        edges = {}
        for t in range(tiles):
            keeps, gives = t >= across, t < most
            total_own = jnp.zeros(shape, jnp.float32)
            total_next = jnp.zeros(shape, jnp.float32)
            for k in range(sources):
                start = t * frag_rows + at
                held = read(k, start, start + step).reshape(shape)
                if keeps:
                    total_own += weight[k * tiles + t][None] * held
                if gives:
                    total_next += weight[(2 * sources + k) * tiles + t][None] * held
            if at + step == frag_rows:
                mask = (iota(shape, 0) == step // pair - 1) & (iota(shape, 1) >= rows)
                cover = jnp.zeros((pair, lanes), jnp.float32)
                if keeps and not mirror:
                    cover = 1.0 - clear[t - across]
                total_own = jnp.where(mask, cover[None], total_own)
                cover = jnp.zeros((pair, lanes), jnp.float32)
                if t < across and not mirror:
                    cover = 1.0 - clear[most + t]
                total_next = jnp.where(mask, cover[None], total_next)

            def put(ref, slot, total):
                start = slot * frag_rows + at
                ref[start : start + step, :] = total.reshape(step, lanes).astype(ref.dtype)

            if t < across:
                edges[t] = total_next
            if t >= most:
                edges[t] = total_own
            if not mirror:
                if gives:
                    third = most // 2
                    put(next_first if t < third else next_middle, t % third, total_next)
                if keeps:
                    put(out_own, t - across, total_own)
            elif gives and keeps:
                put(out_next, t - across, total_next)
                put(out_own, t - across, total_own)
        first, last = edges[most], edges[tiles - 1]
        top = jnp.where(low_rows, turned(first, -(rows // 2)), last)
        if mirror:
            for c in range(across):
                put(edge_cross, c, edges[c])
                put(edge_over, 1 + c, edges[most + c])
            put(edge_cross, across, top)
            first, last = edges[0], edges[across - 1]
            put(edge_over, 0, jnp.where(low_rows, first, turned(last, rows // 2)))
        else:
            put(out_next, 0, top)

    halo_shape = (plan.halo_pad * rows // pair, pair, lanes)

    def merged(kind, source):
        out = jnp.zeros((pair, lanes), jnp.float32)
        first = across if kind == 0 else 0
        for u in range(most):
            out = jnp.where(lane // 2 == first + u, source(u, first + u), out)
        return out

    def widened(x):
        out = jnp.zeros((pair, lanes), jnp.float32)
        for b in range(plan.blocks):
            moved = pltpu.roll(x, SPAN * b, 1) if b else x
            out = jnp.where(lane // SPAN == b, moved, out)
        return out

    totals = [jnp.zeros(halo_shape, jnp.float32) for _ in range(2)]
    for k in range(sources):
        held = read(k, halo_row, halo_row + plan.halo_pad * rows).reshape(halo_shape)
        for kind in range(2):
            base = (2 * kind + 1) * sources * tiles + k * tiles
            by = widened(merged(kind, lambda u, v: weight[base + v]))
            totals[kind] += by[None] * held
    if not mirror:
        i_cov, b_cov = plan.channels // plan.blocks, plan.channels % plan.blocks
        group = iota(halo_shape, 0) * 2 + iota(halo_shape, 1) // rows
        at_cov = (group == i_cov) & (iota(halo_shape, 2) // SPAN == b_cov)
        for kind in range(2):
            cov = merged(kind, lambda u, v: 1.0 - clear[(2 + kind) * most + u])
            if kind == 1:
                cov = jnp.where(lane // 4 == 0, cov, 0.0)
            cov = pltpu.roll(cov, SPAN * b_cov, 1) if b_cov else cov
            totals[kind] = jnp.where(at_cov, cov[None], totals[kind])
    length = plan.halo_pad * rows

    def put_halo(ref, total):
        start = ref.shape[0] - length
        ref[start : start + length, :] = total.reshape(length, lanes).astype(ref.dtype)

    put_halo(out_own, totals[0])
    if mirror:
        put_halo(out_next, totals[1])
        put_halo(edge_over, totals[1])
        put_halo(edge_cross, totals[0])
    else:
        band = iota(halo_shape, 2) // 4 % TYD
        put_halo(out_next, jnp.where(band == TYD - 1, totals[0], totals[1]))


def conv_kernel(
    plan,
    feats,
    spots,
    panel,
    own,
    kept,
    kept_halo,
    inner,
    edge_over,
    edge_cross,
    *rest,
):
    *got, one, top, low, two, keep, b1, b2, out, field, hidden = rest
    tiles, across, rows, lanes = plan.tiles, plan.across, plan.rows, plan.lanes
    frag_rows = plan.frag * rows
    most = tiles - across
    span = across * lanes
    wide = span + lanes
    has_top, has_low = spots[0], spots[1]
    has_left, has_right = spots[2], spots[3]

    def tile(ref, t, turn=0):
        part = ref[t * frag_rows : (t + 1) * frag_rows, :].astype(jnp.float32)
        if turn:
            part = part.reshape(-1, 2 * rows, lanes)
            part = pltpu.roll(part, turn % (2 * rows), 1).reshape(frag_rows, lanes)
        return part

    def shifted(t, turn=0):
        for ref in got:
            slots = ref.shape[0] // frag_rows
            if t < slots:
                return tile(ref, t, turn)
            t -= slots

    for c in range(across):
        at = slice(c * lanes, (c + 1) * lanes)
        last = c == across - 1
        turn = 0 if last else rows // 2
        value = shifted(most, turn) + tile(edge_cross, across, turn)
        value = jnp.where(has_top != 0, value, 0.0)
        field[0:frag_rows, at] = value.astype(jnp.bfloat16)
        for j in range(TYD):
            t = j * across + c
            if j == 0:
                value = shifted(t) + tile(edge_cross, c)
            elif j < TYD - 1:
                value = shifted(t) + tile(own, t - across) + tile(inner, t - across)
            else:
                value = tile(own, t - across) + tile(edge_over, 1 + c)
            field[(j + 1) * frag_rows : (j + 2) * frag_rows, at] = value.astype(jnp.bfloat16)
        at_low = (TYD + 1) * frag_rows
        value = tile(kept, c) + tile(edge_over, 0, -(rows // 2) if last else 0)
        value = jnp.where(has_low != 0, value, 0.0)
        field[at_low : at_low + frag_rows, at] = value.astype(jnp.bfloat16)

    length = plan.halo_pad * rows

    def edge(ref):
        at = ref.shape[0] - length
        return ref[at : at + length, :].astype(jnp.float32)

    h_got = edge(got[-1])
    band = iota((length, lanes), 1) // 4 % TYD
    h_all = edge(own) + edge(inner) + jnp.where(band == TYD - 1, 0.0, h_got)
    h_kept = edge(kept_halo) + edge(edge_over)
    h_got = h_got + edge(edge_cross)
    lane = iota((rows, lanes), 1)
    valid = ((lane < 2) & (has_right != 0)) | ((lane >= lanes - 2) & (has_left != 0))

    def unpacked(source, j):
        pieces = []
        for c in range(plan.frag):
            i, b = c // plan.blocks, c % plan.blocks
            piece = source[i * rows : (i + 1) * rows]
            shift = (-(SPAN * b + 4 * j + 2)) % lanes
            pieces.append(jnp.where(valid, pltpu.roll(piece, shift, 1), 0.0))
        return jnp.concatenate(pieces, axis=0).astype(jnp.bfloat16)

    wide_zero = jnp.zeros((frag_rows, lanes), jnp.bfloat16)
    at = slice(span, wide)
    field[0:frag_rows, at] = jnp.where(has_top != 0, unpacked(h_got, TYD - 1), wide_zero)
    for j in range(TYD):
        field[(j + 1) * frag_rows : (j + 2) * frag_rows, at] = unpacked(h_all, j)
    at_low = (TYD + 1) * frag_rows
    field[at_low : at_low + frag_rows, at] = jnp.where(has_low != 0, unpacked(h_kept, 0), wide_zero)

    def shifted_sum(y):
        part = y.shape[0] // 3
        return (
            pltpu.roll(y[:part], 1, 1)
            + y[part : 2 * part]
            + pltpu.roll(y[2 * part :], wide - 1, 1)
        )

    def act(y, bias):
        x = shifted_sum(y) + bias
        return x * (1.0 / (1.0 + jnp.exp(-x)))

    half = 2 * rows
    groups = TYD // 2
    col = iota((1, wide), 1)
    inside = ((col != span) | (has_right != 0)) & ((col != wide - 1) | (has_left != 0))

    def layer(weights, field, first, height, apart):
        spots = [slice(first + g * apart, first + g * apart + height) for g in range(groups)]
        sides = jnp.concatenate([field[at, span:wide] for at in spots], axis=1)
        sides = jnp.dot(weights[...], sides, preferred_element_type=jnp.float32)
        for g, at in enumerate(spots):
            plain = jnp.dot(weights[...], field[at, 0:span], preferred_element_type=jnp.float32)
            yield g, jnp.concatenate([plain, sides[:, g * lanes : (g + 1) * lanes]], axis=1)

    for g, y in layer(one, field, 0, 4 * frag_rows, 2 * frag_rows):
        h = jnp.where(inside, act(y, b1[...]), 0.0)
        at = feats + g * half * feats
        hidden[at : at + half * feats, :] = h.astype(jnp.bfloat16)
    for ref, at_field, at_hidden, has in (
        (top, 0, 0, has_top),
        (low, TYD * frag_rows, feats * (1 + groups * half), has_low),
    ):
        window = field[at_field : at_field + 2 * frag_rows, :]
        y = jnp.dot(ref[...], window, preferred_element_type=jnp.float32)
        h = jnp.where(inside & (has != 0), act(y, b1[0:feats]), 0.0)
        hidden[at_hidden : at_hidden + feats, :] = h.astype(jnp.bfloat16)
    strip = out.shape[1]
    for g, y in layer(two, hidden, 0, (half + 2) * feats, half * feats):
        plain = field[(2 * g + 1) * frag_rows : (2 * g + 3) * frag_rows, 0:span]
        base = jnp.dot(keep[...], plain, preferred_element_type=jnp.float32)
        total = (shifted_sum(y)[:, 0:span] + b2[...] + base).astype(jnp.bfloat16)
        for s in range(half * feats // strip):
            out[panel[g * (half * feats // strip) + s]] = total[s * strip : (s + 1) * strip]


def display_kernel(span, shown, out, sem):
    for s in range(shown.shape[0]):
        pltpu.make_async_copy(shown.at[s], out.at[:, pl.ds(s * span, span)], sem).start()
    pltpu.make_async_copy(out, out, sem).wait()


def spread_kernel(plan, feats, outs, w1, w2, one, top, low, two, keep):
    rows, frag = plan.rows, plan.frag
    block = frag * rows
    part = 3 * feats

    def place(shape):
        channel = iota(shape, 0)
        column = iota(shape, 1)
        inner = column % block
        pixel = column // block * rows + inner % rows
        return jnp.where(inner // rows == channel, pixel, -1)

    def taps(weight, i):
        return weight[i * part : (i + 1) * part, :]

    def sums(weight, hit, first):
        total = 0.0
        for i in range(3):
            mask = (hit == first + i).astype(jnp.float32).astype(jnp.bfloat16)
            total = total + jnp.dot(taps(weight, i), mask, preferred_element_type=jnp.float32)
        return total.astype(jnp.bfloat16)

    hit = place((frag, one.shape[1]))
    for q in range(outs):
        rows_q = sums(w1, hit, q + rows - 1)
        for s in range(3):
            at = (s * outs + q) * feats
            one[at : at + feats, :] = rows_q[s * feats : (s + 1) * feats]
        if q == 0:
            low[...] = rows_q[:, : low.shape[1]]
    top[...] = sums(w1, place((frag, top.shape[1])), rows - 2)
    shape = (feats, two.shape[1])
    hit = jnp.where(iota(shape, 1) % feats == iota(shape, 0), iota(shape, 1) // feats, -1)
    for q in range(outs):
        rows_q = sums(w2, hit, q)
        for s in range(3):
            at = (s * outs + q) * feats
            two[at : at + feats, :] = rows_q[s * feats : (s + 1) * feats]
    shape = keep.shape
    inner = iota(shape, 1) % block
    pixel = iota(shape, 1) // block * rows + inner % rows
    same = (iota(shape, 0) // feats == pixel) & (iota(shape, 0) % feats == inner // rows)
    keep[...] = same.astype(jnp.float32).astype(jnp.bfloat16)


def shards(
    payload,
    opacity,
    depth_order,
    footprints,
    panel_map,
    conv1_weight,
    conv1_bias,
    conv2_weight,
    conv2_bias,
):
    row_groups = lax.axis_size("gx")
    n = lax.axis_size("gy")
    x = lax.axis_index("gx")
    y = lax.axis_index("gy")
    _, rows, channels, lanes = payload.shape
    tiles, depth = depth_order.shape
    plan = Plan(n, tiles, rows, channels, lanes, depth)
    feats = conv2_weight.shape[1]
    across = plan.across
    most = tiles - across

    half = n // 2
    spec_s = pl.BlockSpec(memory_space=pltpu.SMEM)
    spec_v = pl.BlockSpec(memory_space=pltpu.VMEM)
    spec_h = pl.BlockSpec(memory_space=pltpu.HBM)
    limit = pltpu.CompilerParams(vmem_limit_bytes=40 << 20)
    pixels = payload.transpose(0, 2, 1, 3)

    def cost(micros):
        return pl.CostEstimate(flops=0, bytes_accessed=int(micros * 3.6e6), transcendentals=0)

    message = jax.ShapeDtypeStruct((plan.groups, rows, lanes), payload.dtype)
    *packed, thin, table = pl.pallas_call(
        functools.partial(first_kernel, plan),
        out_shape=[message] * half
        + [
            jax.ShapeDtypeStruct((n, plan.thin_pair, rows, lanes), payload.dtype),
            jax.ShapeDtypeStruct((n * tiles,), jnp.int32),
        ],
        in_specs=[spec_s, spec_v, spec_h, spec_h],
        out_specs=[spec_v] * (half + 1) + [spec_s],
        scratch_shapes=[
            pltpu.VMEM(pixels.shape, payload.dtype),
            pltpu.VMEM(opacity.shape, payload.dtype),
            pltpu.SemaphoreType.DMA((half,)),
            pltpu.SemaphoreType.DMA,
            pltpu.SemaphoreType.DMA,
        ],
        compiler_params=pltpu.CompilerParams(vmem_limit_bytes=60 << 20),
        cost_estimate=cost(5),
        name="first",
    )(footprints, depth_order, pixels, opacity)
    inbox_mirror = [packed[0]] + [paired(packed[k], "gy", k) for k in range(1, half)]
    inbox_mirror = [block.reshape(-1, lanes) for block in inbox_mirror]

    thin = lax.all_to_all(thin, "gy", split_axis=0, concat_axis=0, tiled=True)
    thins = [thin, rotated(thin, "gx", 1), rotated(thin, "gx", -1)]

    near = [list(range(i, i + half)) for i in range(0, n, half)]
    inbox_own = pl.pallas_call(
        functools.partial(pack_kernel, plan),
        out_shape=jax.ShapeDtypeStruct((half, plan.groups, rows, lanes), payload.dtype),
        in_specs=[spec_s] + [spec_v] * 2,
        out_specs=spec_v,
        scratch_shapes=[pltpu.SemaphoreType.DMA((half,))],
        compiler_params=limit,
        cost_estimate=cost(4),
        name="pack",
    )(table, pixels, opacity)
    inbox_own = lax.all_to_all(
        inbox_own, "gy", split_axis=0, concat_axis=0, axis_index_groups=near, tiled=True
    )
    inbox_own = [inbox_own.reshape(-1, lanes)]

    def order_of(block):
        block = block[:, tiles + 1 : 2 * plan.thin : plan.thin]
        return block.astype(jnp.int32).reshape(n, 2 * rows, lanes)[:, :tiles, :depth]

    orders = [order_of(thins[0]), order_of(thins[2])]
    thins = [block.reshape(-1, lanes) for block in thins]

    def tables(order, kind, halo, mirror):
        slots = jnp.arange(order.shape[0], dtype=jnp.int32)[:, None] + (across if kind == 0 else 0)
        column = order % n
        local = order // n == x
        source = jnp.where(local, 0, 1 + kind) * n + column
        source = source * (tiles + 1) + (tiles if halo else slots)
        mine = local & (column // half == y // half)
        sender = (column ^ y) % half if mirror else column % half
        target = ((2 * kind + halo) * half + sender) * tiles + slots
        return source, jnp.where(mine, target, 4 * half * tiles)

    frag_rows = plan.frag * rows
    tail = plan.halo_pad * rows

    def blend(mirror, inbox):
        column = y ^ half if mirror else y

        def beside_of(order, step):
            return lax.dynamic_index_in_dim(order, (column + n + step) % n, 0, keepdims=False)

        here = [beside_of(order, 0) for order in orders]
        beside = [
            jnp.stack(
                [beside_of(order, -1)[across - 1 :: across], beside_of(order, 1)[0::across]], axis=1
            ).reshape(2 * TYD, depth)
            for order in orders
        ]
        pieces = [
            tables(here[0][across:], 0, 0, mirror),
            tables(here[1][:most], 1, 0, mirror),
            tables(beside[0][across:], 0, 1, mirror),
            tables(beside[1][:most], 1, 1, mirror),
        ]
        alpha_at = jnp.concatenate([a for a, _ in pieces]).reshape(-1)
        weight_at = jnp.concatenate([w for _, w in pieces]).reshape(-1)
        def sums(slots, dtype=payload.dtype):
            return jax.ShapeDtypeStruct((slots * frag_rows + tail, lanes), dtype)

        middle = most - across
        if mirror:
            made = [sums(middle, jnp.float32), sums(middle), sums(across + 1), sums(across + 1)]
        else:
            piece = jax.ShapeDtypeStruct((most // 2 * frag_rows, lanes), payload.dtype)
            made = [sums(most, jnp.float32), piece, piece, sums(1)]
        return pl.pallas_call(
            functools.partial(blend_kernel, plan, mirror),
            out_shape=made,
            in_specs=[spec_s] * 2 + [spec_v] * (3 + len(inbox)),
            out_specs=[spec_v] * len(made),
            scratch_shapes=[
                pltpu.VMEM((3 * n * (tiles + 1), 2 * rows, lanes), jnp.float32),
                pltpu.VMEM((4 * half * tiles + 1, 2 * rows, lanes), jnp.float32),
                pltpu.VMEM((4 * most, 2 * rows, lanes), jnp.float32),
            ],
            compiler_params=limit,
            cost_estimate=cost(3),
            name="blend_mirror" if mirror else "blend_own",
        )(alpha_at, weight_at, *thins, *inbox)

    inner, inner_next, edge_over, edge_cross = blend(1, inbox_mirror)
    edge_over = paired(edge_over, "gy", half)
    route = [
        (i * n + j, (i + 1) % row_groups * n + (j ^ half))
        for i in range(row_groups)
        for j in range(n)
    ]
    edge_cross = lax.ppermute(edge_cross, ("gx", "gy"), route)
    inner_next = rotated(inner_next, "gx", 1)
    inner = (inner + inner_next.astype(jnp.float32)).astype(payload.dtype)
    inner, thins[0] = lax.optimization_barrier((inner, thins[0]))
    inner = paired(inner, "gy", half)
    own, *kept = blend(0, inbox_own)
    got = [rotated(piece, "gx", 1) for piece in kept]

    band_half = 2 * rows
    w1, w2, _ = lax.optimization_barrier((conv1_weight, conv2_weight, table))
    w1 = w1.reshape(-1, w1.shape[2])
    w2 = w2.reshape(-1, w2.shape[2])

    def matrix(height, width):
        return jax.ShapeDtypeStruct((height, width), payload.dtype)

    one, top, low, two, keep = pl.pallas_call(
        functools.partial(spread_kernel, plan, feats, band_half),
        out_shape=[
            matrix(3 * band_half * feats, 4 * frag_rows),
            matrix(3 * feats, 2 * frag_rows),
            matrix(3 * feats, 2 * frag_rows),
            matrix(3 * band_half * feats, (band_half + 2) * feats),
            matrix(band_half * feats, 2 * frag_rows),
        ],
        in_specs=[spec_v] * 2,
        out_specs=[spec_v] * 5,
        compiler_params=limit,
        cost_estimate=cost(4),
        name="spread",
    )(w1, w2)
    b1 = jnp.tile(conv1_bias, band_half)[:, None]
    b2 = jnp.tile(conv2_bias, band_half)[:, None]
    spots = jnp.stack([x > 0, x < row_groups - 1, y > 0, y < n - 1]).astype(jnp.int32)
    band = TYD * rows
    strip = band // n
    span = across * lanes
    pieces = pl.pallas_call(
        functools.partial(conv_kernel, plan, feats),
        out_shape=jax.ShapeDtypeStruct((n, strip * feats, span), jnp.bfloat16),
        in_specs=[spec_s] * 2 + [spec_v] * (13 + len(got)),
        out_specs=spec_v,
        scratch_shapes=[
            pltpu.VMEM(((TYD + 2) * frag_rows, span + lanes), jnp.bfloat16),
            pltpu.VMEM(((band + 2) * feats, span + lanes), jnp.bfloat16),
        ],
        compiler_params=limit,
        cost_estimate=cost(4),
        name="conv",
    )(spots, panel_map, own, kept[0], kept[2], inner, edge_over, edge_cross, *got, one, top, low, two, keep, b1, b2)
    shown = lax.all_to_all(pieces, "gy", split_axis=0, concat_axis=0, tiled=True)
    shown = pl.pallas_call(
        functools.partial(display_kernel, span),
        out_shape=jax.ShapeDtypeStruct((strip * feats, n * span), payload.dtype),
        in_specs=[spec_v],
        out_specs=spec_h,
        scratch_shapes=[pltpu.SemaphoreType.DMA],
        compiler_params=limit,
        name="display",
    )(shown)
    return shown.reshape(1, 1, strip, feats, n * span)


def solution(mesh):
    return jax.shard_map(
        shards,
        mesh=mesh,
        in_specs=(
            P(("gx", "gy"), None, None, None),
            P(("gx", "gy"), None, None),
            P(("gx", "gy"), None),
            P(),
            P(),
            P(),
            P(),
            P(),
            P(),
        ),
        out_specs=P("gx", "gy", None, None, None),
        check_vma=False,
    )
```

```python
import functools

import jax
import jax.numpy as jnp
from jax import lax
from jax.experimental import pallas as pl
from jax.experimental.pallas import tpu as pltpu
from jax.sharding import PartitionSpec as P

TYD = 4
SPAN = 4 * TYD


def rotated(block, axis, distance):
    count = lax.axis_size(axis)
    return lax.ppermute(block, axis, [(i, (i + distance) % count) for i in range(count)])


def paired(block, axis, step):
    return lax.ppermute(block, axis, [(i, i ^ step) for i in range(lax.axis_size(axis))])


def split(value, size):
    if size & (size - 1) == 0:
        return value >> (size.bit_length() - 1), value & (size - 1)
    return lax.div(value, size), lax.rem(value, size)


def iota(shape, dim):
    return lax.broadcasted_iota(jnp.int32, shape, dim)


class Plan:
    def __init__(self, count, tiles, rows, channels, lanes, depth):
        self.count = count
        self.half = count // 2
        self.tiles = tiles
        self.across = tiles // TYD
        self.rows = rows
        self.channels = channels
        self.lanes = lanes
        self.depth = depth
        self.frag = channels + 1
        self.blocks = lanes // SPAN
        self.halo = -(-self.frag // self.blocks)
        self.at_halo = tiles * self.frag
        per = 16 // rows
        self.groups = -(-(self.at_halo + self.halo) // per) * per
        self.halo_pad = self.groups - self.at_halo
        self.thin = -(-(tiles + 2) // 2) * 2
        self.thin_pair = -(-2 * self.thin // per) * per


def neighbours(plan, column):
    n, tiles = plan.count, plan.tiles
    right = jnp.where(column == n - 1, 0, column + 1) * tiles
    left = jnp.where(column == 0, n - 1, column - 1) * tiles + plan.across - 1
    return right, left


def joined(right, left, j, lane, axis):
    both = jnp.where(lane < 2, right.astype(jnp.float32), left.astype(jnp.float32))
    return pltpu.roll(both, 4 * j + 2, axis)


def thin_part(plan, table, opacity, order, out):
    n, tiles = plan.count, plan.tiles
    lane = iota((plan.rows, plan.lanes), 1)
    empty = jnp.zeros((plan.rows, plan.lanes), jnp.bfloat16)
    for d in range(n):
        places = [(d, 0), (d ^ plan.half, plan.thin)]
        for t in range(tiles):
            group = opacity[table[d * tiles + t]]
            for to, at in places:
                out[to, at + t] = group
        right = (d + 1) % n * tiles
        left = (d - 1) % n * tiles + plan.across - 1
        halo = jnp.zeros((plan.rows, plan.lanes), jnp.float32)
        for j in range(TYD):
            f_r, f_l = table[right + j * plan.across], table[left + j * plan.across]
            inside = (lane >= 4 * j) & (lane < 4 * j + 4)
            halo = jnp.where(inside, joined(opacity[f_r], opacity[f_l], j, lane, 1), halo)
        for to, at in places:
            out[to, at + tiles] = halo.astype(jnp.bfloat16)
        for i in range(2):
            out[d, i * plan.thin + tiles + 1] = order[i * plan.rows : (i + 1) * plan.rows]
            for g in range(tiles + 2, plan.thin):
                out[d, i * plan.thin + g] = empty
        for g in range(2 * plan.thin, plan.thin_pair):
            out[d, g] = empty


def send_fragments(plan, columns, table, payload, outs, sem):
    for e, column in enumerate(columns):

        def move(t, _, e=e, column=column):
            f = table[column * plan.tiles + t]
            pltpu.make_async_copy(
                payload.at[f], outs[e].at[pl.ds(t * plan.frag, plan.channels)], sem.at[e]
            ).start()
            return 0

        lax.fori_loop(0, plan.tiles, move, 0)


def add_edges(plan, columns, table, payload, opacity, outs):
    across = plan.across
    lane = iota((plan.channels, plan.rows, plan.lanes), 2)
    lane_one = iota((plan.rows, plan.lanes), 1)
    for out, column in zip(outs, columns):
        for t in range(plan.tiles):
            out[t * plan.frag + plan.channels] = opacity[table[column * plan.tiles + t]]
        right, left = neighbours(plan, column)
        spread = jnp.zeros((plan.channels, plan.rows, plan.lanes), jnp.float32)
        for j in range(TYD):
            f_r, f_l = table[right + j * across], table[left + j * across]
            inside = (lane >= 4 * j) & (lane < 4 * j + 4)
            spread = jnp.where(inside, joined(payload[f_r], payload[f_l], j, lane, 2), spread)
        for i in range(plan.halo_pad):
            group = jnp.zeros((plan.rows, plan.lanes), jnp.float32)
            for b in range(plan.blocks):
                c = i * plan.blocks + b
                if c < plan.channels:
                    moved = pltpu.roll(spread[c], SPAN * b, 1) if b else spread[c]
                    group = jnp.where(
                        (lane_one >= SPAN * b) & (lane_one < SPAN * b + SPAN), moved, group
                    )
            out[plan.at_halo + i] = group.astype(jnp.bfloat16)


def await_fragments(plan, outs, sem):
    for e, out in enumerate(outs):
        whole = out.at[pl.ds(0, plan.tiles * plan.channels)]
        pltpu.make_async_copy(whole, whole, sem.at[e]).wait()


def first_kernel(plan, footprints, depth_order, payload, opacity, *rest):
    n, tiles, half = plan.count, plan.tiles, plan.half
    outs = rest[:half]
    thin, table, held, cover, sem, sem_held, sem_cover = rest[half:]
    x, y = lax.axis_index("gx"), lax.axis_index("gy")
    me = x * n + y
    bring_cover = pltpu.make_async_copy(opacity, cover, sem_cover)
    bring_cover.start()
    bring = pltpu.make_async_copy(payload, held, sem_held)
    bring.start()

    def look(f, _):
        owner, slot = split(footprints[me, f], tiles)
        table[split(owner, n)[1] * tiles + slot] = f
        return 0

    lax.fori_loop(0, footprints.shape[1], look, 0, unroll=8)
    columns = [y ^ half ^ k for k in range(half)]
    send_fragments(plan, columns, table, payload, outs, sem)
    order = depth_order[...].astype(jnp.float32)
    order = jnp.concatenate(
        [order, jnp.zeros((tiles, plan.lanes - plan.depth), jnp.float32)], axis=1
    ).astype(jnp.bfloat16)
    bring_cover.wait()
    thin_part(plan, table, cover, order, thin)
    bring.wait()
    add_edges(plan, columns, table, held, cover, outs)
    await_fragments(plan, outs, sem)


def pack_kernel(plan, table, payload, opacity, out, sem):
    half = plan.half
    y = lax.axis_index("gy")
    base = y - (y & (half - 1))
    columns = [base + e for e in range(half)]
    outs = [out.at[e] for e in range(half)]
    send_fragments(plan, columns, table, payload, outs, sem)
    add_edges(plan, columns, table, payload, opacity, outs)
    await_fragments(plan, outs, sem)


def fold(x):
    return x.reshape(x.shape[0] * x.shape[1], x.shape[2])


def blend_kernel(plan, mirror, alpha_at, weight_at, own_in, prev_in, next_in, *rest):
    if mirror:
        *inbox, out_own, out_next, edge_over, edge_cross, alpha, weight, clear = rest
    else:
        *inbox, out_own, next_first, next_middle, out_next, alpha, weight, clear = rest
    n, tiles, across, sources = plan.count, plan.tiles, plan.across, plan.half
    rows, lanes = plan.rows, plan.lanes
    pair = 2 * rows
    frag_rows = plan.frag * rows
    halo_row = plan.at_halo * rows
    message = plan.groups * rows
    lane = iota((pair, lanes), 1)
    most = tiles - across

    def read(k, start, stop):
        ref, at = (inbox[k], 0) if mirror else (inbox[0], k * message)
        return ref[at + start : at + stop, :].astype(jnp.float32)

    for kind, ref in enumerate((own_in, prev_in, next_in)):
        for s in range(n):
            for t in range(tiles + 1):
                if kind and t < tiles and not across <= t < most:
                    continue
                row = (s * plan.thin_pair + mirror * plan.thin + t) * rows
                base = row // 16 * 16
                held = ref[base : base + 16, :].astype(jnp.float32)
                part = held[row - base : row - base + rows]
                alpha[(kind * n + s) * (tiles + 1) + t] = jnp.concatenate([part, part], axis=0)

    weight[...] = jnp.zeros_like(weight)

    def through(i, _):
        found = []
        for u in range(4):
            at = (4 * i + u) * plan.depth
            found.append([alpha[alpha_at[at + d]] for d in range(plan.depth)])
        ahead = []
        for u in range(4):
            seen = jnp.ones((pair, lanes), jnp.float32)
            for d in range(plan.depth):
                ahead.append((weight_at[(4 * i + u) * plan.depth + d], seen))
                seen = seen * (1.0 - found[u][d])
            found[u] = seen
        for at, seen in ahead:
            weight[at] = seen
        for u in range(4):
            clear[4 * i + u] = found[u]
        return 0

    lax.fori_loop(0, most, through, 0)

    step = 3 * pair
    while frag_rows % step or step % 16:
        step += pair
    shape = (step // pair, pair, lanes)
    def turned(x, by):
        return pltpu.roll(x, by % pair, 1)

    low_rows = iota(shape, 1) % rows < rows // 2
    for at in range(0, frag_rows, step):
        edges = {}
        for t in range(tiles):
            keeps, gives = t >= across, t < most
            total_own = jnp.zeros(shape, jnp.float32)
            total_next = jnp.zeros(shape, jnp.float32)
            for k in range(sources):
                start = t * frag_rows + at
                held = read(k, start, start + step).reshape(shape)
                if keeps:
                    total_own += weight[k * tiles + t][None] * held
                if gives:
                    total_next += weight[(2 * sources + k) * tiles + t][None] * held
            if at + step == frag_rows:
                mask = (iota(shape, 0) == step // pair - 1) & (iota(shape, 1) >= rows)
                cover = jnp.zeros((pair, lanes), jnp.float32)
                if keeps and not mirror:
                    cover = 1.0 - clear[t - across]
                total_own = jnp.where(mask, cover[None], total_own)
                cover = jnp.zeros((pair, lanes), jnp.float32)
                if t < across and not mirror:
                    cover = 1.0 - clear[most + t]
                total_next = jnp.where(mask, cover[None], total_next)

            def put(ref, slot, total):
                start = slot * frag_rows + at
                ref[start : start + step, :] = total.reshape(step, lanes).astype(ref.dtype)

            if t < across:
                edges[t] = total_next
            if t >= most:
                edges[t] = total_own
            if not mirror:
                if gives:
                    third = most // 2
                    put(next_first if t < third else next_middle, t % third, total_next)
                if keeps:
                    put(out_own, t - across, total_own)
            elif gives and keeps:
                put(out_next, t - across, total_next)
                put(out_own, t - across, total_own)
        first, last = edges[most], edges[tiles - 1]
        top = jnp.where(low_rows, turned(first, -(rows // 2)), last)
        if mirror:
            for c in range(across):
                put(edge_cross, c, edges[c])
                put(edge_over, 1 + c, edges[most + c])
            put(edge_cross, across, top)
            first, last = edges[0], edges[across - 1]
            put(edge_over, 0, jnp.where(low_rows, first, turned(last, rows // 2)))
        else:
            put(out_next, 0, top)

    halo_shape = (plan.halo_pad * rows // pair, pair, lanes)

    def merged(kind, source):
        out = jnp.zeros((pair, lanes), jnp.float32)
        first = across if kind == 0 else 0
        for u in range(most):
            out = jnp.where(lane // 2 == first + u, source(u, first + u), out)
        return out

    def widened(x):
        out = jnp.zeros((pair, lanes), jnp.float32)
        for b in range(plan.blocks):
            moved = pltpu.roll(x, SPAN * b, 1) if b else x
            out = jnp.where(lane // SPAN == b, moved, out)
        return out

    totals = [jnp.zeros(halo_shape, jnp.float32) for _ in range(2)]
    for k in range(sources):
        held = read(k, halo_row, halo_row + plan.halo_pad * rows).reshape(halo_shape)
        for kind in range(2):
            base = (2 * kind + 1) * sources * tiles + k * tiles
            by = widened(merged(kind, lambda u, v: weight[base + v]))
            totals[kind] += by[None] * held
    if not mirror:
        i_cov, b_cov = plan.channels // plan.blocks, plan.channels % plan.blocks
        group = iota(halo_shape, 0) * 2 + iota(halo_shape, 1) // rows
        at_cov = (group == i_cov) & (iota(halo_shape, 2) // SPAN == b_cov)
        for kind in range(2):
            cov = merged(kind, lambda u, v: 1.0 - clear[(2 + kind) * most + u])
            if kind == 1:
                cov = jnp.where(lane // 4 == 0, cov, 0.0)
            cov = pltpu.roll(cov, SPAN * b_cov, 1) if b_cov else cov
            totals[kind] = jnp.where(at_cov, cov[None], totals[kind])
    length = plan.halo_pad * rows

    def put_halo(ref, total):
        start = ref.shape[0] - length
        ref[start : start + length, :] = total.reshape(length, lanes).astype(ref.dtype)

    put_halo(out_own, totals[0])
    if mirror:
        put_halo(out_next, totals[1])
        put_halo(edge_over, totals[1])
        put_halo(edge_cross, totals[0])
    else:
        band = iota(halo_shape, 2) // 4 % TYD
        put_halo(out_next, jnp.where(band == TYD - 1, totals[0], totals[1]))


def conv_kernel(
    plan,
    feats,
    panel,
    own,
    kept,
    kept_halo,
    inner,
    edge_over,
    edge_cross,
    *rest,
):
    *got, one, top, low, two, keep, b1, b2, out, field, hidden = rest
    tiles, across, rows, lanes = plan.tiles, plan.across, plan.rows, plan.lanes
    frag_rows = plan.frag * rows
    most = tiles - across
    span = across * lanes
    wide = span + lanes
    x, y = lax.axis_index("gx"), lax.axis_index("gy")
    has_top, has_low = x, lax.axis_size("gx") - 1 - x
    has_left, has_right = y, lax.axis_size("gy") - 1 - y
    panels = panel[...]
    order = iota(panels.shape, 1)
    places = [jnp.sum(jnp.where(order == s, panels, 0)) for s in range(panels.shape[1])]

    def tile(ref, t, turn=0):
        part = ref[t * frag_rows : (t + 1) * frag_rows, :].astype(jnp.float32)
        if turn:
            part = part.reshape(-1, 2 * rows, lanes)
            part = pltpu.roll(part, turn % (2 * rows), 1).reshape(frag_rows, lanes)
        return part

    def shifted(t, turn=0):
        for ref in got:
            slots = ref.shape[0] // frag_rows
            if t < slots:
                return tile(ref, t, turn)
            t -= slots

    for c in range(across):
        at = slice(c * lanes, (c + 1) * lanes)
        last = c == across - 1
        turn = 0 if last else rows // 2
        value = shifted(most, turn) + tile(edge_cross, across, turn)
        value = jnp.where(has_top != 0, value, 0.0)
        field[0:frag_rows, at] = value.astype(jnp.bfloat16)
        for j in range(TYD):
            t = j * across + c
            if j == 0:
                value = shifted(t) + tile(edge_cross, c)
            elif j < TYD - 1:
                value = shifted(t) + tile(own, t - across) + tile(inner, t - across)
            else:
                value = tile(own, t - across) + tile(edge_over, 1 + c)
            field[(j + 1) * frag_rows : (j + 2) * frag_rows, at] = value.astype(jnp.bfloat16)
        at_low = (TYD + 1) * frag_rows
        value = tile(kept, c) + tile(edge_over, 0, -(rows // 2) if last else 0)
        value = jnp.where(has_low != 0, value, 0.0)
        field[at_low : at_low + frag_rows, at] = value.astype(jnp.bfloat16)

    length = plan.halo_pad * rows

    def edge(ref):
        at = ref.shape[0] - length
        return ref[at : at + length, :].astype(jnp.float32)

    h_got = edge(got[-1])
    band = iota((length, lanes), 1) // 4 % TYD
    h_all = edge(own) + edge(inner) + jnp.where(band == TYD - 1, 0.0, h_got)
    h_kept = edge(kept_halo) + edge(edge_over)
    h_got = h_got + edge(edge_cross)
    lane = iota((rows, lanes), 1)
    valid = ((lane < 2) & (has_right != 0)) | ((lane >= lanes - 2) & (has_left != 0))

    def unpacked(source, j):
        pieces = []
        for c in range(plan.frag):
            i, b = c // plan.blocks, c % plan.blocks
            piece = source[i * rows : (i + 1) * rows]
            shift = (-(SPAN * b + 4 * j + 2)) % lanes
            pieces.append(jnp.where(valid, pltpu.roll(piece, shift, 1), 0.0))
        return jnp.concatenate(pieces, axis=0).astype(jnp.bfloat16)

    wide_zero = jnp.zeros((frag_rows, lanes), jnp.bfloat16)
    at = slice(span, wide)
    field[0:frag_rows, at] = jnp.where(has_top != 0, unpacked(h_got, TYD - 1), wide_zero)
    for j in range(TYD):
        field[(j + 1) * frag_rows : (j + 2) * frag_rows, at] = unpacked(h_all, j)
    at_low = (TYD + 1) * frag_rows
    field[at_low : at_low + frag_rows, at] = jnp.where(has_low != 0, unpacked(h_kept, 0), wide_zero)

    def shifted_sum(y):
        part = y.shape[0] // 3
        return (
            pltpu.roll(y[:part], 1, 1)
            + y[part : 2 * part]
            + pltpu.roll(y[2 * part :], wide - 1, 1)
        )

    def act(y, bias):
        x = shifted_sum(y) + bias
        x = 0.5 * x
        return x + x * jnp.tanh(x)

    half = 2 * rows
    groups = TYD // 2
    col = iota((1, wide), 1)
    inside = ((col != span) | (has_right != 0)) & ((col != wide - 1) | (has_left != 0))

    def layer(weights, field, first, height, apart):
        spots = [slice(first + g * apart, first + g * apart + height) for g in range(groups)]
        sides = jnp.concatenate([field[at, span:wide] for at in spots], axis=1)
        sides = jnp.dot(weights[...], sides, preferred_element_type=jnp.float32)
        for g, at in enumerate(spots):
            plain = jnp.dot(weights[...], field[at, 0:span], preferred_element_type=jnp.float32)
            yield g, jnp.concatenate([plain, sides[:, g * lanes : (g + 1) * lanes]], axis=1)

    for g, y in layer(one, field, 0, 4 * frag_rows, 2 * frag_rows):
        h = jnp.where(inside, act(y, b1[...]), 0.0)
        at = feats + g * half * feats
        hidden[at : at + half * feats, :] = h.astype(jnp.bfloat16)
    for ref, at_field, at_hidden, has in (
        (top, 0, 0, has_top),
        (low, TYD * frag_rows, feats * (1 + groups * half), has_low),
    ):
        window = field[at_field : at_field + 2 * frag_rows, :]
        y = jnp.dot(ref[...], window, preferred_element_type=jnp.float32)
        h = jnp.where(inside & (has != 0), act(y, b1[0:feats]), 0.0)
        hidden[at_hidden : at_hidden + feats, :] = h.astype(jnp.bfloat16)
    strip = out.shape[1]
    for g, y in layer(two, hidden, 0, (half + 2) * feats, half * feats):
        plain = field[(2 * g + 1) * frag_rows : (2 * g + 3) * frag_rows, 0:span]
        base = jnp.dot(keep[...], plain, preferred_element_type=jnp.float32)
        total = (shifted_sum(y)[:, 0:span] + b2[...] + base).astype(jnp.bfloat16)
        for s in range(half * feats // strip):
            out[places[g * (half * feats // strip) + s]] = total[s * strip : (s + 1) * strip]


def display_kernel(span, shown, out, sem):
    for s in range(shown.shape[0]):
        pltpu.make_async_copy(shown.at[s], out.at[:, pl.ds(s * span, span)], sem).start()
    pltpu.make_async_copy(out, out, sem).wait()


def spread_kernel(plan, feats, outs, w1, w2, one, top, low, two, keep):
    rows, frag = plan.rows, plan.frag
    block = frag * rows
    part = 3 * feats

    def place(shape):
        channel = iota(shape, 0)
        column = iota(shape, 1)
        inner = column % block
        pixel = column // block * rows + inner % rows
        return jnp.where(inner // rows == channel, pixel, -1)

    def taps(weight, i):
        return weight[i * part : (i + 1) * part, :]

    def sums(weight, hit, first):
        total = 0.0
        for i in range(3):
            mask = (hit == first + i).astype(jnp.float32).astype(jnp.bfloat16)
            total = total + jnp.dot(taps(weight, i), mask, preferred_element_type=jnp.float32)
        return total.astype(jnp.bfloat16)

    hit = place((frag, one.shape[1]))
    for q in range(outs):
        rows_q = sums(w1, hit, q + rows - 1)
        for s in range(3):
            at = (s * outs + q) * feats
            one[at : at + feats, :] = rows_q[s * feats : (s + 1) * feats]
        if q == 0:
            low[...] = rows_q[:, : low.shape[1]]
    top[...] = sums(w1, place((frag, top.shape[1])), rows - 2)
    shape = (feats, two.shape[1])
    hit = jnp.where(iota(shape, 1) % feats == iota(shape, 0), iota(shape, 1) // feats, -1)
    for q in range(outs):
        rows_q = sums(w2, hit, q)
        for s in range(3):
            at = (s * outs + q) * feats
            two[at : at + feats, :] = rows_q[s * feats : (s + 1) * feats]
    shape = keep.shape
    inner = iota(shape, 1) % block
    pixel = iota(shape, 1) // block * rows + inner % rows
    same = (iota(shape, 0) // feats == pixel) & (iota(shape, 0) % feats == inner // rows)
    keep[...] = same.astype(jnp.float32).astype(jnp.bfloat16)


def shards(
    payload,
    opacity,
    depth_order,
    footprints,
    panel_map,
    conv1_weight,
    conv1_bias,
    conv2_weight,
    conv2_bias,
):
    row_groups = lax.axis_size("gx")
    n = lax.axis_size("gy")
    x = lax.axis_index("gx")
    y = lax.axis_index("gy")
    _, rows, channels, lanes = payload.shape
    tiles, depth = depth_order.shape
    plan = Plan(n, tiles, rows, channels, lanes, depth)
    feats = conv2_weight.shape[1]
    across = plan.across
    most = tiles - across

    half = n // 2
    spec_s = pl.BlockSpec(memory_space=pltpu.SMEM)
    spec_v = pl.BlockSpec(memory_space=pltpu.VMEM)
    spec_h = pl.BlockSpec(memory_space=pltpu.HBM)
    limit = pltpu.CompilerParams(vmem_limit_bytes=40 << 20)
    pixels = payload.transpose(0, 2, 1, 3)

    def cost(micros):
        return pl.CostEstimate(flops=0, bytes_accessed=int(micros * 3.6e6), transcendentals=0)

    message = jax.ShapeDtypeStruct((plan.groups, rows, lanes), payload.dtype)
    *packed, thin, table = pl.pallas_call(
        functools.partial(first_kernel, plan),
        out_shape=[message] * half
        + [
            jax.ShapeDtypeStruct((n, plan.thin_pair, rows, lanes), payload.dtype),
            jax.ShapeDtypeStruct((n * tiles,), jnp.int32),
        ],
        in_specs=[spec_s, spec_v, spec_h, spec_h],
        out_specs=[spec_v] * (half + 1) + [spec_s],
        scratch_shapes=[
            pltpu.VMEM(pixels.shape, payload.dtype),
            pltpu.VMEM(opacity.shape, payload.dtype),
            pltpu.SemaphoreType.DMA((half,)),
            pltpu.SemaphoreType.DMA,
            pltpu.SemaphoreType.DMA,
        ],
        compiler_params=pltpu.CompilerParams(vmem_limit_bytes=60 << 20),
        cost_estimate=cost(5),
        name="first",
    )(footprints, depth_order, pixels, opacity)
    inbox_mirror = [packed[0]] + [paired(packed[k], "gy", k) for k in range(1, half)]
    inbox_mirror = [block.reshape(-1, lanes) for block in inbox_mirror]

    thin = lax.all_to_all(thin, "gy", split_axis=0, concat_axis=0, tiled=True)
    thins = [thin, rotated(thin, "gx", 1), rotated(thin, "gx", -1)]

    near = [list(range(i, i + half)) for i in range(0, n, half)]
    inbox_own = pl.pallas_call(
        functools.partial(pack_kernel, plan),
        out_shape=jax.ShapeDtypeStruct((half, plan.groups, rows, lanes), payload.dtype),
        in_specs=[spec_s] + [spec_v] * 2,
        out_specs=spec_v,
        scratch_shapes=[pltpu.SemaphoreType.DMA((half,))],
        compiler_params=limit,
        cost_estimate=cost(4),
        name="pack",
    )(table, pixels, opacity)
    inbox_own = lax.all_to_all(
        inbox_own, "gy", split_axis=0, concat_axis=0, axis_index_groups=near, tiled=True
    )
    inbox_own = [inbox_own.reshape(-1, lanes)]

    def order_of(block):
        block = block[:, tiles + 1 : 2 * plan.thin : plan.thin]
        return block.astype(jnp.int32).reshape(n, 2 * rows, lanes)[:, :tiles, :depth]

    orders = [order_of(thins[0]), order_of(thins[2])]
    thins = [block.reshape(-1, lanes) for block in thins]

    def tables(order, kind, halo, mirror):
        slots = jnp.arange(order.shape[0], dtype=jnp.int32)[:, None] + (across if kind == 0 else 0)
        column = order % n
        local = order // n == x
        source = jnp.where(local, 0, 1 + kind) * n + column
        source = source * (tiles + 1) + (tiles if halo else slots)
        mine = local & (column // half == y // half)
        sender = (column ^ y) % half if mirror else column % half
        target = ((2 * kind + halo) * half + sender) * tiles + slots
        return source, jnp.where(mine, target, 4 * half * tiles)

    frag_rows = plan.frag * rows
    tail = plan.halo_pad * rows

    def blend(mirror, inbox):
        column = y ^ half if mirror else y

        def beside_of(order, step):
            return lax.dynamic_index_in_dim(order, (column + n + step) % n, 0, keepdims=False)

        here = [beside_of(order, 0) for order in orders]
        beside = [
            jnp.stack(
                [beside_of(order, -1)[across - 1 :: across], beside_of(order, 1)[0::across]], axis=1
            ).reshape(2 * TYD, depth)
            for order in orders
        ]
        pieces = [
            tables(here[0][across:], 0, 0, mirror),
            tables(here[1][:most], 1, 0, mirror),
            tables(beside[0][across:], 0, 1, mirror),
            tables(beside[1][:most], 1, 1, mirror),
        ]
        alpha_at = jnp.concatenate([a for a, _ in pieces]).reshape(-1)
        weight_at = jnp.concatenate([w for _, w in pieces]).reshape(-1)
        def sums(slots, dtype=payload.dtype):
            return jax.ShapeDtypeStruct((slots * frag_rows + tail, lanes), dtype)

        middle = most - across
        if mirror:
            made = [sums(middle, jnp.float32), sums(middle), sums(across + 1), sums(across + 1)]
        else:
            piece = jax.ShapeDtypeStruct((most // 2 * frag_rows, lanes), payload.dtype)
            made = [sums(most, jnp.float32), piece, piece, sums(1)]
        return pl.pallas_call(
            functools.partial(blend_kernel, plan, mirror),
            out_shape=made,
            in_specs=[spec_s] * 2 + [spec_v] * (3 + len(inbox)),
            out_specs=[spec_v] * len(made),
            scratch_shapes=[
                pltpu.VMEM((3 * n * (tiles + 1), 2 * rows, lanes), jnp.float32),
                pltpu.VMEM((4 * half * tiles + 1, 2 * rows, lanes), jnp.float32),
                pltpu.VMEM((4 * most, 2 * rows, lanes), jnp.float32),
            ],
            compiler_params=limit,
            cost_estimate=cost(3),
            name="blend_mirror" if mirror else "blend_own",
        )(alpha_at, weight_at, *thins, *inbox)

    inner, inner_next, edge_over, edge_cross = blend(1, inbox_mirror)
    edge_over = paired(edge_over, "gy", half)
    route = [
        (i * n + j, (i + 1) % row_groups * n + (j ^ half))
        for i in range(row_groups)
        for j in range(n)
    ]
    edge_cross = lax.ppermute(edge_cross, ("gx", "gy"), route)
    inner_next = rotated(inner_next, "gx", 1)
    inner = (inner + inner_next.astype(jnp.float32)).astype(payload.dtype)
    inner, thins[0] = lax.optimization_barrier((inner, thins[0]))
    inner = paired(inner, "gy", half)
    own, *kept = blend(0, inbox_own)
    got = [rotated(piece, "gx", 1) for piece in kept]

    band_half = 2 * rows
    w1, w2, _ = lax.optimization_barrier((conv1_weight, conv2_weight, table))
    w1 = w1.reshape(-1, w1.shape[2])
    w2 = w2.reshape(-1, w2.shape[2])

    def matrix(height, width):
        return jax.ShapeDtypeStruct((height, width), payload.dtype)

    one, top, low, two, keep = pl.pallas_call(
        functools.partial(spread_kernel, plan, feats, band_half),
        out_shape=[
            matrix(3 * band_half * feats, 4 * frag_rows),
            matrix(3 * feats, 2 * frag_rows),
            matrix(3 * feats, 2 * frag_rows),
            matrix(3 * band_half * feats, (band_half + 2) * feats),
            matrix(band_half * feats, 2 * frag_rows),
        ],
        in_specs=[spec_v] * 2,
        out_specs=[spec_v] * 5,
        compiler_params=limit,
        cost_estimate=cost(4),
        name="spread",
    )(w1, w2)
    b1 = jnp.tile(conv1_bias, band_half)[:, None]
    b2 = jnp.tile(conv2_bias, band_half)[:, None]
    band = TYD * rows
    strip = band // n
    span = across * lanes
    pieces = pl.pallas_call(
        functools.partial(conv_kernel, plan, feats),
        out_shape=jax.ShapeDtypeStruct((n, strip * feats, span), jnp.bfloat16),
        in_specs=[spec_v] * (14 + len(got)),
        out_specs=spec_v,
        scratch_shapes=[
            pltpu.VMEM(((TYD + 2) * frag_rows, span + lanes), jnp.bfloat16),
            pltpu.VMEM(((band + 2) * feats, span + lanes), jnp.bfloat16),
        ],
        compiler_params=limit,
        cost_estimate=cost(4),
        name="conv",
    )(panel_map[None], own, kept[0], kept[2], inner, edge_over, edge_cross, *got, one, top, low, two, keep, b1, b2)
    shown = lax.all_to_all(pieces, "gy", split_axis=0, concat_axis=0, tiled=True)
    shown = pl.pallas_call(
        functools.partial(display_kernel, span),
        out_shape=jax.ShapeDtypeStruct((strip * feats, n * span), payload.dtype),
        in_specs=[spec_v],
        out_specs=spec_h,
        scratch_shapes=[pltpu.SemaphoreType.DMA],
        compiler_params=limit,
        name="display",
    )(shown)
    return shown.reshape(1, 1, strip, feats, n * span)


def solution(mesh):
    return jax.shard_map(
        shards,
        mesh=mesh,
        in_specs=(
            P(("gx", "gy"), None, None, None),
            P(("gx", "gy"), None, None),
            P(("gx", "gy"), None),
            P(),
            P(),
            P(),
            P(),
            P(),
            P(),
        ),
        out_specs=P("gx", "gy", None, None, None),
        check_vma=False,
    )
```

```python
import functools

import jax
import jax.numpy as jnp
from jax import lax
from jax.experimental import pallas as pl
from jax.experimental.pallas import tpu as pltpu
from jax.sharding import PartitionSpec as P

TYD = 4
SPAN = 4 * TYD


def rotated(block, axis, distance):
    count = lax.axis_size(axis)
    return lax.ppermute(block, axis, [(i, (i + distance) % count) for i in range(count)])


def paired(block, axis, step):
    return lax.ppermute(block, axis, [(i, i ^ step) for i in range(lax.axis_size(axis))])


def split(value, size):
    if size & (size - 1) == 0:
        return value >> (size.bit_length() - 1), value & (size - 1)
    return lax.div(value, size), lax.rem(value, size)


def iota(shape, dim):
    return lax.broadcasted_iota(jnp.int32, shape, dim)


class Plan:
    def __init__(self, count, tiles, rows, channels, lanes, depth):
        self.count = count
        self.half = count // 2
        self.tiles = tiles
        self.across = tiles // TYD
        self.rows = rows
        self.channels = channels
        self.lanes = lanes
        self.depth = depth
        self.frag = channels + 1
        self.blocks = lanes // SPAN
        self.halo = -(-self.frag // self.blocks)
        self.at_halo = tiles * self.frag
        per = 16 // rows
        self.groups = -(-(self.at_halo + self.halo) // per) * per
        self.halo_pad = self.groups - self.at_halo
        self.thin = -(-(tiles + 2) // 2) * 2
        self.thin_pair = -(-2 * self.thin // per) * per


def neighbours(plan, column):
    n, tiles = plan.count, plan.tiles
    right = jnp.where(column == n - 1, 0, column + 1) * tiles
    left = jnp.where(column == 0, n - 1, column - 1) * tiles + plan.across - 1
    return right, left


def joined(right, left, j, lane, axis):
    both = jnp.where(lane < 2, right.astype(jnp.float32), left.astype(jnp.float32))
    return pltpu.roll(both, 4 * j + 2, axis)


def thin_part(plan, table, opacity, order, out):
    n, tiles = plan.count, plan.tiles
    lane = iota((plan.rows, plan.lanes), 1)
    empty = jnp.zeros((plan.rows, plan.lanes), jnp.bfloat16)
    for d in range(n):
        places = [(d, 0), (d ^ plan.half, plan.thin)]
        for t in range(tiles):
            group = opacity[table[d * tiles + t]]
            for to, at in places:
                out[to, at + t] = group
        right = (d + 1) % n * tiles
        left = (d - 1) % n * tiles + plan.across - 1
        halo = jnp.zeros((plan.rows, plan.lanes), jnp.float32)
        for j in range(TYD):
            f_r, f_l = table[right + j * plan.across], table[left + j * plan.across]
            inside = (lane >= 4 * j) & (lane < 4 * j + 4)
            halo = jnp.where(inside, joined(opacity[f_r], opacity[f_l], j, lane, 1), halo)
        for to, at in places:
            out[to, at + tiles] = halo.astype(jnp.bfloat16)
        for i in range(2):
            out[d, i * plan.thin + tiles + 1] = order[i * plan.rows : (i + 1) * plan.rows]
            for g in range(tiles + 2, plan.thin):
                out[d, i * plan.thin + g] = empty
        for g in range(2 * plan.thin, plan.thin_pair):
            out[d, g] = empty


def send_fragments(plan, columns, table, payload, outs, sem):
    for e, column in enumerate(columns):

        def move(t, _, e=e, column=column):
            f = table[column * plan.tiles + t]
            pltpu.make_async_copy(
                payload.at[f], outs[e].at[pl.ds(t * plan.frag, plan.channels)], sem.at[e]
            ).start()
            return 0

        lax.fori_loop(0, plan.tiles, move, 0)


def add_edges(plan, columns, table, payload, opacity, outs):
    across = plan.across
    lane = iota((plan.channels, plan.rows, plan.lanes), 2)
    lane_one = iota((plan.rows, plan.lanes), 1)
    for out, column in zip(outs, columns):
        for t in range(plan.tiles):
            out[t * plan.frag + plan.channels] = opacity[table[column * plan.tiles + t]]
        right, left = neighbours(plan, column)
        spread = jnp.zeros((plan.channels, plan.rows, plan.lanes), jnp.float32)
        for j in range(TYD):
            f_r, f_l = table[right + j * across], table[left + j * across]
            inside = (lane >= 4 * j) & (lane < 4 * j + 4)
            spread = jnp.where(inside, joined(payload[f_r], payload[f_l], j, lane, 2), spread)
        for i in range(plan.halo_pad):
            group = jnp.zeros((plan.rows, plan.lanes), jnp.float32)
            for b in range(plan.blocks):
                c = i * plan.blocks + b
                if c < plan.channels:
                    moved = pltpu.roll(spread[c], SPAN * b, 1) if b else spread[c]
                    group = jnp.where(
                        (lane_one >= SPAN * b) & (lane_one < SPAN * b + SPAN), moved, group
                    )
            out[plan.at_halo + i] = group.astype(jnp.bfloat16)


def await_fragments(plan, outs, sem):
    for e, out in enumerate(outs):
        whole = out.at[pl.ds(0, plan.tiles * plan.channels)]
        pltpu.make_async_copy(whole, whole, sem.at[e]).wait()


def first_kernel(plan, footprints, depth_order, payload, opacity, *rest):
    n, tiles, half = plan.count, plan.tiles, plan.half
    outs = rest[:half]
    thin, table, held, cover, sem, sem_held, sem_cover = rest[half:]
    x, y = lax.axis_index("gx"), lax.axis_index("gy")
    me = x * n + y
    bring_cover = pltpu.make_async_copy(opacity, cover, sem_cover)
    bring_cover.start()
    bring = pltpu.make_async_copy(payload, held, sem_held)
    bring.start()

    def look(f, _):
        owner, slot = split(footprints[me, f], tiles)
        table[split(owner, n)[1] * tiles + slot] = f
        return 0

    lax.fori_loop(0, footprints.shape[1], look, 0, unroll=8)
    columns = [y ^ half ^ k for k in range(half)]
    send_fragments(plan, columns, table, payload, outs, sem)
    order = depth_order[...].astype(jnp.float32)
    order = jnp.concatenate(
        [order, jnp.zeros((tiles, plan.lanes - plan.depth), jnp.float32)], axis=1
    ).astype(jnp.bfloat16)
    bring_cover.wait()
    thin_part(plan, table, cover, order, thin)
    bring.wait()
    add_edges(plan, columns, table, held, cover, outs)
    await_fragments(plan, outs, sem)


def pack_kernel(plan, table, payload, opacity, out, sem):
    half = plan.half
    y = lax.axis_index("gy")
    base = y - (y & (half - 1))
    columns = [base + e for e in range(half)]
    outs = [out.at[e] for e in range(half)]
    send_fragments(plan, columns, table, payload, outs, sem)
    add_edges(plan, columns, table, payload, opacity, outs)
    await_fragments(plan, outs, sem)


def fold(x):
    return x.reshape(x.shape[0] * x.shape[1], x.shape[2])


def blend_kernel(plan, mirror, alpha_at, weight_at, own_in, prev_in, next_in, *rest):
    if mirror:
        *inbox, out_own, out_next, edge_over, edge_cross, alpha, weight, clear = rest
    else:
        *inbox, out_own, next_first, next_middle, out_next, alpha, weight, clear = rest
    n, tiles, across, sources = plan.count, plan.tiles, plan.across, plan.half
    rows, lanes = plan.rows, plan.lanes
    pair = 2 * rows
    frag_rows = plan.frag * rows
    halo_row = plan.at_halo * rows
    message = plan.groups * rows
    lane = iota((pair, lanes), 1)
    most = tiles - across

    def read(k, start, stop):
        ref, at = (inbox[k], 0) if mirror else (inbox[0], k * message)
        return ref[at + start : at + stop, :].astype(jnp.float32)

    for kind, ref in enumerate((own_in, prev_in, next_in)):
        for s in range(n):
            for t in range(tiles + 1):
                if kind and t < tiles and not across <= t < most:
                    continue
                row = (s * plan.thin_pair + mirror * plan.thin + t) * rows
                base = row // 16 * 16
                held = ref[base : base + 16, :].astype(jnp.float32)
                part = held[row - base : row - base + rows]
                alpha[(kind * n + s) * (tiles + 1) + t] = jnp.concatenate([part, part], axis=0)

    weight[...] = jnp.zeros_like(weight)

    def through(i, _):
        found = []
        for u in range(4):
            at = (4 * i + u) * plan.depth
            found.append([alpha[alpha_at[at + d]] for d in range(plan.depth)])
        ahead = []
        for u in range(4):
            seen = jnp.ones((pair, lanes), jnp.float32)
            for d in range(plan.depth):
                ahead.append((weight_at[(4 * i + u) * plan.depth + d], seen))
                seen = seen * (1.0 - found[u][d])
            found[u] = seen
        for at, seen in ahead:
            weight[at] = seen
        for u in range(4):
            clear[4 * i + u] = found[u]
        return 0

    lax.fori_loop(0, most, through, 0)

    step = 3 * pair
    while frag_rows % step or step % 16:
        step += pair
    shape = (step // pair, pair, lanes)
    def turned(x, by):
        return pltpu.roll(x, by % pair, 1)

    low_rows = iota(shape, 1) % rows < rows // 2
    for at in range(0, frag_rows, step):
        edges = {}
        for t in range(tiles):
            keeps, gives = t >= across, t < most
            total_own = jnp.zeros(shape, jnp.float32)
            total_next = jnp.zeros(shape, jnp.float32)
            for k in range(sources):
                start = t * frag_rows + at
                held = read(k, start, start + step).reshape(shape)
                if keeps:
                    total_own += weight[k * tiles + t][None] * held
                if gives:
                    total_next += weight[(2 * sources + k) * tiles + t][None] * held
            if at + step == frag_rows:
                mask = (iota(shape, 0) == step // pair - 1) & (iota(shape, 1) >= rows)
                cover = jnp.zeros((pair, lanes), jnp.float32)
                if keeps and not mirror:
                    cover = 1.0 - clear[t - across]
                total_own = jnp.where(mask, cover[None], total_own)
                cover = jnp.zeros((pair, lanes), jnp.float32)
                if t < across and not mirror:
                    cover = 1.0 - clear[most + t]
                total_next = jnp.where(mask, cover[None], total_next)

            def put(ref, slot, total):
                start = slot * frag_rows + at
                ref[start : start + step, :] = total.reshape(step, lanes).astype(ref.dtype)

            if t < across:
                edges[t] = total_next
            if t >= most:
                edges[t] = total_own
            if not mirror:
                if gives:
                    third = most // 2
                    put(next_first if t < third else next_middle, t % third, total_next)
                if keeps:
                    put(out_own, t - across, total_own)
            elif gives and keeps:
                put(out_next, t - across, total_next)
                put(out_own, t - across, total_own)
        first, last = edges[most], edges[tiles - 1]
        top = jnp.where(low_rows, turned(first, -(rows // 2)), last)
        if mirror:
            for c in range(across):
                put(edge_cross, c, edges[c])
                put(edge_over, 1 + c, edges[most + c])
            put(edge_cross, across, top)
            first, last = edges[0], edges[across - 1]
            put(edge_over, 0, jnp.where(low_rows, first, turned(last, rows // 2)))
        else:
            put(out_next, 0, top)

    halo_shape = (plan.halo_pad * rows // pair, pair, lanes)

    def merged(kind, source):
        out = jnp.zeros((pair, lanes), jnp.float32)
        first = across if kind == 0 else 0
        for u in range(most):
            out = jnp.where(lane // 2 == first + u, source(u, first + u), out)
        return out

    def widened(x):
        out = jnp.zeros((pair, lanes), jnp.float32)
        for b in range(plan.blocks):
            moved = pltpu.roll(x, SPAN * b, 1) if b else x
            out = jnp.where(lane // SPAN == b, moved, out)
        return out

    totals = [jnp.zeros(halo_shape, jnp.float32) for _ in range(2)]
    for k in range(sources):
        held = read(k, halo_row, halo_row + plan.halo_pad * rows).reshape(halo_shape)
        for kind in range(2):
            base = (2 * kind + 1) * sources * tiles + k * tiles
            by = widened(merged(kind, lambda u, v: weight[base + v]))
            totals[kind] += by[None] * held
    if not mirror:
        i_cov, b_cov = plan.channels // plan.blocks, plan.channels % plan.blocks
        group = iota(halo_shape, 0) * 2 + iota(halo_shape, 1) // rows
        at_cov = (group == i_cov) & (iota(halo_shape, 2) // SPAN == b_cov)
        for kind in range(2):
            cov = merged(kind, lambda u, v: 1.0 - clear[(2 + kind) * most + u])
            if kind == 1:
                cov = jnp.where(lane // 4 == 0, cov, 0.0)
            cov = pltpu.roll(cov, SPAN * b_cov, 1) if b_cov else cov
            totals[kind] = jnp.where(at_cov, cov[None], totals[kind])
    length = plan.halo_pad * rows

    def put_halo(ref, total):
        start = ref.shape[0] - length
        ref[start : start + length, :] = total.reshape(length, lanes).astype(ref.dtype)

    put_halo(out_own, totals[0])
    if mirror:
        put_halo(out_next, totals[1])
        put_halo(edge_over, totals[1])
        put_halo(edge_cross, totals[0])
    else:
        band = iota(halo_shape, 2) // 4 % TYD
        put_halo(out_next, jnp.where(band == TYD - 1, totals[0], totals[1]))


def conv_kernel(
    plan,
    feats,
    panel,
    own,
    kept,
    kept_halo,
    inner,
    edge_over,
    edge_cross,
    *rest,
):
    *got, one, top, low, two, keep, b1, b2, out, field, hidden = rest
    tiles, across, rows, lanes = plan.tiles, plan.across, plan.rows, plan.lanes
    frag_rows = plan.frag * rows
    most = tiles - across
    span = across * lanes
    wide = span + lanes
    x, y = lax.axis_index("gx"), lax.axis_index("gy")
    has_top, has_low = x, lax.axis_size("gx") - 1 - x
    has_left, has_right = y, lax.axis_size("gy") - 1 - y
    panels = panel[...]
    order = iota(panels.shape, 1)
    places = [jnp.sum(jnp.where(order == s, panels, 0)) for s in range(panels.shape[1])]

    def tile(ref, t, turn=0):
        part = ref[t * frag_rows : (t + 1) * frag_rows, :].astype(jnp.float32)
        if turn:
            part = part.reshape(-1, 2 * rows, lanes)
            part = pltpu.roll(part, turn % (2 * rows), 1).reshape(frag_rows, lanes)
        return part

    def shifted(t, turn=0):
        for ref in got:
            slots = ref.shape[0] // frag_rows
            if t < slots:
                return tile(ref, t, turn)
            t -= slots

    for c in range(across):
        at = slice(c * lanes, (c + 1) * lanes)
        last = c == across - 1
        turn = 0 if last else rows // 2
        value = shifted(most, turn) + tile(edge_cross, across, turn)
        value = jnp.where(has_top != 0, value, 0.0)
        field[0:frag_rows, at] = value.astype(jnp.bfloat16)
        for j in range(TYD):
            t = j * across + c
            if j == 0:
                value = shifted(t) + tile(edge_cross, c)
            elif j < TYD - 1:
                value = shifted(t) + tile(own, t - across) + tile(inner, t - across)
            else:
                value = tile(own, t - across) + tile(edge_over, 1 + c)
            field[(j + 1) * frag_rows : (j + 2) * frag_rows, at] = value.astype(jnp.bfloat16)
        at_low = (TYD + 1) * frag_rows
        value = tile(kept, c) + tile(edge_over, 0, -(rows // 2) if last else 0)
        value = jnp.where(has_low != 0, value, 0.0)
        field[at_low : at_low + frag_rows, at] = value.astype(jnp.bfloat16)

    length = plan.halo_pad * rows

    def edge(ref):
        at = ref.shape[0] - length
        return ref[at : at + length, :].astype(jnp.float32)

    h_got = edge(got[-1])
    band = iota((length, lanes), 1) // 4 % TYD
    h_all = edge(own) + edge(inner) + jnp.where(band == TYD - 1, 0.0, h_got)
    h_kept = edge(kept_halo) + edge(edge_over)
    h_got = h_got + edge(edge_cross)
    lane = iota((rows, lanes), 1)
    valid = ((lane < 2) & (has_right != 0)) | ((lane >= lanes - 2) & (has_left != 0))

    def unpacked(source, j):
        pieces = []
        for c in range(plan.frag):
            i, b = c // plan.blocks, c % plan.blocks
            piece = source[i * rows : (i + 1) * rows]
            shift = (-(SPAN * b + 4 * j + 2)) % lanes
            pieces.append(jnp.where(valid, pltpu.roll(piece, shift, 1), 0.0))
        return jnp.concatenate(pieces, axis=0).astype(jnp.bfloat16)

    wide_zero = jnp.zeros((frag_rows, lanes), jnp.bfloat16)
    at = slice(span, wide)
    field[0:frag_rows, at] = jnp.where(has_top != 0, unpacked(h_got, TYD - 1), wide_zero)
    for j in range(TYD):
        field[(j + 1) * frag_rows : (j + 2) * frag_rows, at] = unpacked(h_all, j)
    at_low = (TYD + 1) * frag_rows
    field[at_low : at_low + frag_rows, at] = jnp.where(has_low != 0, unpacked(h_kept, 0), wide_zero)

    def shifted_sum(y):
        part = y.shape[0] // 3
        return (
            pltpu.roll(y[:part], 1, 1)
            + y[part : 2 * part]
            + pltpu.roll(y[2 * part :], wide - 1, 1)
        )

    def act(y, bias):
        x = shifted_sum(y) + bias
        x = 0.5 * x
        return x + x * jnp.tanh(x)

    half = 2 * rows
    groups = TYD // 2
    col = iota((1, wide), 1)
    inside = ((col != span) | (has_right != 0)) & ((col != wide - 1) | (has_left != 0))

    def layer(weights, field, first, height, apart):
        spots = [slice(first + g * apart, first + g * apart + height) for g in range(groups)]
        sides = jnp.concatenate([field[at, span:wide] for at in spots], axis=1)
        sides = jnp.dot(weights[...], sides, preferred_element_type=jnp.float32)
        for g, at in enumerate(spots):
            plain = jnp.dot(weights[...], field[at, 0:span], preferred_element_type=jnp.float32)
            yield g, jnp.concatenate([plain, sides[:, g * lanes : (g + 1) * lanes]], axis=1)

    for g, y in layer(one, field, 0, 4 * frag_rows, 2 * frag_rows):
        h = jnp.where(inside, act(y, b1[...]), 0.0)
        at = feats + g * half * feats
        hidden[at : at + half * feats, :] = h.astype(jnp.bfloat16)
    for ref, at_field, at_hidden, has in (
        (top, 0, 0, has_top),
        (low, TYD * frag_rows, feats * (1 + groups * half), has_low),
    ):
        window = field[at_field : at_field + 2 * frag_rows, :]
        y = jnp.dot(ref[...], window, preferred_element_type=jnp.float32)
        h = jnp.where(inside & (has != 0), act(y, b1[0:feats]), 0.0)
        hidden[at_hidden : at_hidden + feats, :] = h.astype(jnp.bfloat16)
    strip = out.shape[1]
    for g, y in layer(two, hidden, 0, (half + 2) * feats, half * feats):
        plain = field[(2 * g + 1) * frag_rows : (2 * g + 3) * frag_rows, 0:span]
        base = jnp.dot(keep[...], plain, preferred_element_type=jnp.float32)
        total = (shifted_sum(y)[:, 0:span] + b2[...] + base).astype(jnp.bfloat16)
        for s in range(half * feats // strip):
            out[places[g * (half * feats // strip) + s]] = total[s * strip : (s + 1) * strip]


def display_kernel(span, shown, out, sem):
    for s in range(shown.shape[0]):
        pltpu.make_async_copy(shown.at[s], out.at[:, pl.ds(s * span, span)], sem).start()
    pltpu.make_async_copy(out, out, sem).wait()


def spread_kernel(plan, feats, outs, w1, w2, one, top, low, two, keep):
    rows, frag = plan.rows, plan.frag
    block = frag * rows
    part = 3 * feats

    def place(shape):
        channel = iota(shape, 0)
        column = iota(shape, 1)
        inner = column % block
        pixel = column // block * rows + inner % rows
        return jnp.where(inner // rows == channel, pixel, -1)

    def taps(weight, i):
        return weight[i * part : (i + 1) * part, :]

    def sums(weight, hit, first):
        total = 0.0
        for i in range(3):
            mask = (hit == first + i).astype(jnp.float32).astype(jnp.bfloat16)
            total = total + jnp.dot(taps(weight, i), mask, preferred_element_type=jnp.float32)
        return total.astype(jnp.bfloat16)

    hit = place((frag, one.shape[1]))
    for q in range(outs):
        rows_q = sums(w1, hit, q + rows - 1)
        for s in range(3):
            at = (s * outs + q) * feats
            one[at : at + feats, :] = rows_q[s * feats : (s + 1) * feats]
        if q == 0:
            low[...] = rows_q[:, : low.shape[1]]
    top[...] = sums(w1, place((frag, top.shape[1])), rows - 2)
    shape = (feats, two.shape[1])
    hit = jnp.where(iota(shape, 1) % feats == iota(shape, 0), iota(shape, 1) // feats, -1)
    for q in range(outs):
        rows_q = sums(w2, hit, q)
        for s in range(3):
            at = (s * outs + q) * feats
            two[at : at + feats, :] = rows_q[s * feats : (s + 1) * feats]
    shape = keep.shape
    inner = iota(shape, 1) % block
    pixel = iota(shape, 1) // block * rows + inner % rows
    same = (iota(shape, 0) // feats == pixel) & (iota(shape, 0) % feats == inner // rows)
    keep[...] = same.astype(jnp.float32).astype(jnp.bfloat16)


def shards(
    payload,
    opacity,
    depth_order,
    footprints,
    panel_map,
    conv1_weight,
    conv1_bias,
    conv2_weight,
    conv2_bias,
):
    row_groups = lax.axis_size("gx")
    n = lax.axis_size("gy")
    x = lax.axis_index("gx")
    y = lax.axis_index("gy")
    _, rows, channels, lanes = payload.shape
    tiles, depth = depth_order.shape
    plan = Plan(n, tiles, rows, channels, lanes, depth)
    feats = conv2_weight.shape[1]
    across = plan.across
    most = tiles - across

    half = n // 2
    spec_s = pl.BlockSpec(memory_space=pltpu.SMEM)
    spec_v = pl.BlockSpec(memory_space=pltpu.VMEM)
    spec_h = pl.BlockSpec(memory_space=pltpu.HBM)
    limit = pltpu.CompilerParams(vmem_limit_bytes=40 << 20)
    pixels = payload.transpose(0, 2, 1, 3)

    def cost(micros):
        return pl.CostEstimate(flops=0, bytes_accessed=int(micros * 3.6e6), transcendentals=0)

    message = jax.ShapeDtypeStruct((plan.groups, rows, lanes), payload.dtype)
    *packed, thin, table = pl.pallas_call(
        functools.partial(first_kernel, plan),
        out_shape=[message] * half
        + [
            jax.ShapeDtypeStruct((n, plan.thin_pair, rows, lanes), payload.dtype),
            jax.ShapeDtypeStruct((n * tiles,), jnp.int32),
        ],
        in_specs=[spec_s, spec_v, spec_h, spec_h],
        out_specs=[spec_v] * (half + 1) + [spec_s],
        scratch_shapes=[
            pltpu.VMEM(pixels.shape, payload.dtype),
            pltpu.VMEM(opacity.shape, payload.dtype),
            pltpu.SemaphoreType.DMA((half,)),
            pltpu.SemaphoreType.DMA,
            pltpu.SemaphoreType.DMA,
        ],
        compiler_params=pltpu.CompilerParams(vmem_limit_bytes=60 << 20),
        cost_estimate=cost(5),
        name="first",
    )(footprints, depth_order, pixels, opacity)
    inbox_mirror = [paired(packed[k], "gy", k) for k in range(half - 1, 0, -1)]
    inbox_mirror = inbox_mirror + [packed[0]]
    inbox_mirror = [block.reshape(-1, lanes) for block in inbox_mirror]

    thin = lax.all_to_all(thin, "gy", split_axis=0, concat_axis=0, tiled=True)
    thins = [thin, rotated(thin, "gx", 1), rotated(thin, "gx", -1)]

    near = [list(range(i, i + half)) for i in range(0, n, half)]
    inbox_own = pl.pallas_call(
        functools.partial(pack_kernel, plan),
        out_shape=jax.ShapeDtypeStruct((half, plan.groups, rows, lanes), payload.dtype),
        in_specs=[spec_s] + [spec_v] * 2,
        out_specs=spec_v,
        scratch_shapes=[pltpu.SemaphoreType.DMA((half,))],
        compiler_params=limit,
        cost_estimate=cost(4),
        name="pack",
    )(table, pixels, opacity)
    inbox_own = lax.all_to_all(
        inbox_own, "gy", split_axis=0, concat_axis=0, axis_index_groups=near, tiled=True
    )
    inbox_own = [inbox_own.reshape(-1, lanes)]

    def order_of(block):
        block = block[:, tiles + 1 : 2 * plan.thin : plan.thin]
        return block.astype(jnp.int32).reshape(n, 2 * rows, lanes)[:, :tiles, :depth]

    orders = [order_of(thins[0]), order_of(thins[2])]
    thins = [block.reshape(-1, lanes) for block in thins]

    def tables(order, kind, halo, mirror):
        slots = jnp.arange(order.shape[0], dtype=jnp.int32)[:, None] + (across if kind == 0 else 0)
        column = order % n
        local = order // n == x
        source = jnp.where(local, 0, 1 + kind) * n + column
        source = source * (tiles + 1) + (tiles if halo else slots)
        mine = local & (column // half == y // half)
        sender = half - 1 - (column ^ y) % half if mirror else column % half
        target = ((2 * kind + halo) * half + sender) * tiles + slots
        return source, jnp.where(mine, target, 4 * half * tiles)

    frag_rows = plan.frag * rows
    tail = plan.halo_pad * rows

    def blend(mirror, inbox):
        column = y ^ half if mirror else y

        def beside_of(order, step):
            return lax.dynamic_index_in_dim(order, (column + n + step) % n, 0, keepdims=False)

        here = [beside_of(order, 0) for order in orders]
        beside = [
            jnp.stack(
                [beside_of(order, -1)[across - 1 :: across], beside_of(order, 1)[0::across]], axis=1
            ).reshape(2 * TYD, depth)
            for order in orders
        ]
        pieces = [
            tables(here[0][across:], 0, 0, mirror),
            tables(here[1][:most], 1, 0, mirror),
            tables(beside[0][across:], 0, 1, mirror),
            tables(beside[1][:most], 1, 1, mirror),
        ]
        alpha_at = jnp.concatenate([a for a, _ in pieces]).reshape(-1)
        weight_at = jnp.concatenate([w for _, w in pieces]).reshape(-1)
        def sums(slots, dtype=payload.dtype):
            return jax.ShapeDtypeStruct((slots * frag_rows + tail, lanes), dtype)

        middle = most - across
        if mirror:
            made = [sums(middle, jnp.float32), sums(middle), sums(across + 1), sums(across + 1)]
        else:
            piece = jax.ShapeDtypeStruct((most // 2 * frag_rows, lanes), payload.dtype)
            made = [sums(most, jnp.float32), piece, piece, sums(1)]
        return pl.pallas_call(
            functools.partial(blend_kernel, plan, mirror),
            out_shape=made,
            in_specs=[spec_s] * 2 + [spec_v] * (3 + len(inbox)),
            out_specs=[spec_v] * len(made),
            scratch_shapes=[
                pltpu.VMEM((3 * n * (tiles + 1), 2 * rows, lanes), jnp.float32),
                pltpu.VMEM((4 * half * tiles + 1, 2 * rows, lanes), jnp.float32),
                pltpu.VMEM((4 * most, 2 * rows, lanes), jnp.float32),
            ],
            compiler_params=limit,
            cost_estimate=cost(3),
            name="blend_mirror" if mirror else "blend_own",
        )(alpha_at, weight_at, *thins, *inbox)

    inner, inner_next, edge_over, edge_cross = blend(1, inbox_mirror)
    edge_over = paired(edge_over, "gy", half)
    route = [
        (i * n + j, (i + 1) % row_groups * n + (j ^ half))
        for i in range(row_groups)
        for j in range(n)
    ]
    edge_cross = lax.ppermute(edge_cross, ("gx", "gy"), route)
    inner_next = rotated(inner_next, "gx", 1)
    inner = (inner + inner_next.astype(jnp.float32)).astype(payload.dtype)
    inner, thins[0] = lax.optimization_barrier((inner, thins[0]))
    inner = paired(inner, "gy", half)
    own, *kept = blend(0, inbox_own)
    got = [rotated(piece, "gx", 1) for piece in kept]

    band_half = 2 * rows
    w1, w2, _ = lax.optimization_barrier((conv1_weight, conv2_weight, table))
    w1 = w1.reshape(-1, w1.shape[2])
    w2 = w2.reshape(-1, w2.shape[2])

    def matrix(height, width):
        return jax.ShapeDtypeStruct((height, width), payload.dtype)

    one, top, low, two, keep = pl.pallas_call(
        functools.partial(spread_kernel, plan, feats, band_half),
        out_shape=[
            matrix(3 * band_half * feats, 4 * frag_rows),
            matrix(3 * feats, 2 * frag_rows),
            matrix(3 * feats, 2 * frag_rows),
            matrix(3 * band_half * feats, (band_half + 2) * feats),
            matrix(band_half * feats, 2 * frag_rows),
        ],
        in_specs=[spec_v] * 2,
        out_specs=[spec_v] * 5,
        compiler_params=limit,
        cost_estimate=cost(4),
        name="spread",
    )(w1, w2)
    b1 = jnp.tile(conv1_bias, band_half)[:, None]
    b2 = jnp.tile(conv2_bias, band_half)[:, None]
    band = TYD * rows
    strip = band // n
    span = across * lanes
    pieces = pl.pallas_call(
        functools.partial(conv_kernel, plan, feats),
        out_shape=jax.ShapeDtypeStruct((n, strip * feats, span), jnp.bfloat16),
        in_specs=[spec_v] * (14 + len(got)),
        out_specs=spec_v,
        scratch_shapes=[
            pltpu.VMEM(((TYD + 2) * frag_rows, span + lanes), jnp.bfloat16),
            pltpu.VMEM(((band + 2) * feats, span + lanes), jnp.bfloat16),
        ],
        compiler_params=limit,
        cost_estimate=cost(4),
        name="conv",
    )(panel_map[None], own, kept[0], kept[2], inner, edge_over, edge_cross, *got, one, top, low, two, keep, b1, b2)
    shown = lax.all_to_all(pieces, "gy", split_axis=0, concat_axis=0, tiled=True)
    shown = pl.pallas_call(
        functools.partial(display_kernel, span),
        out_shape=jax.ShapeDtypeStruct((strip * feats, n * span), payload.dtype),
        in_specs=[spec_v],
        out_specs=spec_h,
        scratch_shapes=[pltpu.SemaphoreType.DMA],
        compiler_params=limit,
        name="display",
    )(shown)
    return shown.reshape(1, 1, strip, feats, n * span)


def solution(mesh):
    return jax.shard_map(
        shards,
        mesh=mesh,
        in_specs=(
            P(("gx", "gy"), None, None, None),
            P(("gx", "gy"), None, None),
            P(("gx", "gy"), None),
            P(),
            P(),
            P(),
            P(),
            P(),
            P(),
        ),
        out_specs=P("gx", "gy", None, None, None),
        check_vma=False,
    )
```
